32 devices in a mesh: subj: 2 (over x), row: 8 (over z, y), col: 2 (over core).
Axes of the slice: x: 2, y: 2, z: 4, core: 2. Of those that a mesh axis runs over, the one named last changes fastest.
Arguments:
- bold: bfloat16 [4, 256, 16, 16, 128], P('subj', None, 'row', 'col'), parts along dimension 0, may hold values from -6 to 6
- gm_index: int32 [16384], P(('row', 'col')), may hold values from -1 to 2047, as said below
- partners: int32 [128, 16], P(('row', 'col')), may hold values from -1 to 127, as said below
Outputs:
- connectome: bfloat16 [128, 16, 4, 128, 128], P(('row', 'col'), None, 'subj'), parts along dimension 2
The draws below stay inside these ranges and needn't reach their ends.
There are 2 independent parts, one for each index of `subj`. The reference program is written for one: setup_inputs(seed, part) draws one part's arguments, and reference() takes and returns one part's arrays. A program takes and returns all parts, laid end to end along the dimension named above; an argument that names none is the same for every part. Nothing has to cross between parts.
Inputs may be any that keep to these rules, and one draw needn't show every extreme that they name: `gm_index`: entries of one slab's 1024 rows are distinct voxel numbers, the last few of them -1; every slab has some -1 rows. `partners`: block g lies in slab g // 8, slabs numbered row-major over slab rows and columns. Slot 0 of block i names i, slot 1 names (i + 1) mod 128, slot 2 names (i - 1) mod 128; every named block lies in a slab whose slab row is within 2 of block i's slab row, counted cyclically. -1 marks an empty slot.
All inputs are finite; a program needn't handle non-finite values.
Results may differ from the reference program's by a relative error of at most 0.0053.
Values may be sent and summed in bfloat16 or wider, within the bound.
No kernel may reach another device: no remote copies, remote signals or barrier semaphores. Data moves between devices by JAX's collectives and lax.ppermute only.
A program may use at most 128 MiB of HBM per device.

```python
import math
import jax
import jax.numpy as jnp
from jax import lax

W = 2
F = 256
BLOCK = 128
SX = 2
SY = 8
SZ = 128
K = 16
HOP = 2
GROUP = 16
NX = 16
NY = 16
NZ = 128
VLOC = 2048
ROWS_DEV = 1024
NBD = 8
NB = 128
N_ROW = 8
N_COL = 2


def draw_gm_index(key, part):
    slab_keys = jax.random.split(key, GROUP)

    def slab_rows(slab_key):
        first_key, second_key = jax.random.split(slab_key)
        shuffled = jax.random.permutation(first_key, VLOC).astype(jnp.int32)
        chosen = shuffled[:ROWS_DEV]
        spare = shuffled[ROWS_DEV]
        chosen = jnp.where(chosen == VLOC - 1, spare, chosen)
        chosen = chosen.at[0].set(VLOC - 1)
        padding = jax.random.randint(second_key, (), 1, BLOCK // 2 + 1)
        position = jnp.arange(ROWS_DEV).astype(jnp.int32)
        chosen = jnp.where(position >= ROWS_DEV - padding, -1, chosen)
        return chosen.astype(jnp.int32)
    return jax.vmap(slab_rows)(slab_keys).reshape(-1)


def draw_partners(key, part):
    row_key, col_key, block_key, empty_key = jax.random.split(key, 4)
    block_ids = jnp.arange(NB).astype(jnp.int32)
    home_row = block_ids // NBD // N_COL
    offsets = jax.random.randint(row_key, (NB, K), -HOP, HOP + 1)
    target_col = jax.random.randint(col_key, (NB, K), 0, N_COL)
    target_block = jax.random.randint(block_key, (NB, K), 0, NBD)
    target_row = (home_row[:, None] + offsets + N_ROW) % N_ROW
    named = (target_row * N_COL + target_col) * NBD + target_block
    empty = jax.random.randint(empty_key, (NB, K), 0, 4) == 0
    named = jnp.where(empty, -1, named)
    slot = jnp.arange(K).astype(jnp.int32)[None, :]
    named = jnp.where(slot == 0, block_ids[:, None], named)
    named = jnp.where(slot == 1, ((block_ids + 1) % NB)[:, None], named)
    named = jnp.where(slot == 2, ((block_ids - 1 + NB) % NB)[:, None], named)
    named = named.at[0, K - 1].set(-1)
    return named.astype(jnp.int32)


def shard_levels(key, shape, pieces, least, top_value):
    def one(dim, shards_of):
        steps = jax.random.uniform(jax.random.fold_in(jax.random.fold_in(key, 6), dim), (shards_of,), jnp.float32, least / len(pieces), top_value / len(pieces))
        return jnp.repeat(jnp.exp(steps), shape[dim] // shards_of).reshape((-1,) + (1,) * (len(shape) - dim - 1))

    gain = one(*pieces[0])
    for cut in pieces[1:]:
        gain = gain * one(*cut)
    return gain


def gaussian(rng, shape, width, most, shards=(), kind=jnp.bfloat16):
    entries = jax.random.normal(rng, shape, jnp.float32) * width
    if len(shards) > 0:
        entries = shard_levels(rng, shape, shards, -0.22, 0.18) * entries
    return jnp.clip(entries, min=-most, max=most).astype(kind)


def setup_inputs(seed: int = 0, part: int = 0) -> dict:
    seeds = jax.random.split(jax.random.key(seed), 4)
    own_keys = jax.random.split(jax.random.fold_in(seeds[3], part), 4)
    bold = gaussian(own_keys[0], (W, F, NX, NY, NZ), 1.0, 6.0, ((2, 8), (3, 2)))
    gm_index = draw_gm_index(jax.random.fold_in(seeds[3], 71), part)
    partners = draw_partners(jax.random.fold_in(seeds[3], 71), part)
    return dict(bold=bold, gm_index=gm_index, partners=partners)


side_weight = math.exp(-0.5) / (1.0 + 2.0 * math.exp(-0.5))
centre_weight = 1.0 / (1.0 + 2.0 * math.exp(-0.5))

def gaussian_blur(padded):
    first = side_weight * padded[:, :, :-2] + centre_weight * padded[:, :, 1:-1] + side_weight * padded[:, :, 2:]
    second = side_weight * first[:, :, :, :-2] + centre_weight * first[:, :, :, 1:-1] + side_weight * first[:, :, :, 2:]
    return side_weight * second[..., :-2] + centre_weight * second[..., 1:-1] + side_weight * second[..., 2:]

def standardize(smooth):
    windows, frames = (smooth.shape[0], smooth.shape[1])
    series = smooth.reshape(windows, frames, -1)
    centred = series - lax.optimization_barrier(jnp.mean(series, axis=1, keepdims=True))
    spread = lax.optimization_barrier(jnp.mean(centred * centred, axis=1, keepdims=True))
    scored = centred * lax.rsqrt((spread + 1e-05) * frames)
    return jnp.transpose(scored, (2, 0, 1)).astype(jnp.bfloat16)

def reference(bold, gm_index, partners):
    padded = jnp.pad(bold.astype(jnp.float32), ((0, 0), (0, 0), (1, 1), (1, 1), (1, 1)))
    scored = standardize(gaussian_blur(padded))
    row_ids = jnp.arange(NB * BLOCK).astype(jnp.int32)
    slab = row_ids // ROWS_DEV
    slab_row = slab // N_COL
    slab_col = slab % N_COL
    voxel = jnp.maximum(gm_index, 0).astype(jnp.int32)
    local_x = voxel // (SY * SZ)
    local_y = voxel // SZ % SY
    local_z = voxel % SZ
    global_ids = ((slab_row * SX + local_x) * NY + slab_col * SY + local_y) * NZ + local_z
    picked = jnp.take(scored, global_ids.astype(jnp.int32), axis=0)
    panel = jnp.where((gm_index >= 0)[:, None, None], picked, jnp.zeros_like(picked))
    blocks = panel.reshape(NB, BLOCK, W, F)

    def block_tiles(inputs):
        local_block, partner_ids = inputs
        partner_rows = jnp.take(blocks, jnp.maximum(partner_ids, 0).astype(jnp.int32), axis=0)
        tiles_out = jnp.einsum('awf,kbwf->kwab', local_block.astype(jnp.float32), partner_rows.astype(jnp.float32))
        tiles_out = jnp.where((partner_ids >= 0)[:, None, None, None], tiles_out, jnp.zeros_like(tiles_out))
        return tiles_out.astype(jnp.bfloat16)
    return lax.map(block_tiles, (blocks, partners))
```

```python
import functools
import math

import jax
import jax.numpy as jnp
from jax import lax
from jax.experimental import pallas as pl
from jax.experimental.pallas import tpu as pltpu
from jax.sharding import PartitionSpec as P

BLOCK = 128
SIDE = math.exp(-0.5) / (1.0 + 2.0 * math.exp(-0.5))
CENTRE = 1.0 / (1.0 + 2.0 * math.exp(-0.5))
VMEM_BYTES = 48 * 1024 * 1024


def panel_kernel(
    col_ref, bold_ref, low_ref, high_ref, edge_ref, corner_ref, gm_ref, out_ref,
    wide, wide_low, wide_high, planes, scored,
):
    frames, slab_x, slab_y, slab_z = bold_ref.shape[1:]
    per_frame = slab_x * slab_y
    wide[...] = bold_ref[0].reshape(frames * per_frame, slab_z).astype(jnp.float32)
    wide_low[...] = low_ref[...].reshape(frames * slab_y, slab_z).astype(jnp.float32)
    wide_high[...] = high_ref[...].reshape(frames * slab_y, slab_z).astype(jnp.float32)

    def along_x(before, here, after):
        return SIDE * before + CENTRE * here + SIDE * after

    for y in range(slab_y):
        layers = [wide_low[pl.ds(y, frames, stride=slab_y), :]]
        for x in range(slab_x):
            layers.append(wide[pl.ds(x * slab_y + y, frames, stride=per_frame), :])
        layers.append(wide_high[pl.ds(y, frames, stride=slab_y), :])
        for x in range(slab_x):
            planes[x, y + 1] = along_x(*layers[x : x + 3])
    edges = [corner_ref[0].astype(jnp.float32)]
    for x in range(slab_x):
        edges.append(edge_ref[x].astype(jnp.float32))
    edges.append(corner_ref[1].astype(jnp.float32))
    for x in range(slab_x):
        edge = along_x(*edges[x : x + 3])
        planes[x, 0] = jnp.where(col_ref[0] == 0, 0.0, edge)
        planes[x, slab_y + 1] = jnp.where(col_ref[0] == 0, edge, 0.0)

    lane = lax.broadcasted_iota(jnp.int32, (frames, slab_z), 1)
    for x in range(slab_x):
        for y in range(slab_y):
            part = along_x(planes[x, y], planes[x, y + 1], planes[x, y + 2])
            before = jnp.where(lane == 0, 0.0, pltpu.roll(part, 1, 1))
            after = jnp.where(lane == slab_z - 1, 0.0, pltpu.roll(part, slab_z - 1, 1))
            smooth = along_x(before, part, after)
            centred = smooth - jnp.mean(smooth, axis=0, keepdims=True)
            spread = jnp.mean(centred * centred, axis=0, keepdims=True)
            value = centred * lax.rsqrt((spread + 1e-05) * frames)
            start = (x * slab_y + y) * slab_z
            scored[:, start : start + slab_z] = value.astype(jnp.bfloat16)

    voxels = per_frame * slab_z
    rows = gm_ref.shape[1]
    step = 2 * BLOCK
    for start in range(0, rows, step):
        wanted = gm_ref[:, start : start + step]
        voxel = lax.broadcasted_iota(jnp.int32, (voxels, step), 0)
        chosen = jnp.where(voxel == wanted, 1.0, 0.0).astype(jnp.bfloat16)
        picked = jnp.dot(scored[...], chosen, preferred_element_type=jnp.float32)
        out_ref[:, start : start + step] = picked.astype(jnp.bfloat16)


def make_panel(window, col, bold, low, high, edge, corner, gm):
    _, frames, slab_x, slab_y, slab_z = bold.shape
    rows = gm.shape[1]
    whole = lambda array: pl.BlockSpec(array.shape, lambda *_: (0,) * array.ndim)
    f32 = jnp.float32
    return pl.pallas_call(
        panel_kernel,
        grid=(1,),
        in_specs=[
            pl.BlockSpec(memory_space=pltpu.SMEM),
            pl.BlockSpec((1, frames, slab_x, slab_y, slab_z), lambda _: (window, 0, 0, 0, 0)),
            whole(low), whole(high), whole(edge), whole(corner), whole(gm),
        ],
        out_specs=pl.BlockSpec((frames, rows), lambda _: (0, 0)),
        out_shape=jax.ShapeDtypeStruct((frames, rows), jnp.bfloat16),
        scratch_shapes=[
            pltpu.VMEM((frames * slab_x * slab_y, slab_z), f32),
            pltpu.VMEM((frames * slab_y, slab_z), f32),
            pltpu.VMEM((frames * slab_y, slab_z), f32),
            pltpu.VMEM((slab_x, slab_y + 2, frames, slab_z), f32),
            pltpu.VMEM((frames, slab_x * slab_y * slab_z), jnp.bfloat16),
        ],
        compiler_params=pltpu.CompilerParams(vmem_limit_bytes=VMEM_BYTES),
        cost_estimate=pl.CostEstimate(
            flops=2 * frames * rows * slab_x * slab_y * slab_z,
            bytes_accessed=4 * 1024 * 1024, transcendentals=0,
        ),
        name="blur_score_pick",
    )(col, bold, low, high, edge, corner, gm)


def tiles_kernel(place_ref, present_ref, *refs, sources):
    parts = refs[:sources]
    out_ref, held, sems = refs[-3:]
    block = pl.program_id(0)
    slots = out_ref.shape[1]
    blocks_each = held.shape[2] // BLOCK

    @pl.when(block == 0)
    def _():
        for n, part in enumerate(parts):
            pltpu.make_async_copy(part, held.at[n], sems.at[n]).start()
        for n, part in enumerate(parts):
            pltpu.make_async_copy(part, held.at[n], sems.at[n]).wait()

    own = held[0, :, pl.ds(pl.multiple_of(block * BLOCK, BLOCK), BLOCK)].T

    def partner(slot):
        place = place_ref[block * slots + slot]
        start = pl.multiple_of(lax.rem(place, blocks_each) * BLOCK, BLOCK)
        return held[place // blocks_each, :, pl.ds(start, BLOCK)]

    for slot in range(0, slots, 2):
        pair = jnp.concatenate([partner(slot), partner(slot + 1)], axis=1)
        both = jnp.dot(own, pair, preferred_element_type=jnp.float32)
        for n in range(2):
            keep = present_ref[block * slots + slot + n] != 0
            tile = both[:, n * BLOCK : (n + 1) * BLOCK]
            out_ref[0, slot + n, 0] = jnp.where(keep, tile, 0.0).astype(jnp.bfloat16)


def make_tiles(window, windows, place, present, sources, earlier):
    frames, rows = sources[0].shape
    blocks = rows // BLOCK
    slots = place.shape[0] // blocks
    count = len(sources)
    anywhere = pl.BlockSpec(memory_space=pl.ANY)
    operands = list(sources) + ([] if earlier is None else [earlier])
    return pl.pallas_call(
        functools.partial(tiles_kernel, sources=count),
        grid_spec=pltpu.PrefetchScalarGridSpec(
            num_scalar_prefetch=2,
            grid=(blocks,),
            in_specs=[anywhere] * len(operands),
            out_specs=pl.BlockSpec(
                (1, slots, 1, BLOCK, BLOCK), lambda i, *_: (i, 0, window, 0, 0)
            ),
            scratch_shapes=[
                pltpu.VMEM((count, frames, rows), jnp.bfloat16),
                pltpu.SemaphoreType.DMA((count,)),
            ],
        ),
        out_shape=jax.ShapeDtypeStruct((blocks, slots, windows, BLOCK, BLOCK), jnp.bfloat16),
        input_output_aliases={} if earlier is None else {2 + count: 0},
        compiler_params=pltpu.CompilerParams(vmem_limit_bytes=VMEM_BYTES),
        cost_estimate=pl.CostEstimate(
            flops=2 * blocks * slots * BLOCK * BLOCK * frames,
            bytes_accessed=10 * 1024 * 1024, transcendentals=0,
        ),
        name="tiles",
    )(place, present, *operands)


def on_device(bold, gm_index, partners):
    windows, frames, slab_x, slab_y, slab_z = bold.shape
    row_total = lax.axis_size("row")
    col_total = lax.axis_size("col")
    row = lax.axis_index("row")
    col = lax.axis_index("col")
    even = row % 2 == 0

    def shift_row(value, pairs):
        return lax.ppermute(value, "row", pairs)

    def other_col(value):
        return lax.ppermute(value, "col", [(0, 1), (1, 0)])

    up = [(i, i + 1) for i in range(row_total - 1)]
    down = [(i + 1, i) for i in range(row_total - 1)]
    up_two = [(i, (i + 2) % row_total) for i in range(row_total)]
    down_two = [((i + 2) % row_total, i) for i in range(row_total)]
    pairs = [(i, i ^ 1) for i in range(row_total)]

    gm = gm_index.reshape(1, -1)
    col_arg = col.reshape(1).astype(jnp.int32)

    face = jnp.where(col == 0, bold[:, :, :, -1], bold[:, :, :, 0])
    edge = other_col(jnp.transpose(face, (0, 2, 1, 3)))

    blocks = partners.shape[0]
    ids = jnp.maximum(partners, 0)
    slab = ids // blocks
    distance = (slab // col_total - row + 2 + row_total) % row_total
    kind = jnp.where(
        even,
        jnp.array([1, 4, 0, 3, 2], jnp.int32)[jnp.minimum(distance, 4)],
        jnp.array([1, 3, 0, 4, 2], jnp.int32)[jnp.minimum(distance, 4)],
    )
    away = (slab % col_total != col).astype(jnp.int32)
    place = ((away * 5 + kind) * blocks + ids % blocks).astype(jnp.int32).reshape(-1)
    present = (partners >= 0).astype(jnp.int32).reshape(-1)

    halos = []
    for window in range(windows):
        low = shift_row(bold[window, :, -1], up)
        high = shift_row(bold[window, :, 0], down)
        halos.append((low, high))
    out = None
    for window in range(windows):
        low, high = halos[window]
        ends = jnp.stack(
            [jnp.where(col == 0, layer[:, -1], layer[:, 0]) for layer in (low, high)], 0
        )
        corner = other_col(ends)
        own = make_panel(window, col_arg, bold, low, high, edge[window], corner, gm)
        lower = shift_row(own, up_two)
        upper = shift_row(own, down_two)
        pair = shift_row(own, pairs)
        rest = shift_row(jnp.where(even, upper, lower), pairs)
        mine = [own, lower, upper, pair, rest]
        sources = mine + [other_col(part) for part in mine]
        out = make_tiles(window, windows, place, present, sources, out)
    return out


def solution(mesh):
    in_specs = (P("subj", None, "row", "col", None), P(("row", "col")), P(("row", "col"), None))
    out_specs = P(("row", "col"), None, "subj", None, None)
    return jax.shard_map(
        on_device, mesh=mesh, in_specs=in_specs, out_specs=out_specs, check_vma=False
    )
```

```python
import functools
import math

import jax
import jax.numpy as jnp
from jax import lax
from jax.experimental import pallas as pl
from jax.experimental.pallas import tpu as pltpu
from jax.sharding import PartitionSpec as P

BLOCK = 128
SIDE = math.exp(-0.5) / (1.0 + 2.0 * math.exp(-0.5))
CENTRE = 1.0 / (1.0 + 2.0 * math.exp(-0.5))
SMALL = pl.CostEstimate(flops=1, bytes_accessed=1, transcendentals=0)
VMEM_BYTES = 24 * 1024 * 1024


def faces_kernel(col_ref, bold_ref, first_ref, last_ref, edge_ref, wide):
    frames, slab_x, slab_y, slab_z = bold_ref.shape[1:]
    per_frame = slab_x * slab_y
    wide[...] = bold_ref[0].reshape(frames * per_frame, slab_z).astype(jnp.float32)
    for x, layer_ref in enumerate((first_ref, last_ref)):
        for y in range(slab_y):
            plane = wide[pl.ds(x * slab_y + y, frames, stride=per_frame), :]
            layer_ref[y] = plane.astype(jnp.bfloat16)
        @pl.when(col_ref[0] == 0)
        def _():
            edge_ref[x] = layer_ref[slab_y - 1]

        @pl.when(col_ref[0] != 0)
        def _():
            edge_ref[x] = layer_ref[0]


def make_faces(window, col, bold):
    _, frames, slab_x, slab_y, slab_z = bold.shape
    layer = jax.ShapeDtypeStruct((slab_y, frames, slab_z), jnp.bfloat16)
    edge = jax.ShapeDtypeStruct((slab_x, frames, slab_z), jnp.bfloat16)
    whole = lambda array: pl.BlockSpec(array.shape, lambda _: (0,) * len(array.shape))
    return pl.pallas_call(
        faces_kernel,
        grid=(1,),
        in_specs=[
            pl.BlockSpec(memory_space=pltpu.SMEM),
            pl.BlockSpec((1, frames, slab_x, slab_y, slab_z), lambda _: (window, 0, 0, 0, 0)),
        ],
        out_specs=[whole(layer), whole(layer), whole(edge)],
        out_shape=[layer, layer, edge],
        scratch_shapes=[pltpu.VMEM((frames * slab_x * slab_y, slab_z), jnp.float32)],
        compiler_params=pltpu.CompilerParams(vmem_limit_bytes=VMEM_BYTES),
        cost_estimate=SMALL,
        name="faces",
    )(col, bold)


def panel_kernel(
    col_ref, first_ref, last_ref, low_ref, high_ref, edge_ref, corner_ref, gm_ref, out_ref,
    planes, scored,
):
    slab_y, frames, slab_z = first_ref.shape
    slab_x = edge_ref.shape[0]

    def along_x(before, here, after):
        return SIDE * before + CENTRE * here + SIDE * after

    for y in range(slab_y):
        layers = [ref[y].astype(jnp.float32) for ref in (low_ref, first_ref, last_ref, high_ref)]
        for x in range(slab_x):
            planes[x, y + 1] = along_x(*layers[x : x + 3])
    edges = [corner_ref[0], edge_ref[0], edge_ref[1], corner_ref[1]]
    edges = [edge.astype(jnp.float32) for edge in edges]
    for x in range(slab_x):
        edge = along_x(*edges[x : x + 3])
        planes[x, 0] = jnp.where(col_ref[0] == 0, 0.0, edge)
        planes[x, slab_y + 1] = jnp.where(col_ref[0] == 0, edge, 0.0)

    lane = lax.broadcasted_iota(jnp.int32, (frames, slab_z), 1)
    for x in range(slab_x):
        for y in range(slab_y):
            part = along_x(planes[x, y], planes[x, y + 1], planes[x, y + 2])
            before = jnp.where(lane == 0, 0.0, pltpu.roll(part, 1, 1))
            after = jnp.where(lane == slab_z - 1, 0.0, pltpu.roll(part, slab_z - 1, 1))
            smooth = along_x(before, part, after)
            centred = smooth - jnp.mean(smooth, axis=0, keepdims=True)
            spread = jnp.mean(centred * centred, axis=0, keepdims=True)
            value = centred * lax.rsqrt((spread + 1e-05) * frames)
            start = (x * slab_y + y) * slab_z
            scored[:, start : start + slab_z] = value.astype(jnp.bfloat16)

    voxels = slab_x * slab_y * slab_z
    rows = gm_ref.shape[1]
    step = 2 * BLOCK
    for start in range(0, rows, step):
        wanted = gm_ref[:, start : start + step]
        voxel = lax.broadcasted_iota(jnp.int32, (voxels, step), 0)
        chosen = jnp.where(voxel == wanted, 1.0, 0.0).astype(jnp.bfloat16)
        picked = jnp.dot(scored[...], chosen, preferred_element_type=jnp.float32)
        out_ref[:, start : start + step] = picked.astype(jnp.bfloat16)


def make_panel(col, first, last, low, high, edge, corner, gm):
    slab_y, frames, slab_z = first.shape
    slab_x = edge.shape[0]
    rows = gm.shape[1]
    voxels = slab_x * slab_y * slab_z
    whole = lambda array: pl.BlockSpec(array.shape, lambda _: (0,) * array.ndim)
    operands = (first, last, low, high, edge, corner, gm)
    return pl.pallas_call(
        panel_kernel,
        grid=(1,),
        in_specs=[pl.BlockSpec(memory_space=pltpu.SMEM)] + [whole(value) for value in operands],
        out_specs=pl.BlockSpec((frames, rows), lambda _: (0, 0)),
        out_shape=jax.ShapeDtypeStruct((frames, rows), jnp.bfloat16),
        scratch_shapes=[
            pltpu.VMEM((slab_x, slab_y + 2, frames, slab_z), jnp.float32),
            pltpu.VMEM((frames, voxels), jnp.bfloat16),
        ],
        compiler_params=pltpu.CompilerParams(vmem_limit_bytes=VMEM_BYTES),
        cost_estimate=SMALL,
        name="blur_score_pick",
    )(col, *operands)


def tiles_kernel(place_ref, present_ref, *refs, sources):
    parts = refs[:sources]
    out_ref, rows_ref, held, sems = refs[-4:]
    block = pl.program_id(0)
    slots = out_ref.shape[1]
    blocks_each = held.shape[2] // BLOCK

    @pl.when(block == 0)
    def _():
        copies, first = [], 0
        for n, part in enumerate(parts):
            target = held.at[pl.ds(first, part.shape[0])]
            copies.append(pltpu.make_async_copy(part, target, sems.at[n]))
            copies[-1].start()
            first += part.shape[0]
        for copy in copies:
            copy.wait()

    own = held[0, :, pl.ds(pl.multiple_of(block * BLOCK, BLOCK), BLOCK)].T
    rows_ref[...] = own

    def partner(slot):
        place = place_ref[block * slots + slot]
        start = pl.multiple_of(lax.rem(place, blocks_each) * BLOCK, BLOCK)
        return held[place // blocks_each, :, pl.ds(start, BLOCK)]

    for slot in range(0, slots, 2):
        pair = jnp.concatenate([partner(slot), partner(slot + 1)], axis=1)
        both = jnp.dot(own, pair, preferred_element_type=jnp.float32)
        for n in range(2):
            keep = present_ref[block * slots + slot + n] != 0
            tile = both[:, n * BLOCK : (n + 1) * BLOCK]
            out_ref[0, slot + n, 0] = jnp.where(keep, tile, 0.0).astype(jnp.bfloat16)


def make_tiles(window, windows, place, present, sources, earlier):
    frames, rows = sources[0].shape[1:]
    total = sum(value.shape[0] for value in sources)
    blocks = rows // BLOCK
    slots = place.shape[0] // blocks
    count = len(sources)
    anywhere = pl.BlockSpec(memory_space=pl.ANY)
    operands = list(sources) + ([] if earlier is None else [earlier])
    return pl.pallas_call(
        functools.partial(tiles_kernel, sources=count),
        grid_spec=pltpu.PrefetchScalarGridSpec(
            num_scalar_prefetch=2,
            grid=(blocks,),
            in_specs=[anywhere] * len(operands),
            out_specs=[
                pl.BlockSpec(
                    (1, slots, 1, BLOCK, BLOCK), lambda i, *_: (i, 0, window, 0, 0)
                ),
                pl.BlockSpec((BLOCK, frames), lambda i, *_: (i, 0)),
            ],
            scratch_shapes=[
                pltpu.VMEM((total, frames, rows), jnp.bfloat16),
                pltpu.SemaphoreType.DMA((count,)),
            ],
        ),
        out_shape=[
            jax.ShapeDtypeStruct((blocks, slots, windows, BLOCK, BLOCK), jnp.bfloat16),
            jax.ShapeDtypeStruct((rows, frames), jnp.bfloat16),
        ],
        input_output_aliases={} if earlier is None else {2 + count: 0},
        compiler_params=pltpu.CompilerParams(vmem_limit_bytes=VMEM_BYTES),
        cost_estimate=SMALL,
        name="tiles",
    )(place, present, *operands)


def late_kernel(
    order_ref, count_ref, place_ref, rows_ref, near_ref, far_ref, earlier_ref, out_ref,
    held, tiles, sems, *, window, group,
):
    blocks, slots = out_ref.shape[:2]
    held[0] = near_ref[...]
    held[1] = far_ref[...]

    def copy(entry):
        slot = order_ref[entry]
        target = out_ref.at[slot // slots, lax.rem(slot, slots), window]
        return pltpu.make_async_copy(tiles.at[entry], target, sems.at[entry])

    def some(step, carry):
        for n in range(group):
            entry = step * group + n
            slot = order_ref[entry]
            place = place_ref[slot]
            start = pl.multiple_of(lax.rem(place, blocks) * BLOCK, BLOCK)
            rows_start = pl.multiple_of(slot // slots * BLOCK, BLOCK)
            tile = jnp.dot(
                rows_ref[pl.ds(rows_start, BLOCK), :],
                held[place // blocks, :, pl.ds(start, BLOCK)],
                preferred_element_type=jnp.float32,
            )
            tiles[entry] = tile.astype(jnp.bfloat16)
        for n in range(group):
            entry = step * group + n

            @pl.when(entry < count_ref[0])
            def _():
                copy(entry).start()

        return carry

    lax.fori_loop(0, (count_ref[0] + group - 1) // group, some, 0)

    def finish(entry, carry):
        copy(entry).wait()
        return carry

    lax.fori_loop(0, count_ref[0], finish, 0)


def make_late(window, order, count, place, own, near, far, earlier):
    rows, frames = own.shape
    total = order.shape[0]
    mine = pl.BlockSpec((rows, frames), lambda *_: (0, 0))
    whole = pl.BlockSpec((frames, rows), lambda *_: (0, 0))
    anywhere = pl.BlockSpec(memory_space=pl.ANY)
    return pl.pallas_call(
        functools.partial(late_kernel, window=window, group=8),
        grid_spec=pltpu.PrefetchScalarGridSpec(
            num_scalar_prefetch=3,
            grid=(1,),
            in_specs=[mine, whole, whole, anywhere],
            out_specs=anywhere,
            scratch_shapes=[
                pltpu.VMEM((2, frames, rows), jnp.bfloat16),
                pltpu.VMEM((total, BLOCK, BLOCK), jnp.bfloat16),
                pltpu.SemaphoreType.DMA((total,)),
            ],
        ),
        out_shape=jax.ShapeDtypeStruct(earlier.shape, earlier.dtype),
        input_output_aliases={6: 0},
        compiler_params=pltpu.CompilerParams(vmem_limit_bytes=VMEM_BYTES),
        cost_estimate=SMALL,
        name="late_tiles",
    )(order, count, place, own, near, far, earlier)


def after(value, *earlier):
    return lax.optimization_barrier((value,) + earlier)[0]


def on_device(bold, gm_index, partners):
    row_total = lax.axis_size("row")
    col_total = lax.axis_size("col")
    row = lax.axis_index("row")
    col = lax.axis_index("col")
    even = row % 2 == 0

    def other_col(value):
        return lax.ppermute(value, "col", [(0, 1), (1, 0)])

    one_up = [(i, i + 1) for i in range(row_total - 1)]
    one_down = [(i + 1, i) for i in range(row_total - 1)]
    ahead = [((i + 2 * (-1) ** i) % row_total, i) for i in range(row_total)]
    behind = [(i, source) for source, i in ahead]
    in_pair = [(i, i ^ 1) for i in range(row_total)]

    gm = gm_index.reshape(1, -1)
    col_arg = col.reshape(1).astype(jnp.int32)

    blocks, slots = partners.shape
    ids = jnp.maximum(partners, 0)
    slab = ids // blocks
    hop = (slab // col_total - row + 2 + row_total) % row_total
    kind = jnp.where((hop == 1) == even, 4, 3)
    kind = jnp.where(hop == 2, 0, jnp.where((hop == 0) | (hop >= 4), 2 - (even == (hop >= 4)), kind))
    away = (slab % col_total != col).astype(jnp.int32)
    within = ids % blocks
    present = partners >= 0
    late = present & (kind == 4)
    early = present & (kind != 4)
    early_place = jnp.where(early, (kind // 2 * 4 + away * 2 + kind % 2) * blocks + within, 0)
    late_place = jnp.where(late, away * blocks + within, 0)
    early, late = early.reshape(-1).astype(jnp.int32), late.reshape(-1)
    early_place = early_place.reshape(-1).astype(jnp.int32)
    late_place = late_place.reshape(-1).astype(jnp.int32)
    entries = jnp.arange(blocks * slots, dtype=jnp.int32)
    rank = jnp.sum((entries[None, :] < entries[:, None]) & late[None, :], axis=1)
    order = jnp.sum(
        jnp.where(late[None, :] & (rank[None, :] == entries[:, None]), entries[None, :], 0), axis=1
    ).astype(jnp.int32)
    count = jnp.sum(late).astype(jnp.int32).reshape(1)

    def halo(first, last):
        return lax.ppermute(last, "row", one_up), lax.ppermute(first, "row", one_down)

    def halves(*parts):
        near = jnp.stack(parts, 0)
        return [near, other_col(near)]

    def corner_of(low, high):
        return other_col(
            jnp.stack([jnp.where(col == 0, part[-1], part[0]) for part in (low, high)], 0)
        )

    windows = bold.shape[0]
    first_0, last_0, face_0 = make_faces(0, col_arg, bold)
    low_0, high_0 = halo(first_0, last_0)
    edge_0 = other_col(face_0)
    first_1, last_1, face_1 = make_faces(1, col_arg, after(bold, edge_0))
    edge_1 = other_col(face_1)
    corner_0 = corner_of(low_0, high_0)
    first_1, last_1 = after(first_1, low_0, high_0, edge_1), after(last_1, low_0, high_0, edge_1)
    low_1, high_1 = halo(first_1, last_1)
    own_0 = make_panel(col_arg, first_0, last_0, low_0, high_0, edge_0, corner_0, gm)
    ahead_0 = lax.ppermute(own_0, "row", ahead)
    behind_0 = lax.ppermute(own_0, "row", behind)
    low_1, high_1 = after(low_1, own_0), after(high_1, own_0)
    pair_0 = lax.ppermute(after(own_0, low_1, high_1), "row", in_pair)
    corner_1 = corner_of(low_1, high_1)
    own_1 = make_panel(col_arg, first_1, last_1, low_1, high_1, edge_1, corner_1, gm)
    ahead_0, behind_0 = after(ahead_0, own_1), after(behind_0, own_1)
    ahead_1 = lax.ppermute(own_1, "row", ahead)
    rest_0 = lax.ppermute(ahead_0, "row", in_pair)
    pair_1 = lax.ppermute(own_1, "row", in_pair)
    sources = halves(own_0, ahead_0) + halves(behind_0, pair_0)
    out, rows_0 = make_tiles(0, windows, early_place, early, sources, None)
    behind_1 = lax.ppermute(after(own_1, ahead_1), "row", behind)
    rest_1 = lax.ppermute(after(ahead_1, rest_0), "row", in_pair)
    behind_1, rest_0 = after(behind_1, out), after(rest_0, out)
    out = make_late(0, order, count, late_place, rows_0, rest_0, other_col(rest_0), out)
    sources = halves(own_1, ahead_1) + halves(behind_1, pair_1)
    out, rows_1 = make_tiles(1, windows, early_place, early, sources, out)
    rest_1 = after(rest_1, out)
    return make_late(1, order, count, late_place, rows_1, rest_1, other_col(rest_1), out)


def solution(mesh):
    in_specs = (P("subj", None, "row", "col", None), P(("row", "col")), P(("row", "col"), None))
    out_specs = P(("row", "col"), None, "subj", None, None)
    return jax.shard_map(
        on_device, mesh=mesh, in_specs=in_specs, out_specs=out_specs, check_vma=False
    )
```

```python
import functools
import math

import jax
import jax.numpy as jnp
from jax import lax
from jax.experimental import pallas as pl
from jax.experimental.pallas import tpu as pltpu
from jax.sharding import PartitionSpec as P

BLOCK = 128
SIDE = math.exp(-0.5) / (1.0 + 2.0 * math.exp(-0.5))
CENTRE = 1.0 / (1.0 + 2.0 * math.exp(-0.5))
SMALL = pl.CostEstimate(flops=1, bytes_accessed=1, transcendentals=0)
VMEM_BYTES = 24 * 1024 * 1024


def faces_kernel(col_ref, bold_ref, first_ref, last_ref, edge_ref, wide):
    frames, slab_x, slab_y, slab_z = bold_ref.shape[1:]
    per_frame = slab_x * slab_y
    wide[...] = bold_ref[0].reshape(frames * per_frame, slab_z).astype(jnp.float32)
    for x, layer_ref in enumerate((first_ref, last_ref)):
        for y in range(slab_y):
            plane = wide[pl.ds(x * slab_y + y, frames, stride=per_frame), :]
            layer_ref[y] = plane.astype(jnp.bfloat16)
        @pl.when(col_ref[0] == 0)
        def _():
            edge_ref[x] = layer_ref[slab_y - 1]

        @pl.when(col_ref[0] != 0)
        def _():
            edge_ref[x] = layer_ref[0]


def make_faces(window, col, bold):
    _, frames, slab_x, slab_y, slab_z = bold.shape
    layer = jax.ShapeDtypeStruct((slab_y, frames, slab_z), jnp.bfloat16)
    edge = jax.ShapeDtypeStruct((slab_x, frames, slab_z), jnp.bfloat16)
    whole = lambda array: pl.BlockSpec(array.shape, lambda _: (0,) * len(array.shape))
    return pl.pallas_call(
        faces_kernel,
        grid=(1,),
        in_specs=[
            pl.BlockSpec(memory_space=pltpu.SMEM),
            pl.BlockSpec((1, frames, slab_x, slab_y, slab_z), lambda _: (window, 0, 0, 0, 0)),
        ],
        out_specs=[whole(layer), whole(layer), whole(edge)],
        out_shape=[layer, layer, edge],
        scratch_shapes=[pltpu.VMEM((frames * slab_x * slab_y, slab_z), jnp.float32)],
        compiler_params=pltpu.CompilerParams(vmem_limit_bytes=VMEM_BYTES),
        cost_estimate=SMALL,
        name="faces",
    )(col, bold)


def panel_kernel(
    col_ref, first_ref, last_ref, low_ref, high_ref, edge_ref, corner_ref, gm_ref, out_ref,
    planes, scored,
):
    slab_y, frames, slab_z = first_ref.shape
    slab_x = edge_ref.shape[0]

    def along_x(before, here, after):
        return SIDE * before + CENTRE * here + SIDE * after

    for y in range(slab_y):
        layers = [ref[y].astype(jnp.float32) for ref in (low_ref, first_ref, last_ref, high_ref)]
        for x in range(slab_x):
            planes[x, y + 1] = along_x(*layers[x : x + 3])
    edges = [corner_ref[0], edge_ref[0], edge_ref[1], corner_ref[1]]
    edges = [edge.astype(jnp.float32) for edge in edges]
    for x in range(slab_x):
        edge = along_x(*edges[x : x + 3])
        planes[x, 0] = jnp.where(col_ref[0] == 0, 0.0, edge)
        planes[x, slab_y + 1] = jnp.where(col_ref[0] == 0, edge, 0.0)

    lane = lax.broadcasted_iota(jnp.int32, (frames, slab_z), 1)
    for x in range(slab_x):
        for y in range(slab_y):
            part = along_x(planes[x, y], planes[x, y + 1], planes[x, y + 2])
            before = jnp.where(lane == 0, 0.0, pltpu.roll(part, 1, 1))
            after = jnp.where(lane == slab_z - 1, 0.0, pltpu.roll(part, slab_z - 1, 1))
            smooth = along_x(before, part, after)
            centred = smooth - jnp.mean(smooth, axis=0, keepdims=True)
            spread = jnp.mean(centred * centred, axis=0, keepdims=True)
            value = centred * lax.rsqrt((spread + 1e-05) * frames)
            start = (x * slab_y + y) * slab_z
            scored[:, start : start + slab_z] = value.astype(jnp.bfloat16)

    voxels = slab_x * slab_y * slab_z
    rows = gm_ref.shape[1]
    step = 2 * BLOCK
    for start in range(0, rows, step):
        wanted = gm_ref[:, start : start + step]
        voxel = lax.broadcasted_iota(jnp.int32, (voxels, step), 0)
        chosen = jnp.where(voxel == wanted, 1.0, 0.0).astype(jnp.bfloat16)
        picked = jnp.dot(scored[...], chosen, preferred_element_type=jnp.float32)
        out_ref[:, start : start + step] = picked.astype(jnp.bfloat16)


def make_panel(col, first, last, low, high, edge, corner, gm):
    slab_y, frames, slab_z = first.shape
    slab_x = edge.shape[0]
    rows = gm.shape[1]
    voxels = slab_x * slab_y * slab_z
    whole = lambda array: pl.BlockSpec(array.shape, lambda _: (0,) * array.ndim)
    operands = (first, last, low, high, edge, corner, gm)
    return pl.pallas_call(
        panel_kernel,
        grid=(1,),
        in_specs=[pl.BlockSpec(memory_space=pltpu.SMEM)] + [whole(value) for value in operands],
        out_specs=pl.BlockSpec((frames, rows), lambda _: (0, 0)),
        out_shape=jax.ShapeDtypeStruct((frames, rows), jnp.bfloat16),
        scratch_shapes=[
            pltpu.VMEM((slab_x, slab_y + 2, frames, slab_z), jnp.float32),
            pltpu.VMEM((frames, voxels), jnp.bfloat16),
        ],
        compiler_params=pltpu.CompilerParams(vmem_limit_bytes=VMEM_BYTES),
        cost_estimate=SMALL,
        name="blur_score_pick",
    )(col, *operands)


def tiles_kernel(place_ref, present_ref, *refs, sources, window):
    parts = refs[:sources]
    out_ref, rows_ref, held, tiles, sems, out_sems = refs[-6:]
    blocks, slots = out_ref.shape[:2]

    loads, first = [], 0
    for n, part in enumerate(parts):
        target = held.at[pl.ds(first, part.shape[0])]
        loads.append(pltpu.make_async_copy(part, target, sems.at[n]))
        loads[-1].start()
        first += part.shape[0]
    for load in loads:
        load.wait()

    def partner(index):
        place = place_ref[index]
        start = pl.multiple_of(lax.rem(place, blocks) * BLOCK, BLOCK)
        return held[lax.div(place, blocks), :, pl.ds(start, BLOCK)]

    stores = []
    for block in range(blocks):
        own = held[0, :, block * BLOCK : (block + 1) * BLOCK].T
        rows_ref[block * BLOCK : (block + 1) * BLOCK, :] = own
        for slot in range(0, slots, 2):
            index = block * slots + slot
            pair = jnp.concatenate([partner(index), partner(index + 1)], axis=1)
            both = jnp.dot(own, pair, preferred_element_type=jnp.float32)
            for n in range(2):
                tile = both[:, n * BLOCK : (n + 1) * BLOCK]
                tile = jnp.where(present_ref[index + n] != 0, tile, 0.0)
                tiles[block, slot + n] = tile.astype(jnp.bfloat16)
        stores.append(
            pltpu.make_async_copy(tiles.at[block], out_ref.at[block, :, window], out_sems.at[block])
        )
        stores[-1].start()
    for store in stores:
        store.wait()


def make_tiles(window, windows, place, present, sources, earlier):
    frames, rows = sources[0].shape[1:]
    total = sum(value.shape[0] for value in sources)
    blocks = rows // BLOCK
    slots = place.shape[0] // blocks
    count = len(sources)
    anywhere = pl.BlockSpec(memory_space=pl.ANY)
    operands = list(sources) + ([] if earlier is None else [earlier])
    return pl.pallas_call(
        functools.partial(tiles_kernel, sources=count, window=window),
        grid_spec=pltpu.PrefetchScalarGridSpec(
            num_scalar_prefetch=2,
            grid=(1,),
            in_specs=[anywhere] * len(operands),
            out_specs=[anywhere, pl.BlockSpec((rows, frames), lambda *_: (0, 0))],
            scratch_shapes=[
                pltpu.VMEM((total, frames, rows), jnp.bfloat16),
                pltpu.VMEM((blocks, slots, BLOCK, BLOCK), jnp.bfloat16),
                pltpu.SemaphoreType.DMA((count,)),
                pltpu.SemaphoreType.DMA((blocks,)),
            ],
        ),
        out_shape=[
            jax.ShapeDtypeStruct((blocks, slots, windows, BLOCK, BLOCK), jnp.bfloat16),
            jax.ShapeDtypeStruct((rows, frames), jnp.bfloat16),
        ],
        input_output_aliases={} if earlier is None else {2 + count: 0},
        compiler_params=pltpu.CompilerParams(vmem_limit_bytes=VMEM_BYTES),
        cost_estimate=SMALL,
        name="tiles",
    )(place, present, *operands)


def late_kernel(
    order_ref, count_ref, place_ref, rows_any, near_any, far_any, earlier_ref, out_ref,
    rows_ref, held, tiles, sems, *, window, group,
):
    blocks, slots = out_ref.shape[:2]
    loads = []
    for n, (source, target) in enumerate(
        ((rows_any, rows_ref), (near_any, held.at[0]), (far_any, held.at[1]))
    ):
        loads.append(pltpu.make_async_copy(source, target, sems.at[n]))
        loads[-1].start()
    for load in loads:
        load.wait()

    def copy(entry):
        slot = order_ref[entry]
        target = out_ref.at[slot // slots, lax.rem(slot, slots), window]
        return pltpu.make_async_copy(tiles.at[entry], target, sems.at[entry])

    def some(step, carry):
        for n in range(group):
            entry = step * group + n
            slot = order_ref[entry]
            place = place_ref[slot]
            start = pl.multiple_of(lax.rem(place, blocks) * BLOCK, BLOCK)
            rows_start = pl.multiple_of(slot // slots * BLOCK, BLOCK)
            tile = jnp.dot(
                rows_ref[pl.ds(rows_start, BLOCK), :],
                held[place // blocks, :, pl.ds(start, BLOCK)],
                preferred_element_type=jnp.float32,
            )
            tiles[entry] = tile.astype(jnp.bfloat16)
        for n in range(group):
            entry = step * group + n

            @pl.when(entry < count_ref[0])
            def _():
                copy(entry).start()

        return carry

    lax.fori_loop(0, (count_ref[0] + group - 1) // group, some, 0)

    def finish(entry, carry):
        copy(entry).wait()
        return carry

    lax.fori_loop(0, count_ref[0], finish, 0)


def make_late(window, order, count, place, own, near, far, earlier):
    rows, frames = own.shape
    total = order.shape[0]
    anywhere = pl.BlockSpec(memory_space=pl.ANY)
    return pl.pallas_call(
        functools.partial(late_kernel, window=window, group=16),
        grid_spec=pltpu.PrefetchScalarGridSpec(
            num_scalar_prefetch=3,
            grid=(1,),
            in_specs=[anywhere] * 4,
            out_specs=anywhere,
            scratch_shapes=[
                pltpu.VMEM((rows, frames), jnp.bfloat16),
                pltpu.VMEM((2, frames, rows), jnp.bfloat16),
                pltpu.VMEM((total, BLOCK, BLOCK), jnp.bfloat16),
                pltpu.SemaphoreType.DMA((total,)),
            ],
        ),
        out_shape=jax.ShapeDtypeStruct(earlier.shape, earlier.dtype),
        input_output_aliases={6: 0},
        compiler_params=pltpu.CompilerParams(vmem_limit_bytes=VMEM_BYTES),
        cost_estimate=SMALL,
        name="late_tiles",
    )(order, count, place, own, near, far, earlier)


def after(value, *earlier):
    return lax.optimization_barrier((value,) + earlier)[0]


def on_device(bold, gm_index, partners):
    row_total = lax.axis_size("row")
    col_total = lax.axis_size("col")
    row = lax.axis_index("row")
    col = lax.axis_index("col")
    even = row % 2 == 0

    def other_col(value):
        return lax.ppermute(value, "col", [(0, 1), (1, 0)])

    one_up = [(i, i + 1) for i in range(row_total - 1)]
    one_down = [(i + 1, i) for i in range(row_total - 1)]
    ahead = [((i + 2 * (-1) ** i) % row_total, i) for i in range(row_total)]
    behind = [(i, source) for source, i in ahead]
    in_pair = [(i, i ^ 1) for i in range(row_total)]

    gm = gm_index.reshape(1, -1)
    col_arg = col.reshape(1).astype(jnp.int32)

    blocks, slots = partners.shape
    ids = jnp.maximum(partners, 0)
    slab = ids // blocks
    hop = (slab // col_total - row + 2 + row_total) % row_total
    kind = jnp.where((hop == 1) == even, 4, 3)
    kind = jnp.where(hop == 2, 0, jnp.where((hop == 0) | (hop >= 4), 2 - (even == (hop >= 4)), kind))
    away = (slab % col_total != col).astype(jnp.int32)
    within = ids % blocks
    present = partners >= 0
    late = present & (kind == 4)
    early = present & (kind != 4)
    early_place = jnp.where(early, (kind // 2 * 4 + away * 2 + kind % 2) * blocks + within, 0)
    late_place = jnp.where(late, away * blocks + within, 0)
    early, late = early.reshape(-1).astype(jnp.int32), late.reshape(-1)
    early_place = early_place.reshape(-1).astype(jnp.int32)
    late_place = late_place.reshape(-1).astype(jnp.int32)
    entries = jnp.arange(blocks * slots, dtype=jnp.int32)
    rank = jnp.sum((entries[None, :] < entries[:, None]) & late[None, :], axis=1)
    order = jnp.sum(
        jnp.where(late[None, :] & (rank[None, :] == entries[:, None]), entries[None, :], 0), axis=1
    ).astype(jnp.int32)
    count = jnp.sum(late).astype(jnp.int32).reshape(1)

    def halo(first, last):
        return lax.ppermute(last, "row", one_up), lax.ppermute(first, "row", one_down)

    def halves(*parts):
        near = jnp.stack(parts, 0)
        return [near, other_col(near)]

    def corner_of(low, high):
        return other_col(
            jnp.stack([jnp.where(col == 0, part[-1], part[0]) for part in (low, high)], 0)
        )

    windows = bold.shape[0]
    first_0, last_0, face_0 = make_faces(0, col_arg, bold)
    low_0, high_0 = halo(first_0, last_0)
    edge_0 = other_col(face_0)
    first_1, last_1, face_1 = make_faces(1, col_arg, after(bold, edge_0))
    edge_1 = other_col(face_1)
    corner_0 = corner_of(low_0, high_0)
    first_1, last_1 = after(first_1, low_0, high_0, edge_1), after(last_1, low_0, high_0, edge_1)
    low_1, high_1 = halo(first_1, last_1)
    own_0 = make_panel(col_arg, first_0, last_0, low_0, high_0, edge_0, corner_0, gm)
    ahead_0 = lax.ppermute(own_0, "row", ahead)
    behind_0 = lax.ppermute(own_0, "row", behind)
    low_1, high_1 = after(low_1, own_0), after(high_1, own_0)
    pair_0 = lax.ppermute(after(own_0, low_1, high_1), "row", in_pair)
    corner_1 = corner_of(low_1, high_1)
    own_1 = make_panel(col_arg, first_1, last_1, low_1, high_1, edge_1, corner_1, gm)
    ahead_0, behind_0 = after(ahead_0, own_1), after(behind_0, own_1)
    ahead_1 = lax.ppermute(own_1, "row", ahead)
    rest_0 = lax.ppermute(ahead_0, "row", in_pair)
    pair_1 = lax.ppermute(own_1, "row", in_pair)
    sources = halves(own_0, ahead_0) + halves(behind_0, pair_0)
    out, rows_0 = make_tiles(0, windows, early_place, early, sources, None)
    behind_1 = lax.ppermute(after(own_1, ahead_1), "row", behind)
    rest_1 = lax.ppermute(after(ahead_1, rest_0), "row", in_pair)
    behind_1, rest_0 = after(behind_1, out), after(rest_0, out)
    out = make_late(0, order, count, late_place, rows_0, rest_0, other_col(rest_0), out)
    sources = halves(own_1, ahead_1) + halves(behind_1, pair_1)
    out, rows_1 = make_tiles(1, windows, early_place, early, sources, out)
    rest_1 = after(rest_1, out)
    return make_late(1, order, count, late_place, rows_1, rest_1, other_col(rest_1), out)


def solution(mesh):
    in_specs = (P("subj", None, "row", "col", None), P(("row", "col")), P(("row", "col"), None))
    out_specs = P(("row", "col"), None, "subj", None, None)
    return jax.shard_map(
        on_device, mesh=mesh, in_specs=in_specs, out_specs=out_specs, check_vma=False
    )
```

```python
import functools
import math

import jax
import jax.numpy as jnp
from jax import lax
from jax.experimental import pallas as pl
from jax.experimental.pallas import tpu as pltpu
from jax.sharding import PartitionSpec as P

BLOCK = 128
SIDE = math.exp(-0.5) / (1.0 + 2.0 * math.exp(-0.5))
CENTRE = 1.0 / (1.0 + 2.0 * math.exp(-0.5))
SMALL = pl.CostEstimate(flops=1, bytes_accessed=1, transcendentals=0)
VMEM_BYTES = 24 * 1024 * 1024


def faces_kernel(col_ref, bold_ref, first_ref, last_ref, edge_ref, wide):
    frames, slab_x, slab_y, slab_z = bold_ref.shape[1:]
    per_frame = slab_x * slab_y
    wide[...] = bold_ref[0].reshape(frames * per_frame, slab_z).astype(jnp.float32)
    for x, layer_ref in enumerate((first_ref, last_ref)):
        for y in range(slab_y):
            plane = wide[pl.ds(x * slab_y + y, frames, stride=per_frame), :]
            layer_ref[y] = plane.astype(jnp.bfloat16)
        @pl.when(col_ref[0] == 0)
        def _():
            edge_ref[x] = layer_ref[slab_y - 1]

        @pl.when(col_ref[0] != 0)
        def _():
            edge_ref[x] = layer_ref[0]


def make_faces(window, col, bold):
    _, frames, slab_x, slab_y, slab_z = bold.shape
    layer = jax.ShapeDtypeStruct((slab_y, frames, slab_z), jnp.bfloat16)
    edge = jax.ShapeDtypeStruct((slab_x, frames, slab_z), jnp.bfloat16)
    whole = lambda array: pl.BlockSpec(array.shape, lambda _: (0,) * len(array.shape))
    return pl.pallas_call(
        faces_kernel,
        grid=(1,),
        in_specs=[
            pl.BlockSpec(memory_space=pltpu.SMEM),
            pl.BlockSpec((1, frames, slab_x, slab_y, slab_z), lambda _: (window, 0, 0, 0, 0)),
        ],
        out_specs=[whole(layer), whole(layer), whole(edge)],
        out_shape=[layer, layer, edge],
        scratch_shapes=[pltpu.VMEM((frames * slab_x * slab_y, slab_z), jnp.float32)],
        compiler_params=pltpu.CompilerParams(vmem_limit_bytes=VMEM_BYTES),
        cost_estimate=SMALL,
        name="faces",
    )(col, bold)


def panel_kernel(
    col_ref, first_ref, last_ref, low_ref, high_ref, edge_ref, corner_ref, gm_ref, out_ref,
    planes, scored,
):
    slab_y, frames, slab_z = first_ref.shape
    slab_x = edge_ref.shape[0]

    def along_x(before, here, after):
        return SIDE * before + CENTRE * here + SIDE * after

    for y in range(slab_y):
        layers = [ref[y].astype(jnp.float32) for ref in (low_ref, first_ref, last_ref, high_ref)]
        for x in range(slab_x):
            planes[x, y + 1] = along_x(*layers[x : x + 3])
    edges = [corner_ref[0], edge_ref[0], edge_ref[1], corner_ref[1]]
    edges = [edge.astype(jnp.float32) for edge in edges]
    for x in range(slab_x):
        edge = along_x(*edges[x : x + 3])
        planes[x, 0] = jnp.where(col_ref[0] == 0, 0.0, edge)
        planes[x, slab_y + 1] = jnp.where(col_ref[0] == 0, edge, 0.0)

    lane = lax.broadcasted_iota(jnp.int32, (frames, slab_z), 1)
    for x in range(slab_x):
        for y in range(slab_y):
            part = along_x(planes[x, y], planes[x, y + 1], planes[x, y + 2])
            before = jnp.where(lane == 0, 0.0, pltpu.roll(part, 1, 1))
            after = jnp.where(lane == slab_z - 1, 0.0, pltpu.roll(part, slab_z - 1, 1))
            smooth = along_x(before, part, after)
            centred = smooth - jnp.mean(smooth, axis=0, keepdims=True)
            spread = jnp.mean(centred * centred, axis=0, keepdims=True)
            value = centred * lax.rsqrt((spread + 1e-05) * frames)
            start = (x * slab_y + y) * slab_z
            scored[:, start : start + slab_z] = value.astype(jnp.bfloat16)

    voxels = slab_x * slab_y * slab_z
    rows = gm_ref.shape[1]
    step = 2 * BLOCK
    for start in range(0, rows, step):
        wanted = gm_ref[:, start : start + step]
        voxel = lax.broadcasted_iota(jnp.int32, (voxels, step), 0)
        chosen = jnp.where(voxel == wanted, 1.0, 0.0).astype(jnp.bfloat16)
        picked = jnp.dot(scored[...], chosen, preferred_element_type=jnp.float32)
        out_ref[:, start : start + step] = picked.astype(jnp.bfloat16)


def make_panel(col, first, last, low, high, edge, corner, gm):
    slab_y, frames, slab_z = first.shape
    slab_x = edge.shape[0]
    rows = gm.shape[1]
    voxels = slab_x * slab_y * slab_z
    whole = lambda array: pl.BlockSpec(array.shape, lambda _: (0,) * array.ndim)
    operands = (first, last, low, high, edge, corner, gm)
    return pl.pallas_call(
        panel_kernel,
        grid=(1,),
        in_specs=[pl.BlockSpec(memory_space=pltpu.SMEM)] + [whole(value) for value in operands],
        out_specs=pl.BlockSpec((frames, rows), lambda _: (0, 0)),
        out_shape=jax.ShapeDtypeStruct((frames, rows), jnp.bfloat16),
        scratch_shapes=[
            pltpu.VMEM((slab_x, slab_y + 2, frames, slab_z), jnp.float32),
            pltpu.VMEM((frames, voxels), jnp.bfloat16),
        ],
        compiler_params=pltpu.CompilerParams(vmem_limit_bytes=VMEM_BYTES),
        cost_estimate=SMALL,
        name="blur_score_pick",
    )(col, *operands)


def tiles_kernel(place_ref, present_ref, *refs, sources, window):
    parts = refs[: len(sources)]
    out_ref, held, tiles, sems, out_sems = refs[-5:]
    blocks, slots = out_ref.shape[:2]

    loads = []
    for n, (part, (first, start)) in enumerate(zip(parts, sources)):
        if len(part.shape) == 3:
            target = held.at[pl.ds(first, part.shape[0])]
        else:
            target = held.at[first, pl.ds(start, part.shape[0])]
        loads.append(pltpu.make_async_copy(part, target, sems.at[n]))
        loads[-1].start()
    for load in loads:
        load.wait()

    def partner(index):
        place = place_ref[index]
        start = pl.multiple_of(lax.rem(place, blocks) * BLOCK, BLOCK)
        return held[lax.div(place, blocks), :, pl.ds(start, BLOCK)]

    stores = []
    for block in range(blocks):
        own = held[0, :, block * BLOCK : (block + 1) * BLOCK].T
        for slot in range(0, slots, 2):
            index = block * slots + slot
            pair = jnp.concatenate([partner(index), partner(index + 1)], axis=1)
            both = jnp.dot(own, pair, preferred_element_type=jnp.float32)
            for n in range(2):
                tile = both[:, n * BLOCK : (n + 1) * BLOCK]
                tile = jnp.where(present_ref[index + n] != 0, tile, 0.0)
                tiles[block, slot + n] = tile.astype(jnp.bfloat16)
        stores.append(
            pltpu.make_async_copy(tiles.at[block], out_ref.at[block, :, window], out_sems.at[block])
        )
        stores[-1].start()
    for store in stores:
        store.wait()


def make_tiles(window, windows, place, present, sources, earlier):
    _, frames, rows = sources[0][2].shape
    blocks = rows // BLOCK
    slots = place.shape[0] // blocks
    count = len(sources)
    where = tuple(source[:2] for source in sources)
    sources = [source[2] for source in sources]
    anywhere = pl.BlockSpec(memory_space=pl.ANY)
    operands = list(sources) + ([] if earlier is None else [earlier])
    return pl.pallas_call(
        functools.partial(tiles_kernel, sources=where, window=window),
        grid_spec=pltpu.PrefetchScalarGridSpec(
            num_scalar_prefetch=2,
            grid=(1,),
            in_specs=[anywhere] * len(operands),
            out_specs=anywhere,
            scratch_shapes=[
                pltpu.VMEM((10, frames, rows), jnp.bfloat16),
                pltpu.VMEM((blocks, slots, BLOCK, BLOCK), jnp.bfloat16),
                pltpu.SemaphoreType.DMA((count,)),
                pltpu.SemaphoreType.DMA((blocks,)),
            ],
        ),
        out_shape=jax.ShapeDtypeStruct((blocks, slots, windows, BLOCK, BLOCK), jnp.bfloat16),
        input_output_aliases={} if earlier is None else {2 + count: 0},
        compiler_params=pltpu.CompilerParams(vmem_limit_bytes=VMEM_BYTES),
        cost_estimate=SMALL,
        name="tiles",
    )(place, present, *operands)


def after(value, *earlier):
    return lax.optimization_barrier((value,) + earlier)[0]


def on_device(bold, gm_index, partners):
    row_total = lax.axis_size("row")
    col_total = lax.axis_size("col")
    row = lax.axis_index("row")
    col = lax.axis_index("col")
    even = row % 2 == 0

    def other_col(value):
        return lax.ppermute(value, "col", [(0, 1), (1, 0)])

    one_up = [(i, i + 1) for i in range(row_total - 1)]
    one_down = [(i + 1, i) for i in range(row_total - 1)]
    ahead = [((i + 2 * (-1) ** i) % row_total, i) for i in range(row_total)]
    behind = [(i, source) for source, i in ahead]
    in_pair = [(i, i ^ 1) for i in range(row_total)]

    gm = gm_index.reshape(1, -1)
    col_arg = col.reshape(1).astype(jnp.int32)

    blocks, slots = partners.shape
    ids = jnp.maximum(partners, 0)
    slab = ids // blocks
    hop = (slab // col_total - row + 2 + row_total) % row_total
    kind = jnp.where((hop == 1) == even, 4, 3)
    kind = jnp.where(hop == 2, 0, jnp.where((hop == 0) | (hop >= 4), 2 - (even == (hop >= 4)), kind))
    away = (slab % col_total != col).astype(jnp.int32)
    within = ids % blocks
    present = partners >= 0
    part = jnp.where(kind < 2, kind + 2 * away, 2 * kind + away)
    place = jnp.where(present, part * blocks + within, 0).reshape(-1).astype(jnp.int32)
    present = present.reshape(-1).astype(jnp.int32)

    def halo(first, last):
        return lax.ppermute(last, "row", one_up), lax.ppermute(first, "row", one_down)

    def both(first, *parts):
        near = jnp.stack(parts, 0)
        return [(first, 0, near), (first + len(parts), 0, other_col(near))]

    def corner_of(low, high):
        return other_col(
            jnp.stack([jnp.where(col == 0, part[-1], part[0]) for part in (low, high)], 0)
        )

    windows = bold.shape[0]
    first_0, last_0, face_0 = make_faces(0, col_arg, bold)
    low_0, high_0 = halo(first_0, last_0)
    edge_0 = other_col(face_0)
    first_1, last_1, face_1 = make_faces(1, col_arg, after(bold, edge_0))
    edge_1 = other_col(face_1)
    corner_0 = corner_of(low_0, high_0)
    first_1, last_1 = after(first_1, low_0, high_0, edge_1), after(last_1, low_0, high_0, edge_1)
    low_1, high_1 = halo(first_1, last_1)
    own_0 = make_panel(col_arg, first_0, last_0, low_0, high_0, edge_0, corner_0, gm)
    ahead_0 = lax.ppermute(own_0, "row", ahead)
    behind_0 = lax.ppermute(own_0, "row", behind)
    low_1, high_1 = after(low_1, own_0), after(high_1, own_0)
    ahead_0 = after(ahead_0, low_1, high_1)
    pair_0 = lax.ppermute(after(own_0, low_1, high_1), "row", in_pair)
    rest_0 = lax.ppermute(ahead_0, "row", in_pair)
    corner_1 = corner_of(low_1, high_1)
    own_1 = make_panel(col_arg, first_1, last_1, low_1, high_1, edge_1, corner_1, gm)
    ahead_1 = lax.ppermute(own_1, "row", ahead)
    pair_1 = lax.ppermute(own_1, "row", in_pair)
    pair_0, rest_0 = after(pair_0, own_1), after(rest_0, own_1)
    behind_0 = after(behind_0, own_1)
    sources = both(0, own_0, ahead_0) + both(4, behind_0) + both(6, pair_0)
    ahead_1 = after(ahead_1, rest_0, behind_0, pair_0)
    behind_1 = lax.ppermute(after(own_1, ahead_1), "row", behind)
    rest_1 = lax.ppermute(ahead_1, "row", in_pair)
    swapped = [source[2] for source in sources]
    pair_1 = after(pair_1, ahead_1, *swapped)
    behind_1 = after(behind_1, pair_1)
    out = make_tiles(0, windows, place, present, sources + both(8, rest_0), None)
    sources = both(0, own_1, ahead_1) + both(4, behind_1) + both(6, pair_1)
    rest_1 = after(rest_1, out, *(source[2] for source in sources))
    return make_tiles(1, windows, place, present, sources + both(8, rest_1), out)


def solution(mesh):
    in_specs = (P("subj", None, "row", "col", None), P(("row", "col")), P(("row", "col"), None))
    out_specs = P(("row", "col"), None, "subj", None, None)
    return jax.shard_map(
        on_device, mesh=mesh, in_specs=in_specs, out_specs=out_specs, check_vma=False
    )
```

```python
import functools
import math

import jax
import jax.numpy as jnp
from jax import lax
from jax.experimental import pallas as pl
from jax.experimental.pallas import tpu as pltpu
from jax.sharding import PartitionSpec as P

BLOCK = 128
SIDE = math.exp(-0.5) / (1.0 + 2.0 * math.exp(-0.5))
CENTRE = 1.0 / (1.0 + 2.0 * math.exp(-0.5))
SMALL = pl.CostEstimate(flops=1, bytes_accessed=1, transcendentals=0)
VMEM_BYTES = 24 * 1024 * 1024
TILES_VMEM_BYTES = 60 * 1024 * 1024


def faces_kernel(col_ref, bold_ref, first_ref, last_ref, edge_ref, wide):
    frames, slab_x, slab_y, slab_z = bold_ref.shape[1:]
    per_frame = slab_x * slab_y
    wide[...] = bold_ref[0].reshape(frames * per_frame, slab_z).astype(jnp.float32)
    for x, layer_ref in enumerate((first_ref, last_ref)):
        for y in range(slab_y):
            plane = wide[pl.ds(x * slab_y + y, frames, stride=per_frame), :]
            layer_ref[y] = plane.astype(jnp.bfloat16)
        @pl.when(col_ref[0] == 0)
        def _():
            edge_ref[x] = layer_ref[slab_y - 1]

        @pl.when(col_ref[0] != 0)
        def _():
            edge_ref[x] = layer_ref[0]


def make_faces(window, col, bold):
    _, frames, slab_x, slab_y, slab_z = bold.shape
    layer = jax.ShapeDtypeStruct((slab_y, frames, slab_z), jnp.bfloat16)
    edge = jax.ShapeDtypeStruct((slab_x, frames, slab_z), jnp.bfloat16)
    whole = lambda array: pl.BlockSpec(array.shape, lambda _: (0,) * len(array.shape))
    return pl.pallas_call(
        faces_kernel,
        grid=(1,),
        in_specs=[
            pl.BlockSpec(memory_space=pltpu.SMEM),
            pl.BlockSpec((1, frames, slab_x, slab_y, slab_z), lambda _: (window, 0, 0, 0, 0)),
        ],
        out_specs=[whole(layer), whole(layer), whole(edge)],
        out_shape=[layer, layer, edge],
        scratch_shapes=[pltpu.VMEM((frames * slab_x * slab_y, slab_z), jnp.float32)],
        compiler_params=pltpu.CompilerParams(vmem_limit_bytes=VMEM_BYTES),
        cost_estimate=SMALL,
        name="faces",
    )(col, bold)


def panel_kernel(
    col_ref, first_ref, last_ref, low_ref, high_ref, edge_ref, corner_ref, gm_ref, out_ref,
    planes, scored,
):
    slab_y, frames, slab_z = first_ref.shape
    slab_x = edge_ref.shape[0]

    def along_x(before, here, after):
        return SIDE * before + CENTRE * here + SIDE * after

    for y in range(slab_y):
        layers = [ref[y].astype(jnp.float32) for ref in (low_ref, first_ref, last_ref, high_ref)]
        for x in range(slab_x):
            planes[x, y + 1] = along_x(*layers[x : x + 3])
    edges = [corner_ref[0], edge_ref[0], edge_ref[1], corner_ref[1]]
    edges = [edge.astype(jnp.float32) for edge in edges]
    for x in range(slab_x):
        edge = along_x(*edges[x : x + 3])
        planes[x, 0] = jnp.where(col_ref[0] == 0, 0.0, edge)
        planes[x, slab_y + 1] = jnp.where(col_ref[0] == 0, edge, 0.0)

    lane = lax.broadcasted_iota(jnp.int32, (frames, slab_z), 1)
    for x in range(slab_x):
        for y in range(slab_y):
            part = along_x(planes[x, y], planes[x, y + 1], planes[x, y + 2])
            before = jnp.where(lane == 0, 0.0, pltpu.roll(part, 1, 1))
            after = jnp.where(lane == slab_z - 1, 0.0, pltpu.roll(part, slab_z - 1, 1))
            smooth = along_x(before, part, after)
            centred = smooth - jnp.mean(smooth, axis=0, keepdims=True)
            spread = jnp.mean(centred * centred, axis=0, keepdims=True)
            value = centred * lax.rsqrt((spread + 1e-05) * frames)
            start = (x * slab_y + y) * slab_z
            scored[:, start : start + slab_z] = value.astype(jnp.bfloat16)

    voxels = slab_x * slab_y * slab_z
    rows = gm_ref.shape[1]
    step = 2 * BLOCK
    for start in range(0, rows, step):
        wanted = gm_ref[:, start : start + step]
        voxel = lax.broadcasted_iota(jnp.int32, (voxels, step), 0)
        chosen = jnp.where(voxel == wanted, 1.0, 0.0).astype(jnp.bfloat16)
        picked = jnp.dot(scored[...], chosen, preferred_element_type=jnp.float32)
        out_ref[:, start : start + step] = picked.astype(jnp.bfloat16)


def make_panel(col, first, last, low, high, edge, corner, gm):
    slab_y, frames, slab_z = first.shape
    slab_x = edge.shape[0]
    rows = gm.shape[1]
    voxels = slab_x * slab_y * slab_z
    whole = lambda array: pl.BlockSpec(array.shape, lambda _: (0,) * array.ndim)
    operands = (first, last, low, high, edge, corner, gm)
    return pl.pallas_call(
        panel_kernel,
        grid=(1,),
        in_specs=[pl.BlockSpec(memory_space=pltpu.SMEM)] + [whole(value) for value in operands],
        out_specs=pl.BlockSpec((frames, rows), lambda _: (0, 0)),
        out_shape=jax.ShapeDtypeStruct((frames, rows), jnp.bfloat16),
        scratch_shapes=[
            pltpu.VMEM((slab_x, slab_y + 2, frames, slab_z), jnp.float32),
            pltpu.VMEM((frames, voxels), jnp.bfloat16),
        ],
        compiler_params=pltpu.CompilerParams(vmem_limit_bytes=VMEM_BYTES),
        cost_estimate=SMALL,
        name="blur_score_pick",
    )(col, *operands)


def tiles_kernel(place_ref, present_ref, *refs, sources, window):
    parts = refs[: len(sources)]
    out_ref, held, tiles, sems, out_sems = refs[-5:]
    blocks, slots = out_ref.shape[:2]

    loads = []
    for n, (part, (first, start)) in enumerate(zip(parts, sources)):
        if len(part.shape) == 3:
            target = held.at[pl.ds(first, part.shape[0])]
        else:
            target = held.at[first, pl.ds(start, part.shape[0])]
        loads.append(pltpu.make_async_copy(part, target, sems.at[n]))
        loads[-1].start()
    for load in loads:
        load.wait()

    def partner(index):
        place = place_ref[index]
        start = pl.multiple_of(lax.rem(place, blocks) * BLOCK, BLOCK)
        return held[lax.div(place, blocks), :, pl.ds(start, BLOCK)]

    stores = []
    for block in range(blocks):
        own = held[0, :, block * BLOCK : (block + 1) * BLOCK].T
        for slot in range(0, slots, 2):
            index = block * slots + slot
            pair = jnp.concatenate([partner(index), partner(index + 1)], axis=1)
            both = jnp.dot(own, pair, preferred_element_type=jnp.float32)
            for n in range(2):
                tile = both[:, n * BLOCK : (n + 1) * BLOCK]
                tile = jnp.where(present_ref[index + n] != 0, tile, 0.0)
                tiles[block, slot + n] = tile.astype(jnp.bfloat16)
        stores.append(
            pltpu.make_async_copy(tiles.at[block], out_ref.at[block, :, window], out_sems.at[block])
        )
        stores[-1].start()
    for store in stores:
        store.wait()


def make_tiles(window, windows, place, present, sources, earlier):
    _, frames, rows = sources[0][2].shape
    blocks = rows // BLOCK
    slots = place.shape[0] // blocks
    count = len(sources)
    where = tuple(source[:2] for source in sources)
    sources = [source[2] for source in sources]
    anywhere = pl.BlockSpec(memory_space=pl.ANY)
    operands = list(sources) + ([] if earlier is None else [earlier])
    return pl.pallas_call(
        functools.partial(tiles_kernel, sources=where, window=window),
        grid_spec=pltpu.PrefetchScalarGridSpec(
            num_scalar_prefetch=2,
            grid=(1,),
            in_specs=[anywhere] * len(operands),
            out_specs=anywhere,
            scratch_shapes=[
                pltpu.VMEM((10, frames, rows), jnp.bfloat16),
                pltpu.VMEM((blocks, slots, BLOCK, BLOCK), jnp.bfloat16),
                pltpu.SemaphoreType.DMA((count,)),
                pltpu.SemaphoreType.DMA((blocks,)),
            ],
        ),
        out_shape=jax.ShapeDtypeStruct((blocks, slots, windows, BLOCK, BLOCK), jnp.bfloat16),
        input_output_aliases={} if earlier is None else {2 + count: 0},
        compiler_params=pltpu.CompilerParams(vmem_limit_bytes=TILES_VMEM_BYTES),
        cost_estimate=SMALL,
        name="tiles",
    )(place, present, *operands)


def after(value, *earlier):
    return lax.optimization_barrier((value,) + earlier)[0]


def on_device(bold, gm_index, partners):
    row_total = lax.axis_size("row")
    col_total = lax.axis_size("col")
    row = lax.axis_index("row")
    col = lax.axis_index("col")
    even = row % 2 == 0

    def other_col(value):
        return lax.ppermute(value, "col", [(0, 1), (1, 0)])

    one_up = [(i, i + 1) for i in range(row_total - 1)]
    one_down = [(i + 1, i) for i in range(row_total - 1)]
    ahead = [((i + 2 * (-1) ** i) % row_total, i) for i in range(row_total)]
    behind = [(i, source) for source, i in ahead]
    in_pair = [(i, i ^ 1) for i in range(row_total)]

    gm = gm_index.reshape(1, -1)
    col_arg = col.reshape(1).astype(jnp.int32)

    blocks, slots = partners.shape
    ids = jnp.maximum(partners, 0)
    slab = ids // blocks
    hop = (slab // col_total - row + 2 + row_total) % row_total
    kind = jnp.where((hop == 1) == even, 4, 3)
    kind = jnp.where(hop == 2, 0, jnp.where((hop == 0) | (hop >= 4), 2 - (even == (hop >= 4)), kind))
    away = (slab % col_total != col).astype(jnp.int32)
    within = ids % blocks
    present = partners >= 0
    part = jnp.where(kind < 2, kind + 2 * away, 2 * kind + away)
    place = jnp.where(present, part * blocks + within, 0).reshape(-1).astype(jnp.int32)
    present = present.reshape(-1).astype(jnp.int32)

    def halo(first, last):
        return lax.ppermute(last, "row", one_up), lax.ppermute(first, "row", one_down)

    def both(first, *parts):
        near = jnp.stack(parts, 0)
        return [(first, 0, near), (first + len(parts), 0, other_col(near))]

    def corner_of(low, high):
        return other_col(
            jnp.stack([jnp.where(col == 0, part[-1], part[0]) for part in (low, high)], 0)
        )

    windows = bold.shape[0]
    first_0, last_0, face_0 = make_faces(0, col_arg, bold)
    low_0, high_0 = halo(first_0, last_0)
    edge_0 = other_col(face_0)
    first_1, last_1, face_1 = make_faces(1, col_arg, after(bold, edge_0))
    edge_1 = other_col(face_1)
    corner_0 = corner_of(low_0, high_0)
    first_1, last_1 = after(first_1, low_0, high_0, edge_1), after(last_1, low_0, high_0, edge_1)
    low_1, high_1 = halo(first_1, last_1)
    own_0 = make_panel(col_arg, first_0, last_0, low_0, high_0, edge_0, corner_0, gm)
    ahead_0 = lax.ppermute(own_0, "row", ahead)
    behind_0 = lax.ppermute(own_0, "row", behind)
    low_1, high_1 = after(low_1, own_0), after(high_1, own_0)
    ahead_0 = after(ahead_0, low_1, high_1)
    pair_0 = lax.ppermute(after(own_0, low_1, high_1), "row", in_pair)
    rest_0 = lax.ppermute(ahead_0, "row", in_pair)
    corner_1 = corner_of(low_1, high_1)
    own_1 = make_panel(col_arg, first_1, last_1, low_1, high_1, edge_1, corner_1, gm)
    ahead_1 = lax.ppermute(own_1, "row", ahead)
    pair_1 = lax.ppermute(own_1, "row", in_pair)
    pair_0, rest_0 = after(pair_0, own_1), after(rest_0, own_1)
    behind_0 = after(behind_0, own_1)
    sources = both(0, own_0, ahead_0) + both(4, behind_0) + both(6, pair_0)
    swapped = [source[2] for source in sources]
    ahead_1 = after(ahead_1, rest_0, *swapped)
    behind_1 = lax.ppermute(after(own_1, ahead_1), "row", behind)
    rest_1 = lax.ppermute(ahead_1, "row", in_pair)
    pair_1 = after(pair_1, ahead_1)
    behind_1 = after(behind_1, pair_1)
    out = make_tiles(0, windows, place, present, sources + both(8, rest_0), None)
    sources = both(0, own_1, ahead_1) + both(4, behind_1) + both(6, pair_1)
    rest_1 = after(rest_1, out, *(source[2] for source in sources))
    return make_tiles(1, windows, place, present, sources + both(8, rest_1), out)


def solution(mesh):
    in_specs = (P("subj", None, "row", "col", None), P(("row", "col")), P(("row", "col"), None))
    out_specs = P(("row", "col"), None, "subj", None, None)
    return jax.shard_map(
        on_device, mesh=mesh, in_specs=in_specs, out_specs=out_specs, check_vma=False
    )
```

```python
import functools
import math

import jax
import jax.numpy as jnp
from jax import lax
from jax.experimental import pallas as pl
from jax.experimental.pallas import tpu as pltpu
from jax.sharding import PartitionSpec as P

BLOCK = 128
SIDE = math.exp(-0.5) / (1.0 + 2.0 * math.exp(-0.5))
CENTRE = 1.0 / (1.0 + 2.0 * math.exp(-0.5))
SMALL = pl.CostEstimate(flops=1, bytes_accessed=1, transcendentals=0)
VMEM_BYTES = 24 * 1024 * 1024
TILES_VMEM_BYTES = 60 * 1024 * 1024


def faces_kernel(col_ref, bold_ref, first_ref, last_ref, edge_ref, wide):
    frames, slab_x, slab_y, slab_z = bold_ref.shape[1:]
    per_frame = slab_x * slab_y
    wide[...] = bold_ref[0].reshape(frames * per_frame, slab_z).astype(jnp.float32)
    for x, layer_ref in enumerate((first_ref, last_ref)):
        for y in range(slab_y):
            plane = wide[pl.ds(x * slab_y + y, frames, stride=per_frame), :]
            layer_ref[y] = plane.astype(jnp.bfloat16)
        @pl.when(col_ref[0] == 0)
        def _():
            edge_ref[x] = layer_ref[slab_y - 1]

        @pl.when(col_ref[0] != 0)
        def _():
            edge_ref[x] = layer_ref[0]


def make_faces(window, col, bold):
    _, frames, slab_x, slab_y, slab_z = bold.shape
    layer = jax.ShapeDtypeStruct((slab_y, frames, slab_z), jnp.bfloat16)
    edge = jax.ShapeDtypeStruct((slab_x, frames, slab_z), jnp.bfloat16)
    whole = lambda array: pl.BlockSpec(array.shape, lambda _: (0,) * len(array.shape))
    return pl.pallas_call(
        faces_kernel,
        grid=(1,),
        in_specs=[
            pl.BlockSpec(memory_space=pltpu.SMEM),
            pl.BlockSpec((1, frames, slab_x, slab_y, slab_z), lambda _: (window, 0, 0, 0, 0)),
        ],
        out_specs=[whole(layer), whole(layer), whole(edge)],
        out_shape=[layer, layer, edge],
        scratch_shapes=[pltpu.VMEM((frames * slab_x * slab_y, slab_z), jnp.float32)],
        compiler_params=pltpu.CompilerParams(vmem_limit_bytes=VMEM_BYTES),
        cost_estimate=SMALL,
        name="faces",
    )(col, bold)


def panel_kernel(
    col_ref, first_ref, last_ref, low_ref, high_ref, edge_ref, corner_ref, gm_ref, out_ref,
    planes, scored,
):
    slab_y, frames, slab_z = first_ref.shape
    slab_x = edge_ref.shape[0]

    def along_x(before, here, after):
        return SIDE * before + CENTRE * here + SIDE * after

    for y in range(slab_y):
        layers = [ref[y].astype(jnp.float32) for ref in (low_ref, first_ref, last_ref, high_ref)]
        for x in range(slab_x):
            planes[x, y + 1] = along_x(*layers[x : x + 3])
    edges = [corner_ref[0], edge_ref[0], edge_ref[1], corner_ref[1]]
    edges = [edge.astype(jnp.float32) for edge in edges]
    for x in range(slab_x):
        edge = along_x(*edges[x : x + 3])
        planes[x, 0] = jnp.where(col_ref[0] == 0, 0.0, edge)
        planes[x, slab_y + 1] = jnp.where(col_ref[0] == 0, edge, 0.0)

    lane = lax.broadcasted_iota(jnp.int32, (frames, slab_z), 1)
    for x in range(slab_x):
        for y in range(slab_y):
            part = along_x(planes[x, y], planes[x, y + 1], planes[x, y + 2])
            before = jnp.where(lane == 0, 0.0, pltpu.roll(part, 1, 1))
            after = jnp.where(lane == slab_z - 1, 0.0, pltpu.roll(part, slab_z - 1, 1))
            smooth = along_x(before, part, after)
            centred = smooth - jnp.mean(smooth, axis=0, keepdims=True)
            spread = jnp.mean(centred * centred, axis=0, keepdims=True)
            value = centred * lax.rsqrt((spread + 1e-05) * frames)
            start = (x * slab_y + y) * slab_z
            scored[:, start : start + slab_z] = value.astype(jnp.bfloat16)

    voxels = slab_x * slab_y * slab_z
    rows = gm_ref.shape[1]
    step = 2 * BLOCK
    for start in range(0, rows, step):
        wanted = gm_ref[:, start : start + step]
        voxel = lax.broadcasted_iota(jnp.int32, (voxels, step), 0)
        chosen = jnp.where(voxel == wanted, 1.0, 0.0).astype(jnp.bfloat16)
        picked = jnp.dot(scored[...], chosen, preferred_element_type=jnp.float32)
        out_ref[:, start : start + step] = picked.astype(jnp.bfloat16)


def make_panel(col, first, last, low, high, edge, corner, gm):
    slab_y, frames, slab_z = first.shape
    slab_x = edge.shape[0]
    rows = gm.shape[1]
    voxels = slab_x * slab_y * slab_z
    whole = lambda array: pl.BlockSpec(array.shape, lambda _: (0,) * array.ndim)
    operands = (first, last, low, high, edge, corner, gm)
    return pl.pallas_call(
        panel_kernel,
        grid=(1,),
        in_specs=[pl.BlockSpec(memory_space=pltpu.SMEM)] + [whole(value) for value in operands],
        out_specs=pl.BlockSpec((frames, rows), lambda _: (0, 0)),
        out_shape=jax.ShapeDtypeStruct((frames, rows), jnp.bfloat16),
        scratch_shapes=[
            pltpu.VMEM((slab_x, slab_y + 2, frames, slab_z), jnp.float32),
            pltpu.VMEM((frames, voxels), jnp.bfloat16),
        ],
        compiler_params=pltpu.CompilerParams(vmem_limit_bytes=VMEM_BYTES),
        cost_estimate=SMALL,
        name="blur_score_pick",
    )(col, *operands)


def tiles_kernel(place_ref, present_ref, *refs, sources, window):
    parts = refs[:sources]
    out_ref, held, tiles, sems, out_sems = refs[-5:]
    blocks, slots = out_ref.shape[:2]

    loads = []
    first = 0
    for n, part in enumerate(parts):
        target = held.at[pl.ds(first, part.shape[0])]
        loads.append(pltpu.make_async_copy(part, target, sems.at[n]))
        loads[-1].start()
        first += part.shape[0]
    for load in loads:
        load.wait()

    def partner(index):
        place = place_ref[index]
        start = pl.multiple_of(lax.rem(place, blocks) * BLOCK, BLOCK)
        return held[lax.div(place, blocks), :, pl.ds(start, BLOCK)]

    stores = []
    for block in range(blocks):
        own = held[0, :, block * BLOCK : (block + 1) * BLOCK].T
        for slot in range(0, slots, 2):
            index = block * slots + slot
            pair = jnp.concatenate([partner(index), partner(index + 1)], axis=1)
            both = jnp.dot(own, pair, preferred_element_type=jnp.float32)
            for n in range(2):
                tile = both[:, n * BLOCK : (n + 1) * BLOCK]
                tile = jnp.where(present_ref[index + n] != 0, tile, 0.0)
                tiles[block, slot + n] = tile.astype(jnp.bfloat16)
        stores.append(
            pltpu.make_async_copy(tiles.at[block], out_ref.at[block, :, window], out_sems.at[block])
        )
        stores[-1].start()
    for store in stores:
        store.wait()


def make_tiles(window, windows, place, present, sources, earlier):
    frames, rows = sources[0].shape[1:]
    total = sum(source.shape[0] for source in sources)
    blocks = rows // BLOCK
    slots = place.shape[0] // blocks
    count = len(sources)
    anywhere = pl.BlockSpec(memory_space=pl.ANY)
    operands = list(sources) + ([] if earlier is None else [earlier])
    return pl.pallas_call(
        functools.partial(tiles_kernel, sources=count, window=window),
        grid_spec=pltpu.PrefetchScalarGridSpec(
            num_scalar_prefetch=2,
            grid=(1,),
            in_specs=[anywhere] * len(operands),
            out_specs=anywhere,
            scratch_shapes=[
                pltpu.VMEM((total, frames, rows), jnp.bfloat16),
                pltpu.VMEM((blocks, slots, BLOCK, BLOCK), jnp.bfloat16),
                pltpu.SemaphoreType.DMA((count,)),
                pltpu.SemaphoreType.DMA((blocks,)),
            ],
        ),
        out_shape=jax.ShapeDtypeStruct((blocks, slots, windows, BLOCK, BLOCK), jnp.bfloat16),
        input_output_aliases={} if earlier is None else {2 + count: 0},
        compiler_params=pltpu.CompilerParams(vmem_limit_bytes=TILES_VMEM_BYTES),
        cost_estimate=SMALL,
        name="tiles",
    )(place, present, *operands)


def after(value, *earlier):
    return lax.optimization_barrier((value,) + earlier)[0]


def on_device(bold, gm_index, partners):
    row_total = lax.axis_size("row")
    col_total = lax.axis_size("col")
    row = lax.axis_index("row")
    col = lax.axis_index("col")
    even = row % 2 == 0

    def other_col(value):
        return lax.ppermute(value, "col", [(0, 1), (1, 0)])

    one_up = [(i, i + 1) for i in range(row_total - 1)]
    one_down = [(i + 1, i) for i in range(row_total - 1)]
    ahead = [((i + 2 * (-1) ** i) % row_total, i) for i in range(row_total)]
    behind = [(i, source) for source, i in ahead]
    in_pair = [(i, i ^ 1) for i in range(row_total)]

    gm = gm_index.reshape(1, -1)
    col_arg = col.reshape(1).astype(jnp.int32)

    blocks, slots = partners.shape
    ids = jnp.maximum(partners, 0)
    slab = ids // blocks
    hop = (slab // col_total - row + 2 + row_total) % row_total
    kind = jnp.where((hop == 1) == even, 4, 3)
    kind = jnp.where(hop == 2, 0, jnp.where((hop == 0) | (hop >= 4), 2 - (even == (hop >= 4)), kind))
    away = (slab % col_total != col).astype(jnp.int32)
    within = ids % blocks
    present = partners >= 0
    parts_0 = jnp.where(kind == 4, 8 + away, kind + 4 * away)
    parts_1 = jnp.where(kind < 2, kind + 2 * away, 2 * kind + away)
    place_0, place_1 = (
        jnp.where(present, part * blocks + within, 0).reshape(-1).astype(jnp.int32)
        for part in (parts_0, parts_1)
    )
    present = present.reshape(-1).astype(jnp.int32)

    def halo(first, last):
        return lax.ppermute(last, "row", one_up), lax.ppermute(first, "row", one_down)

    def both(*parts):
        near = jnp.stack(parts, 0)
        return [near, other_col(near)]

    def corner_of(low, high):
        return other_col(
            jnp.stack([jnp.where(col == 0, part[-1], part[0]) for part in (low, high)], 0)
        )

    windows = bold.shape[0]
    first_0, last_0, face_0 = make_faces(0, col_arg, bold)
    low_0, high_0 = halo(first_0, last_0)
    edge_0 = other_col(face_0)
    first_1, last_1, face_1 = make_faces(1, col_arg, after(bold, edge_0))
    edge_1 = other_col(face_1)
    corner_0 = corner_of(low_0, high_0)
    first_1, last_1 = after(first_1, low_0, high_0, edge_1), after(last_1, low_0, high_0, edge_1)
    low_1, high_1 = halo(first_1, last_1)
    own_0 = make_panel(col_arg, first_0, last_0, low_0, high_0, edge_0, corner_0, gm)
    ahead_0 = lax.ppermute(own_0, "row", ahead)
    behind_0 = lax.ppermute(own_0, "row", behind)
    low_1, high_1 = after(low_1, own_0), after(high_1, own_0)
    pair_0 = lax.ppermute(after(own_0, low_1, high_1), "row", in_pair)
    corner_1 = corner_of(low_1, high_1)
    own_1 = make_panel(col_arg, first_1, last_1, low_1, high_1, edge_1, corner_1, gm)
    ahead_1 = lax.ppermute(own_1, "row", ahead)
    ahead_0 = after(ahead_0, own_1)
    rest_0 = lax.ppermute(ahead_0, "row", in_pair)
    pair_1 = lax.ppermute(own_1, "row", in_pair)
    behind_0, pair_0 = after(behind_0, own_1), after(pair_0, own_1)
    sources = both(own_0, ahead_0, behind_0, pair_0)
    ahead_1 = after(ahead_1, behind_0, pair_0)
    behind_1 = lax.ppermute(after(own_1, ahead_1), "row", behind)
    rest_0 = after(rest_0, ahead_1)
    rest_1 = lax.ppermute(ahead_1, "row", in_pair)
    pair_1 = after(pair_1, rest_0)
    behind_1 = after(behind_1, pair_1)
    out = make_tiles(0, windows, place_0, present, sources + both(rest_0), None)
    sources = both(own_1, ahead_1) + both(behind_1) + both(pair_1)
    rest_1 = after(rest_1, out, *sources)
    return make_tiles(1, windows, place_1, present, sources + both(rest_1), out)


def solution(mesh):
    in_specs = (P("subj", None, "row", "col", None), P(("row", "col")), P(("row", "col"), None))
    out_specs = P(("row", "col"), None, "subj", None, None)
    return jax.shard_map(
        on_device, mesh=mesh, in_specs=in_specs, out_specs=out_specs, check_vma=False
    )
```

```python
import functools
import math

import jax
import jax.numpy as jnp
from jax import lax
from jax.experimental import pallas as pl
from jax.experimental.pallas import tpu as pltpu
from jax.sharding import PartitionSpec as P

BLOCK = 128
SIDE = math.exp(-0.5) / (1.0 + 2.0 * math.exp(-0.5))
CENTRE = 1.0 / (1.0 + 2.0 * math.exp(-0.5))
SMALL = pl.CostEstimate(flops=1, bytes_accessed=1, transcendentals=0)
VMEM_BYTES = 24 * 1024 * 1024
TILES_VMEM_BYTES = 60 * 1024 * 1024


def faces_kernel(col_ref, bold_ref, first_ref, last_ref, edge_ref, wide):
    frames, slab_x, slab_y, slab_z = bold_ref.shape[1:]
    per_frame = slab_x * slab_y
    wide[...] = bold_ref[0].reshape(frames * per_frame, slab_z).astype(jnp.float32)
    for x, layer_ref in enumerate((first_ref, last_ref)):
        for y in range(slab_y):
            plane = wide[pl.ds(x * slab_y + y, frames, stride=per_frame), :]
            layer_ref[y] = plane.astype(jnp.bfloat16)
        @pl.when(col_ref[0] == 0)
        def _():
            edge_ref[x] = layer_ref[slab_y - 1]

        @pl.when(col_ref[0] != 0)
        def _():
            edge_ref[x] = layer_ref[0]


def make_faces(window, col, bold):
    _, frames, slab_x, slab_y, slab_z = bold.shape
    layer = jax.ShapeDtypeStruct((slab_y, frames, slab_z), jnp.bfloat16)
    edge = jax.ShapeDtypeStruct((slab_x, frames, slab_z), jnp.bfloat16)
    whole = lambda array: pl.BlockSpec(array.shape, lambda _: (0,) * len(array.shape))
    return pl.pallas_call(
        faces_kernel,
        grid=(1,),
        in_specs=[
            pl.BlockSpec(memory_space=pltpu.SMEM),
            pl.BlockSpec((1, frames, slab_x, slab_y, slab_z), lambda _: (window, 0, 0, 0, 0)),
        ],
        out_specs=[whole(layer), whole(layer), whole(edge)],
        out_shape=[layer, layer, edge],
        scratch_shapes=[pltpu.VMEM((frames * slab_x * slab_y, slab_z), jnp.float32)],
        compiler_params=pltpu.CompilerParams(vmem_limit_bytes=VMEM_BYTES),
        cost_estimate=SMALL,
        name="faces",
    )(col, bold)


def three_taps(before, here, after):
    return SIDE * before + CENTRE * here + SIDE * after


def along_z(part):
    lane = lax.broadcasted_iota(jnp.int32, part.shape, 1)
    last = part.shape[1] - 1
    before = jnp.where(lane == 0, 0.0, pltpu.roll(part, 1, 1))
    after = jnp.where(lane == last, 0.0, pltpu.roll(part, last, 1))
    return three_taps(before, part, after)


def place_edge(planes, x, edge, col):
    planes[x, 0] = jnp.where(col == 0, 0.0, edge)
    planes[x, planes.shape[1] - 1] = jnp.where(col == 0, edge, 0.0)


def standardise(smooth):
    frames = smooth.shape[0]
    centred = smooth - jnp.mean(smooth, axis=0, keepdims=True)
    spread = jnp.mean(centred * centred, axis=0, keepdims=True)
    return (centred * lax.rsqrt((spread + 1e-05) * frames)).astype(jnp.bfloat16)


def pick(parts, gm_ref, out_ref):
    voxels = parts[0].shape[1]
    rows = gm_ref.shape[1]
    step = 2 * BLOCK
    for start in range(0, rows, step):
        wanted = gm_ref[:, start : start + step]
        voxel = lax.broadcasted_iota(jnp.int32, (voxels, step), 0)
        chosen = jnp.where(voxel == wanted, 1.0, 0.0).astype(jnp.bfloat16)
        total = jnp.dot(parts[0][...], chosen, preferred_element_type=jnp.float32)
        for part in parts[1:]:
            total += jnp.dot(part[...], chosen, preferred_element_type=jnp.float32)
        out_ref[:, start : start + step] = total.astype(out_ref.dtype)


def panel_kernel(
    place_ref, first_ref, last_ref, low_ref, high_ref, edge_ref, corner_ref, gm_ref, out_ref,
    planes, scored,
):
    slab_y, frames, slab_z = first_ref.shape
    slab_x = edge_ref.shape[0]
    for y in range(slab_y):
        layers = [ref[y].astype(jnp.float32) for ref in (low_ref, first_ref, last_ref, high_ref)]
        for x in range(slab_x):
            planes[x, y + 1] = three_taps(*layers[x : x + 3])
    edges = [corner_ref[0], edge_ref[0], edge_ref[1], corner_ref[1]]
    edges = [edge.astype(jnp.float32) for edge in edges]
    for x in range(slab_x):
        place_edge(planes, x, three_taps(*edges[x : x + 3]), place_ref[0])
    for x in range(slab_x):
        for y in range(slab_y):
            part = three_taps(planes[x, y], planes[x, y + 1], planes[x, y + 2])
            start = (x * slab_y + y) * slab_z
            scored[:, start : start + slab_z] = standardise(along_z(part))
    pick([scored], gm_ref, out_ref)


def inner_kernel(
    place_ref, first_ref, last_ref, edge_ref, gm_ref, out_ref, planes, high, middle, low
):
    slab_y, frames, slab_z = first_ref.shape
    slab_x = edge_ref.shape[0]

    def two_taps(here, other):
        return CENTRE * here.astype(jnp.float32) + SIDE * other.astype(jnp.float32)

    for y in range(slab_y):
        planes[0, y + 1] = two_taps(first_ref[y], last_ref[y])
        planes[1, y + 1] = two_taps(last_ref[y], first_ref[y])
    for x in range(slab_x):
        place_edge(planes, x, two_taps(edge_ref[x], edge_ref[1 - x]), place_ref[0])
    for x in range(slab_x):
        for y in range(slab_y):
            part = along_z(three_taps(planes[x, y], planes[x, y + 1], planes[x, y + 2]))
            start = (x * slab_y + y) * slab_z
            for term in (high, middle, low):
                rounded = part.astype(jnp.bfloat16)
                term[:, start : start + slab_z] = rounded
                part = part - rounded.astype(jnp.float32)
    pick([high, middle, low], gm_ref, out_ref)


def halo_kernel(
    place_ref, first_ref, last_ref, beyond_ref, edge_ref, corner_ref, gm_ref, out_ref,
    planes, scored,
):
    slab_y, frames, slab_z = first_ref.shape
    even = place_ref[1] == 0

    def sides(own, beyond):
        own, beyond = own.astype(jnp.float32), beyond.astype(jnp.float32)
        return jnp.where(even, own, beyond), jnp.where(even, beyond, own)

    for y in range(slab_y):
        own = jnp.where(even, last_ref[y], first_ref[y])
        planes[0, y + 1], planes[1, y + 1] = sides(own, beyond_ref[y])
    own = jnp.where(even, edge_ref[1], edge_ref[0])
    for x, edge in enumerate(sides(own, corner_ref[2])):
        place_edge(planes, x, edge, place_ref[0])
    for x in range(2):
        for y in range(slab_y):
            part = three_taps(planes[x, y], planes[x, y + 1], planes[x, y + 2])
            start = (x * slab_y + y) * slab_z
            scored[:, start : start + slab_z] = along_z(part).astype(jnp.bfloat16)
    pick([scored], gm_ref, out_ref)


def join_kernel(inner_ref, halo_ref, out_ref):
    for start in range(0, out_ref.shape[1], BLOCK):
        span = slice(start, start + BLOCK)
        smooth = inner_ref[:, span] + SIDE * halo_ref[:, span].astype(jnp.float32)
        out_ref[:, span] = standardise(smooth)


def call_on_rows(kernel, dtype, frames, place, operands, scratch, name):
    rows = operands[-1].shape[1]
    whole = lambda array: pl.BlockSpec(array.shape, lambda _: (0,) * array.ndim)
    scalars = [] if place is None else [place]
    return pl.pallas_call(
        kernel,
        grid=(1,),
        in_specs=[pl.BlockSpec(memory_space=pltpu.SMEM)] * len(scalars)
        + [whole(value) for value in operands],
        out_specs=pl.BlockSpec((frames, rows), lambda _: (0, 0)),
        out_shape=jax.ShapeDtypeStruct((frames, rows), dtype),
        scratch_shapes=scratch,
        compiler_params=pltpu.CompilerParams(vmem_limit_bytes=VMEM_BYTES),
        cost_estimate=SMALL,
        name=name,
    )(*scalars, *operands)


def blur_scratch(first, terms):
    slab_y, frames, slab_z = first.shape
    planes = pltpu.VMEM((2, slab_y + 2, frames, slab_z), jnp.float32)
    return [planes] + [pltpu.VMEM((frames, 2 * slab_y * slab_z), jnp.bfloat16)] * terms


def make_panel(place, first, last, low, high, edge, corner, gm):
    operands = (first, last, low, high, edge, corner, gm)
    scratch = blur_scratch(first, 1)
    return call_on_rows(
        panel_kernel, jnp.bfloat16, first.shape[1], place, operands, scratch, "blur_score_pick"
    )


def make_inner(place, first, last, edge, gm):
    operands = (first, last, edge, gm)
    scratch = blur_scratch(first, 3)
    return call_on_rows(
        inner_kernel, jnp.float32, first.shape[1], place, operands, scratch, "inner_blur"
    )


def make_halo(place, first, last, beyond, edge, corner, gm):
    operands = (first, last, beyond, edge, corner, gm)
    scratch = blur_scratch(first, 1)
    return call_on_rows(
        halo_kernel, jnp.bfloat16, first.shape[1], place, operands, scratch, "halo_blur"
    )


def join(inner, halo):
    return call_on_rows(
        join_kernel, jnp.bfloat16, inner.shape[0], None, (inner, halo), [], "join_score"
    )


def tiles_kernel(place_ref, present_ref, *refs, sources, window):
    parts = refs[:sources]
    out_ref, held, tiles, sems, out_sems = refs[-5:]
    blocks, slots = out_ref.shape[:2]

    loads = []
    first = 0
    for n, part in enumerate(parts):
        target = held.at[pl.ds(first, part.shape[0])]
        loads.append(pltpu.make_async_copy(part, target, sems.at[n]))
        loads[-1].start()
        first += part.shape[0]
    for load in loads:
        load.wait()

    def partner(index):
        place = place_ref[index]
        start = pl.multiple_of(lax.rem(place, blocks) * BLOCK, BLOCK)
        return held[lax.div(place, blocks), :, pl.ds(start, BLOCK)]

    stores = []
    for block in range(blocks):
        own = held[0, :, block * BLOCK : (block + 1) * BLOCK].T
        for slot in range(0, slots, 2):
            index = block * slots + slot
            pair = jnp.concatenate([partner(index), partner(index + 1)], axis=1)
            both = jnp.dot(own, pair, preferred_element_type=jnp.float32)
            for n in range(2):
                tile = both[:, n * BLOCK : (n + 1) * BLOCK]
                tile = jnp.where(present_ref[index + n] != 0, tile, 0.0)
                tiles[block, slot + n] = tile.astype(jnp.bfloat16)
        stores.append(
            pltpu.make_async_copy(tiles.at[block], out_ref.at[block, :, window], out_sems.at[block])
        )
        stores[-1].start()
    for store in stores:
        store.wait()


def make_tiles(window, windows, place, present, sources, earlier):
    frames, rows = sources[0].shape[1:]
    total = sum(source.shape[0] for source in sources)
    blocks = rows // BLOCK
    slots = place.shape[0] // blocks
    count = len(sources)
    anywhere = pl.BlockSpec(memory_space=pl.ANY)
    operands = list(sources) + ([] if earlier is None else [earlier])
    return pl.pallas_call(
        functools.partial(tiles_kernel, sources=count, window=window),
        grid_spec=pltpu.PrefetchScalarGridSpec(
            num_scalar_prefetch=2,
            grid=(1,),
            in_specs=[anywhere] * len(operands),
            out_specs=anywhere,
            scratch_shapes=[
                pltpu.VMEM((total, frames, rows), jnp.bfloat16),
                pltpu.VMEM((blocks, slots, BLOCK, BLOCK), jnp.bfloat16),
                pltpu.SemaphoreType.DMA((count,)),
                pltpu.SemaphoreType.DMA((blocks,)),
            ],
        ),
        out_shape=jax.ShapeDtypeStruct((blocks, slots, windows, BLOCK, BLOCK), jnp.bfloat16),
        input_output_aliases={} if earlier is None else {2 + count: 0},
        compiler_params=pltpu.CompilerParams(vmem_limit_bytes=TILES_VMEM_BYTES),
        cost_estimate=SMALL,
        name="tiles",
    )(place, present, *operands)


def after(value, *earlier):
    return lax.optimization_barrier((value,) + earlier)[0]


def on_device(bold, gm_index, partners):
    row_total = lax.axis_size("row")
    col_total = lax.axis_size("col")
    row = lax.axis_index("row")
    col = lax.axis_index("col")
    even = row % 2 == 0

    def other_col(value):
        return lax.ppermute(value, "col", [(0, 1), (1, 0)])

    one_up = [(i, i + 1) for i in range(row_total - 1)]
    one_down = [(i + 1, i) for i in range(row_total - 1)]
    ahead = [((i + 2 * (-1) ** i) % row_total, i) for i in range(row_total)]
    behind = [(i, source) for source, i in ahead]
    two_on = [(i, i + 2 * (-1) ** (i + 1)) for i in range(row_total)]
    two_on = [(i, target) for i, target in two_on if 0 <= target < row_total]
    in_pair = [(i, i ^ 1) for i in range(row_total)]

    gm = gm_index.reshape(1, -1)
    here = jnp.stack([col, row % 2]).astype(jnp.int32)

    blocks, slots = partners.shape
    ids = jnp.maximum(partners, 0)
    slab = ids // blocks
    hop = (slab // col_total - row + 2 + row_total) % row_total
    kind = jnp.where((hop == 1) == even, 4, 3)
    kind = jnp.where(hop == 2, 0, jnp.where((hop == 0) | (hop >= 4), 2 - (even == (hop >= 4)), kind))
    away = (slab % col_total != col).astype(jnp.int32)
    within = ids % blocks
    present = partners >= 0
    parts_0 = jnp.where(kind == 2, 6, jnp.where(kind == 4, 8, jnp.where(kind == 3, 2, kind)))
    parts_0 += away * jnp.where((kind == 2) | (kind == 4), 1, 3)
    parts_1 = jnp.where(kind < 2, kind + 2 * away, 2 * kind + away)
    place_0, place_1 = (
        jnp.where(present, part * blocks + within, 0).reshape(-1).astype(jnp.int32)
        for part in (parts_0, parts_1)
    )
    present = present.reshape(-1).astype(jnp.int32)

    def both(*parts):
        near = jnp.stack(parts, 0)
        return [near, other_col(near)]

    windows = bold.shape[0]
    gm_pair = lax.ppermute(gm, "row", in_pair)
    first_0, last_0, face_0 = make_faces(0, here, bold)
    low_0 = lax.ppermute(last_0, "row", one_up)
    high_0 = lax.ppermute(first_0, "row", one_down)
    edge_0 = other_col(face_0)
    first_1, last_1, face_1 = make_faces(1, here, after(bold, edge_0))
    beyond_1 = lax.ppermute(jnp.where(even, first_1, last_1), "row", two_on)
    edge_1 = other_col(face_1)
    inner_1 = make_inner(here, first_1, last_1, edge_1, after(gm, gm_pair))
    beyond_1 = after(beyond_1, inner_1)
    low_0, high_0 = after(low_0, inner_1), after(high_0, inner_1)
    ends = [jnp.where(col == 0, part[-1], part[0]) for part in (low_0, high_0, beyond_1)]
    corner = other_col(jnp.stack(ends, 0))
    halo_1 = make_halo(here, first_1, last_1, beyond_1, edge_1, corner, gm_pair)
    halo_1 = lax.ppermute(halo_1, "row", in_pair)
    own_0 = make_panel(here, first_0, last_0, low_0, high_0, edge_0, corner, gm)
    halo_1 = after(halo_1, own_0)
    ahead_0 = lax.ppermute(own_0, "row", ahead)
    own_1 = join(inner_1, halo_1)
    pair_0 = lax.ppermute(after(own_0, halo_1), "row", in_pair)
    ahead_0 = after(ahead_0, own_1)
    behind_0 = lax.ppermute(after(own_0, ahead_0), "row", behind)
    rest_0 = lax.ppermute(ahead_0, "row", in_pair)
    ahead_1 = lax.ppermute(own_1, "row", ahead)
    pair_1 = lax.ppermute(own_1, "row", in_pair)
    pair_0 = after(pair_0, ahead_0)
    ahead_1 = after(ahead_1, pair_0)
    behind_1 = lax.ppermute(after(own_1, ahead_1), "row", behind)
    rest_1 = lax.ppermute(ahead_1, "row", in_pair)
    behind_0, rest_0 = after(behind_0, ahead_1), after(rest_0, ahead_1)
    pair_1 = after(pair_1, rest_0, behind_0)
    behind_1 = after(behind_1, pair_1)
    sources = both(own_0, ahead_0, pair_0) + both(behind_0)
    out = make_tiles(0, windows, place_0, present, sources + both(rest_0), None)
    sources = both(own_1, ahead_1) + both(behind_1) + both(pair_1)
    rest_1 = after(rest_1, out, *sources)
    return make_tiles(1, windows, place_1, present, sources + both(rest_1), out)


def solution(mesh):
    in_specs = (P("subj", None, "row", "col", None), P(("row", "col")), P(("row", "col"), None))
    out_specs = P(("row", "col"), None, "subj", None, None)
    return jax.shard_map(
        on_device, mesh=mesh, in_specs=in_specs, out_specs=out_specs, check_vma=False
    )
```

```python
import functools
import math

import jax
import jax.numpy as jnp
from jax import lax
from jax.experimental import pallas as pl
from jax.experimental.pallas import tpu as pltpu
from jax.sharding import PartitionSpec as P

BLOCK = 128
SIDE = math.exp(-0.5) / (1.0 + 2.0 * math.exp(-0.5))
CENTRE = 1.0 / (1.0 + 2.0 * math.exp(-0.5))
SMALL = pl.CostEstimate(flops=1, bytes_accessed=1, transcendentals=0)
VMEM_BYTES = 20 * 1024 * 1024
TILES_VMEM_BYTES = 60 * 1024 * 1024


def faces_kernel(col_ref, bold_ref, first_ref, last_ref, edge_ref, wide):
    frames, slab_x, slab_y, slab_z = bold_ref.shape[1:]
    per_frame = slab_x * slab_y
    wide[...] = bold_ref[0].reshape(frames * per_frame, slab_z).astype(jnp.float32)
    for x, layer_ref in enumerate((first_ref, last_ref)):
        for y in range(slab_y):
            plane = wide[pl.ds(x * slab_y + y, frames, stride=per_frame), :]
            layer_ref[y] = plane.astype(jnp.bfloat16)
        @pl.when(col_ref[0] == 0)
        def _():
            edge_ref[x] = layer_ref[slab_y - 1]

        @pl.when(col_ref[0] != 0)
        def _():
            edge_ref[x] = layer_ref[0]


def make_faces(window, col, bold):
    _, frames, slab_x, slab_y, slab_z = bold.shape
    layer = jax.ShapeDtypeStruct((slab_y, frames, slab_z), jnp.bfloat16)
    edge = jax.ShapeDtypeStruct((slab_x, frames, slab_z), jnp.bfloat16)
    whole = lambda array: pl.BlockSpec(array.shape, lambda _: (0,) * len(array.shape))
    return pl.pallas_call(
        faces_kernel,
        grid=(1,),
        in_specs=[
            pl.BlockSpec(memory_space=pltpu.SMEM),
            pl.BlockSpec((1, frames, slab_x, slab_y, slab_z), lambda _: (window, 0, 0, 0, 0)),
        ],
        out_specs=[whole(layer), whole(layer), whole(edge)],
        out_shape=[layer, layer, edge],
        scratch_shapes=[pltpu.VMEM((frames * slab_x * slab_y, slab_z), jnp.float32)],
        compiler_params=pltpu.CompilerParams(vmem_limit_bytes=VMEM_BYTES),
        cost_estimate=SMALL,
        name="faces",
    )(col, bold)


def three_taps(before, here, after):
    return SIDE * before + CENTRE * here + SIDE * after


def along_z(part):
    lane = lax.broadcasted_iota(jnp.int32, part.shape, 1)
    last = part.shape[1] - 1
    before = jnp.where(lane == 0, 0.0, pltpu.roll(part, 1, 1))
    after = jnp.where(lane == last, 0.0, pltpu.roll(part, last, 1))
    return three_taps(before, part, after)


def place_edge(planes, x, edge, col):
    planes[x, 0] = jnp.where(col == 0, 0.0, edge)
    planes[x, planes.shape[1] - 1] = jnp.where(col == 0, edge, 0.0)


def standardise(smooth):
    frames = smooth.shape[0]
    centred = smooth - jnp.mean(smooth, axis=0, keepdims=True)
    spread = jnp.mean(centred * centred, axis=0, keepdims=True)
    return (centred * lax.rsqrt((spread + 1e-05) * frames)).astype(jnp.bfloat16)


def pick(parts, gm_ref, out_ref):
    voxels = parts[0].shape[1]
    rows = gm_ref.shape[1]
    step = 2 * BLOCK
    for start in range(0, rows, step):
        wanted = gm_ref[:, start : start + step]
        voxel = lax.broadcasted_iota(jnp.int32, (voxels, step), 0)
        chosen = jnp.where(voxel == wanted, 1.0, 0.0).astype(jnp.bfloat16)
        total = jnp.dot(parts[0][...], chosen, preferred_element_type=jnp.float32)
        for part in parts[1:]:
            total += jnp.dot(part[...], chosen, preferred_element_type=jnp.float32)
        out_ref[:, start : start + step] = total.astype(out_ref.dtype)


def panel_kernel(
    place_ref, first_ref, last_ref, low_ref, high_ref, edge_ref, corner_ref, gm_ref, out_ref,
    planes, scored,
):
    slab_y, frames, slab_z = first_ref.shape
    slab_x = edge_ref.shape[0]
    for y in range(slab_y):
        layers = [ref[y].astype(jnp.float32) for ref in (low_ref, first_ref, last_ref, high_ref)]
        for x in range(slab_x):
            planes[x, y + 1] = three_taps(*layers[x : x + 3])
    edges = [corner_ref[0], edge_ref[0], edge_ref[1], corner_ref[1]]
    edges = [edge.astype(jnp.float32) for edge in edges]
    for x in range(slab_x):
        place_edge(planes, x, three_taps(*edges[x : x + 3]), place_ref[0])
    for x in range(slab_x):
        for y in range(slab_y):
            part = three_taps(planes[x, y], planes[x, y + 1], planes[x, y + 2])
            start = (x * slab_y + y) * slab_z
            scored[:, start : start + slab_z] = standardise(along_z(part))
    pick([scored], gm_ref, out_ref)


def inner_kernel(
    place_ref, first_ref, last_ref, edge_ref, gm_ref, out_ref, planes, high, middle, low
):
    slab_y, frames, slab_z = first_ref.shape
    slab_x = edge_ref.shape[0]

    def two_taps(here, other):
        return CENTRE * here.astype(jnp.float32) + SIDE * other.astype(jnp.float32)

    for y in range(slab_y):
        planes[0, y + 1] = two_taps(first_ref[y], last_ref[y])
        planes[1, y + 1] = two_taps(last_ref[y], first_ref[y])
    for x in range(slab_x):
        place_edge(planes, x, two_taps(edge_ref[x], edge_ref[1 - x]), place_ref[0])
    for x in range(slab_x):
        for y in range(slab_y):
            part = along_z(three_taps(planes[x, y], planes[x, y + 1], planes[x, y + 2]))
            start = (x * slab_y + y) * slab_z
            for term in (high, middle, low):
                rounded = part.astype(jnp.bfloat16)
                term[:, start : start + slab_z] = rounded
                part = part - rounded.astype(jnp.float32)
    pick([high, middle, low], gm_ref, out_ref)


def halo_kernel(
    place_ref, first_ref, last_ref, beyond_ref, edge_ref, corner_ref, gm_ref, out_ref,
    planes, scored,
):
    slab_y, frames, slab_z = first_ref.shape
    even = place_ref[1] == 0

    def sides(own, beyond):
        own, beyond = own.astype(jnp.float32), beyond.astype(jnp.float32)
        return jnp.where(even, own, beyond), jnp.where(even, beyond, own)

    for y in range(slab_y):
        own = jnp.where(even, last_ref[y], first_ref[y])
        planes[0, y + 1], planes[1, y + 1] = sides(own, beyond_ref[y])
    own = jnp.where(even, edge_ref[1], edge_ref[0])
    for x, edge in enumerate(sides(own, corner_ref[2])):
        place_edge(planes, x, edge, place_ref[0])
    for x in range(2):
        for y in range(slab_y):
            part = three_taps(planes[x, y], planes[x, y + 1], planes[x, y + 2])
            start = (x * slab_y + y) * slab_z
            scored[:, start : start + slab_z] = along_z(part).astype(jnp.bfloat16)
    pick([scored], gm_ref, out_ref)


def join_kernel(inner_ref, halo_ref, out_ref):
    for start in range(0, out_ref.shape[1], BLOCK):
        span = slice(start, start + BLOCK)
        smooth = inner_ref[:, span] + SIDE * halo_ref[:, span].astype(jnp.float32)
        out_ref[:, span] = standardise(smooth)


def call_on_rows(kernel, dtype, frames, place, operands, scratch, name):
    rows = operands[-1].shape[1]
    whole = lambda array: pl.BlockSpec(array.shape, lambda _: (0,) * array.ndim)
    scalars = [] if place is None else [place]
    return pl.pallas_call(
        kernel,
        grid=(1,),
        in_specs=[pl.BlockSpec(memory_space=pltpu.SMEM)] * len(scalars)
        + [whole(value) for value in operands],
        out_specs=pl.BlockSpec((frames, rows), lambda _: (0, 0)),
        out_shape=jax.ShapeDtypeStruct((frames, rows), dtype),
        scratch_shapes=scratch,
        compiler_params=pltpu.CompilerParams(vmem_limit_bytes=VMEM_BYTES),
        cost_estimate=SMALL,
        name=name,
    )(*scalars, *operands)


def blur_scratch(first, terms):
    slab_y, frames, slab_z = first.shape
    planes = pltpu.VMEM((2, slab_y + 2, frames, slab_z), jnp.float32)
    return [planes] + [pltpu.VMEM((frames, 2 * slab_y * slab_z), jnp.bfloat16)] * terms


def make_panel(place, first, last, low, high, edge, corner, gm):
    operands = (first, last, low, high, edge, corner, gm)
    scratch = blur_scratch(first, 1)
    return call_on_rows(
        panel_kernel, jnp.bfloat16, first.shape[1], place, operands, scratch, "blur_score_pick"
    )


def make_inner(place, first, last, edge, gm):
    operands = (first, last, edge, gm)
    scratch = blur_scratch(first, 3)
    return call_on_rows(
        inner_kernel, jnp.float32, first.shape[1], place, operands, scratch, "inner_blur"
    )


def make_halo(place, first, last, beyond, edge, corner, gm):
    operands = (first, last, beyond, edge, corner, gm)
    scratch = blur_scratch(first, 1)
    return call_on_rows(
        halo_kernel, jnp.bfloat16, first.shape[1], place, operands, scratch, "halo_blur"
    )


def join(inner, halo):
    return call_on_rows(
        join_kernel, jnp.bfloat16, inner.shape[0], None, (inner, halo), [], "join_score"
    )


def tiles_kernel(place_ref, present_ref, *refs, sources, window):
    parts = refs[:sources]
    out_ref, held, tiles, sems, out_sems = refs[-5:]
    blocks, slots = out_ref.shape[:2]

    loads = []
    first = 0
    for n, part in enumerate(parts):
        target = held.at[pl.ds(first, part.shape[0])]
        first += part.shape[0]
        loads.append(pltpu.make_async_copy(part, target, sems.at[n]))
        loads[-1].start()
    for load in loads:
        load.wait()

    def partner(block, slot):
        place = place_ref[block, slot]
        start = pl.multiple_of(lax.rem(place, blocks) * BLOCK, BLOCK)
        return held[lax.div(place, blocks), :, pl.ds(start, BLOCK)]

    stores = []
    for block in range(blocks):
        own = held[0, :, block * BLOCK : (block + 1) * BLOCK].T
        for slot in range(0, slots, 2):
            pair = jnp.concatenate([partner(block, slot), partner(block, slot + 1)], axis=1)
            both = jnp.dot(own, pair, preferred_element_type=jnp.float32)
            for n in range(2):
                tile = both[:, n * BLOCK : (n + 1) * BLOCK]
                tile = jnp.where(present_ref[block, slot + n] != 0, tile, 0.0)
                tiles[block, slot + n] = tile.astype(jnp.bfloat16)
        stores.append(
            pltpu.make_async_copy(tiles.at[block], out_ref.at[block, :, window], out_sems.at[block])
        )
        stores[-1].start()
    for store in stores:
        store.wait()


def make_tiles(window, windows, place, present, sources, earlier):
    frames, rows = sources[0].shape[1:]
    total = sum(source.shape[0] for source in sources)
    blocks = rows // BLOCK
    slots = place.shape[1]
    count = len(sources)
    anywhere = pl.BlockSpec(memory_space=pl.ANY)
    operands = list(sources) + ([] if earlier is None else [earlier])
    return pl.pallas_call(
        functools.partial(tiles_kernel, sources=count, window=window),
        grid_spec=pltpu.PrefetchScalarGridSpec(
            num_scalar_prefetch=2,
            grid=(1,),
            in_specs=[anywhere] * len(operands),
            out_specs=anywhere,
            scratch_shapes=[
                pltpu.VMEM((total, frames, rows), jnp.bfloat16),
                pltpu.VMEM((blocks, slots, BLOCK, BLOCK), jnp.bfloat16),
                pltpu.SemaphoreType.DMA((count,)),
                pltpu.SemaphoreType.DMA((blocks,)),
            ],
        ),
        out_shape=jax.ShapeDtypeStruct((blocks, slots, windows, BLOCK, BLOCK), jnp.bfloat16),
        input_output_aliases={} if earlier is None else {2 + count: 0},
        compiler_params=pltpu.CompilerParams(vmem_limit_bytes=VMEM_BYTES if window else TILES_VMEM_BYTES),
        cost_estimate=SMALL,
        name="tiles",
    )(place, present, *operands)


def after(value, *earlier):
    return lax.optimization_barrier((value,) + earlier)[0]


def on_device(bold, gm_index, partners):
    row_total = lax.axis_size("row")
    col_total = lax.axis_size("col")
    row = lax.axis_index("row")
    col = lax.axis_index("col")
    even = row % 2 == 0

    def other_col(value):
        return lax.ppermute(value, "col", [(0, 1), (1, 0)])

    one_up = [(i, i + 1) for i in range(row_total - 1)]
    one_down = [(i + 1, i) for i in range(row_total - 1)]
    ahead = [((i + 2 * (-1) ** i) % row_total, i) for i in range(row_total)]
    behind = [(i, source) for source, i in ahead]
    two_on = [(i, i + 2 * (-1) ** (i + 1)) for i in range(row_total)]
    two_on = [(i, target) for i, target in two_on if 0 <= target < row_total]
    in_pair = [(i, i ^ 1) for i in range(row_total)]

    gm = gm_index.reshape(1, -1)
    here = jnp.stack([col, row % 2]).astype(jnp.int32)

    blocks, slots = partners.shape
    ids = jnp.maximum(partners, 0)
    slab = ids // blocks
    hop = (slab // col_total - row + 2 + row_total) % row_total
    kind = jnp.where((hop == 1) == even, 4, 3)
    kind = jnp.where(hop == 2, 0, jnp.where((hop == 0) | (hop >= 4), 2 - (even == (hop >= 4)), kind))
    away = (slab % col_total != col).astype(jnp.int32)
    within = ids % blocks
    present = partners >= 0
    parts_0 = jnp.where(kind == 4, 8 + away, kind // 2 * 4 + kind % 2 + 2 * away)
    parts_1 = jnp.where(kind == 3, 4 + away, jnp.where(kind < 2, kind, kind // 2 + 5) + 2 * away)
    place_0, place_1 = (
        jnp.where(present, part * blocks + within, 0).astype(jnp.int32)
        for part in (parts_0, parts_1)
    )
    present = present.astype(jnp.int32)

    def both(*parts):
        near = jnp.stack(parts, 0)
        return [near, other_col(near)]

    windows = bold.shape[0]
    gm_pair = lax.ppermute(gm, "row", in_pair)
    first_0, last_0, face_0 = make_faces(0, here, bold)
    low_0 = lax.ppermute(last_0, "row", one_up)
    high_0 = lax.ppermute(first_0, "row", one_down)
    edge_0 = other_col(face_0)
    first_1, last_1, face_1 = make_faces(1, here, after(bold, edge_0, gm_pair))
    beyond_1 = lax.ppermute(jnp.where(even, first_1, last_1), "row", two_on)
    edge_1 = other_col(face_1)
    inner_1 = make_inner(here, first_1, last_1, edge_1, gm)
    beyond_1 = after(beyond_1, inner_1)
    low_0, high_0 = after(low_0, inner_1), after(high_0, inner_1)
    ends = [jnp.where(col == 0, part[-1], part[0]) for part in (low_0, high_0, beyond_1)]
    corner = other_col(jnp.stack(ends, 0))
    halo_1 = make_halo(here, first_1, last_1, beyond_1, edge_1, corner, gm_pair)
    halo_1 = lax.ppermute(halo_1, "row", in_pair)
    own_0 = make_panel(here, first_0, last_0, low_0, high_0, edge_0, corner, gm)
    halo_1 = after(halo_1, own_0)
    ahead_0 = lax.ppermute(own_0, "row", ahead)
    own_1 = join(inner_1, halo_1)
    pair_0 = lax.ppermute(after(own_0, halo_1), "row", in_pair)
    ahead_0 = after(ahead_0, own_1)
    behind_0 = lax.ppermute(after(own_0, ahead_0), "row", behind)
    rest_0 = lax.ppermute(ahead_0, "row", in_pair)
    ahead_1 = lax.ppermute(own_1, "row", ahead)
    pair_1 = lax.ppermute(own_1, "row", in_pair)
    pair_0 = after(pair_0, ahead_0)
    ahead_1 = after(ahead_1, pair_0)
    behind_1 = lax.ppermute(after(own_1, ahead_1), "row", behind)
    rest_1 = lax.ppermute(ahead_1, "row", in_pair)
    behind_0, rest_0 = after(behind_0, ahead_1), after(rest_0, ahead_1)
    pair_1 = after(pair_1, rest_0, behind_0)
    sources = both(own_0, ahead_0) + both(behind_0, pair_0)
    out = make_tiles(0, windows, place_0, present, sources + both(rest_0), None)
    sources = both(own_1, ahead_1) + both(pair_1)
    behind_1, rest_1 = after(behind_1, out, *sources), after(rest_1, out, *sources)
    sources += both(behind_1, rest_1)
    return make_tiles(1, windows, place_1, present, sources, out)


def solution(mesh):
    in_specs = (P("subj", None, "row", "col", None), P(("row", "col")), P(("row", "col"), None))
    out_specs = P(("row", "col"), None, "subj", None, None)
    return jax.shard_map(
        on_device, mesh=mesh, in_specs=in_specs, out_specs=out_specs, check_vma=False
    )
```

```python
import functools
import math

import jax
import jax.numpy as jnp
from jax import lax
from jax.experimental import pallas as pl
from jax.experimental.pallas import tpu as pltpu
from jax.sharding import PartitionSpec as P

BLOCK = 128
SIDE = math.exp(-0.5) / (1.0 + 2.0 * math.exp(-0.5))
CENTRE = 1.0 / (1.0 + 2.0 * math.exp(-0.5))
SMALL = pl.CostEstimate(flops=1, bytes_accessed=1, transcendentals=0)
VMEM_BYTES = 20 * 1024 * 1024


def faces_kernel(col_ref, bold_ref, first_ref, last_ref, edge_ref, wide):
    frames, slab_x, slab_y, slab_z = bold_ref.shape[1:]
    per_frame = slab_x * slab_y
    wide[...] = bold_ref[0].reshape(frames * per_frame, slab_z).astype(jnp.float32)
    for x, layer_ref in enumerate((first_ref, last_ref)):
        for y in range(slab_y):
            plane = wide[pl.ds(x * slab_y + y, frames, stride=per_frame), :]
            layer_ref[y] = plane.astype(jnp.bfloat16)
        @pl.when(col_ref[0] == 0)
        def _():
            edge_ref[x] = layer_ref[slab_y - 1]

        @pl.when(col_ref[0] != 0)
        def _():
            edge_ref[x] = layer_ref[0]


def make_faces(window, col, bold):
    _, frames, slab_x, slab_y, slab_z = bold.shape
    layer = jax.ShapeDtypeStruct((slab_y, frames, slab_z), jnp.bfloat16)
    edge = jax.ShapeDtypeStruct((slab_x, frames, slab_z), jnp.bfloat16)
    whole = lambda array: pl.BlockSpec(array.shape, lambda _: (0,) * len(array.shape))
    return pl.pallas_call(
        faces_kernel,
        grid=(1,),
        in_specs=[
            pl.BlockSpec(memory_space=pltpu.SMEM),
            pl.BlockSpec((1, frames, slab_x, slab_y, slab_z), lambda _: (window, 0, 0, 0, 0)),
        ],
        out_specs=[whole(layer), whole(layer), whole(edge)],
        out_shape=[layer, layer, edge],
        scratch_shapes=[pltpu.VMEM((frames * slab_x * slab_y, slab_z), jnp.float32)],
        compiler_params=pltpu.CompilerParams(vmem_limit_bytes=VMEM_BYTES),
        cost_estimate=SMALL,
        name="faces",
    )(col, bold)


def three_taps(before, here, after):
    return SIDE * before + CENTRE * here + SIDE * after


def along_z(part):
    lane = lax.broadcasted_iota(jnp.int32, part.shape, 1)
    last = part.shape[1] - 1
    before = jnp.where(lane == 0, 0.0, pltpu.roll(part, 1, 1))
    after = jnp.where(lane == last, 0.0, pltpu.roll(part, last, 1))
    return three_taps(before, part, after)


def place_edge(planes, x, edge, col):
    planes[x, 0] = jnp.where(col == 0, 0.0, edge)
    planes[x, planes.shape[1] - 1] = jnp.where(col == 0, edge, 0.0)


def standardise(smooth):
    frames = smooth.shape[0]
    centred = smooth - jnp.mean(smooth, axis=0, keepdims=True)
    spread = jnp.mean(centred * centred, axis=0, keepdims=True)
    return (centred * lax.rsqrt((spread + 1e-05) * frames)).astype(jnp.bfloat16)


def pick(parts, gm_ref, out_ref):
    voxels = parts[0].shape[1]
    rows = gm_ref.shape[1]
    step = 2 * BLOCK
    for start in range(0, rows, step):
        wanted = gm_ref[:, start : start + step]
        voxel = lax.broadcasted_iota(jnp.int32, (voxels, step), 0)
        chosen = jnp.where(voxel == wanted, 1.0, 0.0).astype(jnp.bfloat16)
        total = jnp.dot(parts[0][...], chosen, preferred_element_type=jnp.float32)
        for part in parts[1:]:
            total += jnp.dot(part[...], chosen, preferred_element_type=jnp.float32)
        out_ref[:, start : start + step] = total.astype(out_ref.dtype)


def inner_kernel(
    place_ref, first_ref, last_ref, edge_ref, gm_ref, out_ref, planes, high, middle, low
):
    slab_y, frames, slab_z = first_ref.shape
    slab_x = edge_ref.shape[0]

    def two_taps(here, other):
        return CENTRE * here.astype(jnp.float32) + SIDE * other.astype(jnp.float32)

    for y in range(slab_y):
        planes[0, y + 1] = two_taps(first_ref[y], last_ref[y])
        planes[1, y + 1] = two_taps(last_ref[y], first_ref[y])
    for x in range(slab_x):
        place_edge(planes, x, two_taps(edge_ref[x], edge_ref[1 - x]), place_ref[0])
    for x in range(slab_x):
        for y in range(slab_y):
            part = along_z(three_taps(planes[x, y], planes[x, y + 1], planes[x, y + 2]))
            start = (x * slab_y + y) * slab_z
            for term in (high, middle, low):
                rounded = part.astype(jnp.bfloat16)
                term[:, start : start + slab_z] = rounded
                part = part - rounded.astype(jnp.float32)
    pick([high, middle, low], gm_ref, out_ref)


def halo_kernel(
    place_ref, first_ref, last_ref, beyond_ref, edge_ref, corner_ref, gm_ref, out_ref,
    planes, scored,
):
    slab_y, frames, slab_z = first_ref.shape
    even = place_ref[1] == 0

    def sides(own, beyond):
        own, beyond = own.astype(jnp.float32), beyond.astype(jnp.float32)
        return jnp.where(even, own, beyond), jnp.where(even, beyond, own)

    for y in range(slab_y):
        own = jnp.where(even, last_ref[y], first_ref[y])
        planes[0, y + 1], planes[1, y + 1] = sides(own, beyond_ref[y])
    own = jnp.where(even, edge_ref[1], edge_ref[0])
    for x, edge in enumerate(sides(own, corner_ref[...])):
        place_edge(planes, x, edge, place_ref[0])
    for x in range(2):
        for y in range(slab_y):
            part = three_taps(planes[x, y], planes[x, y + 1], planes[x, y + 2])
            start = (x * slab_y + y) * slab_z
            scored[:, start : start + slab_z] = along_z(part).astype(jnp.bfloat16)
    pick([scored], gm_ref, out_ref)


def join_kernel(inner_ref, halo_ref, out_ref):
    for start in range(0, out_ref.shape[1], BLOCK):
        span = slice(start, start + BLOCK)
        smooth = inner_ref[:, span] + SIDE * halo_ref[:, span].astype(jnp.float32)
        out_ref[:, span] = standardise(smooth)


def call_on_rows(kernel, dtype, frames, place, operands, scratch, name):
    rows = operands[-1].shape[1]
    whole = lambda array: pl.BlockSpec(array.shape, lambda _: (0,) * array.ndim)
    scalars = [] if place is None else [place]
    return pl.pallas_call(
        kernel,
        grid=(1,),
        in_specs=[pl.BlockSpec(memory_space=pltpu.SMEM)] * len(scalars)
        + [whole(value) for value in operands],
        out_specs=pl.BlockSpec((frames, rows), lambda _: (0, 0)),
        out_shape=jax.ShapeDtypeStruct((frames, rows), dtype),
        scratch_shapes=scratch,
        compiler_params=pltpu.CompilerParams(vmem_limit_bytes=VMEM_BYTES),
        cost_estimate=SMALL,
        name=name,
    )(*scalars, *operands)


def blur_scratch(first, terms):
    slab_y, frames, slab_z = first.shape
    planes = pltpu.VMEM((2, slab_y + 2, frames, slab_z), jnp.float32)
    return [planes] + [pltpu.VMEM((frames, 2 * slab_y * slab_z), jnp.bfloat16)] * terms


def make_inner(place, first, last, edge, gm):
    operands = (first, last, edge, gm)
    scratch = blur_scratch(first, 3)
    return call_on_rows(
        inner_kernel, jnp.float32, first.shape[1], place, operands, scratch, "inner_blur"
    )


def make_halo(place, first, last, beyond, edge, corner, gm):
    operands = (first, last, beyond, edge, corner, gm)
    scratch = blur_scratch(first, 1)
    return call_on_rows(
        halo_kernel, jnp.bfloat16, first.shape[1], place, operands, scratch, "halo_blur"
    )


def join(inner, halo):
    return call_on_rows(
        join_kernel, jnp.bfloat16, inner.shape[0], None, (inner, halo), [], "join_score"
    )


def tiles_kernel(place_ref, present_ref, *refs, sources, window):
    parts = refs[:sources]
    out_ref, held, tiles, sems, out_sems = refs[-5:]
    blocks, slots = out_ref.shape[:2]

    loads = []
    first = 0
    for n, part in enumerate(parts):
        target = held.at[pl.ds(first, part.shape[0])]
        first += part.shape[0]
        loads.append(pltpu.make_async_copy(part, target, sems.at[n]))
        loads[-1].start()
    for load in loads:
        load.wait()

    def partner(block, slot):
        place = place_ref[block, slot]
        start = pl.multiple_of(lax.rem(place, blocks) * BLOCK, BLOCK)
        return held[lax.div(place, blocks), :, pl.ds(start, BLOCK)]

    stores = []
    for block in range(blocks):
        own = held[0, :, block * BLOCK : (block + 1) * BLOCK].T
        for slot in range(0, slots, 2):
            pair = jnp.concatenate([partner(block, slot), partner(block, slot + 1)], axis=1)
            both = jnp.dot(own, pair, preferred_element_type=jnp.float32)
            for n in range(2):
                tile = both[:, n * BLOCK : (n + 1) * BLOCK]
                tile = jnp.where(present_ref[block, slot + n] != 0, tile, 0.0)
                tiles[block, slot + n] = tile.astype(jnp.bfloat16)
        stores.append(
            pltpu.make_async_copy(tiles.at[block], out_ref.at[block, :, window], out_sems.at[block])
        )
        stores[-1].start()
    for store in stores:
        store.wait()


def make_tiles(window, windows, place, present, sources, earlier):
    frames, rows = sources[0].shape[1:]
    total = sum(source.shape[0] for source in sources)
    blocks = rows // BLOCK
    slots = place.shape[1]
    count = len(sources)
    anywhere = pl.BlockSpec(memory_space=pl.ANY)
    operands = list(sources) + ([] if earlier is None else [earlier])
    return pl.pallas_call(
        functools.partial(tiles_kernel, sources=count, window=window),
        grid_spec=pltpu.PrefetchScalarGridSpec(
            num_scalar_prefetch=2,
            grid=(1,),
            in_specs=[anywhere] * len(operands),
            out_specs=anywhere,
            scratch_shapes=[
                pltpu.VMEM((total, frames, rows), jnp.bfloat16),
                pltpu.VMEM((blocks, slots, BLOCK, BLOCK), jnp.bfloat16),
                pltpu.SemaphoreType.DMA((count,)),
                pltpu.SemaphoreType.DMA((blocks,)),
            ],
        ),
        out_shape=jax.ShapeDtypeStruct((blocks, slots, windows, BLOCK, BLOCK), jnp.bfloat16),
        input_output_aliases={} if earlier is None else {2 + count: 0},
        compiler_params=pltpu.CompilerParams(vmem_limit_bytes=VMEM_BYTES),
        cost_estimate=SMALL,
        name="tiles",
    )(place, present, *operands)


def after(value, *earlier):
    return lax.optimization_barrier((value,) + earlier)[0]


def on_device(bold, gm_index, partners):
    row_total = lax.axis_size("row")
    col_total = lax.axis_size("col")
    row = lax.axis_index("row")
    col = lax.axis_index("col")
    even = row % 2 == 0

    def other_col(value):
        return lax.ppermute(value, "col", [(0, 1), (1, 0)])

    ahead = [((i + 2 * (-1) ** i) % row_total, i) for i in range(row_total)]
    behind = [(i, source) for source, i in ahead]
    two_on = [(i, i + 2 * (-1) ** (i + 1)) for i in range(row_total)]
    two_on = [(i, target) for i, target in two_on if 0 <= target < row_total]
    in_pair = [(i, i ^ 1) for i in range(row_total)]

    gm = gm_index.reshape(1, -1)
    here = jnp.stack([col, row % 2]).astype(jnp.int32)

    blocks, slots = partners.shape
    ids = jnp.maximum(partners, 0)
    slab = ids // blocks
    hop = (slab // col_total - row + 2 + row_total) % row_total
    kind = jnp.where((hop == 1) == even, 4, 3)
    kind = jnp.where(hop == 2, 0, jnp.where((hop == 0) | (hop >= 4), 2 - (even == (hop >= 4)), kind))
    away = (slab % col_total != col).astype(jnp.int32)
    within = ids % blocks
    present = partners >= 0
    parts_0 = jnp.where(kind == 4, 8 + away, kind // 2 * 4 + kind % 2 + 2 * away)
    parts_1 = jnp.where(kind == 3, 4 + away, jnp.where(kind < 2, kind, kind // 2 + 5) + 2 * away)
    place_0, place_1 = (
        jnp.where(present, part * blocks + within, 0).astype(jnp.int32)
        for part in (parts_0, parts_1)
    )
    present = present.astype(jnp.int32)

    def both(*parts):
        near = jnp.stack(parts, 0)
        return [near, other_col(near)]

    windows = bold.shape[0]
    gm_pair = lax.ppermute(gm, "row", in_pair)

    def outer(first, last):
        return lax.ppermute(jnp.where(even, first, last), "row", two_on)

    def halo_for_pair(first, last, beyond, edge):
        corner = other_col(jnp.where(col == 0, beyond[-1], beyond[0]))
        return make_halo(here, first, last, beyond, edge, corner, gm_pair)

    first_0, last_0, face_0 = make_faces(0, here, bold)
    beyond_0 = outer(first_0, last_0)
    edge_0 = other_col(face_0)
    first_1, last_1, face_1 = make_faces(1, here, after(bold, edge_0, gm_pair))
    beyond_1 = outer(first_1, last_1)
    edge_1 = other_col(face_1)
    inner_0 = make_inner(here, first_0, last_0, edge_0, after(gm, edge_1))
    beyond_0 = after(beyond_0, inner_0)
    given_0 = halo_for_pair(first_0, last_0, beyond_0, edge_0)
    halo_0 = lax.ppermute(given_0, "row", in_pair)
    inner_1 = make_inner(here, first_1, last_1, edge_1, after(gm, given_0))
    beyond_1 = after(beyond_1, inner_1)
    given_1 = halo_for_pair(first_1, last_1, beyond_1, edge_1)
    halo_1 = lax.ppermute(given_1, "row", in_pair)
    own_0 = join(inner_0, after(halo_0, given_1))
    halo_1 = after(halo_1, own_0)
    ahead_0 = lax.ppermute(own_0, "row", ahead)
    own_1 = join(inner_1, halo_1)
    pair_0 = lax.ppermute(after(own_0, halo_1), "row", in_pair)
    ahead_0 = after(ahead_0, own_1)
    behind_0 = lax.ppermute(after(own_0, ahead_0), "row", behind)
    rest_0 = lax.ppermute(ahead_0, "row", in_pair)
    ahead_1 = lax.ppermute(own_1, "row", ahead)
    pair_1 = lax.ppermute(own_1, "row", in_pair)
    pair_0 = after(pair_0, ahead_0)
    ahead_1 = after(ahead_1, pair_0)
    behind_1 = lax.ppermute(after(own_1, ahead_1), "row", behind)
    rest_1 = lax.ppermute(ahead_1, "row", in_pair)
    behind_0, rest_0 = after(behind_0, ahead_1), after(rest_0, ahead_1)
    pair_1 = after(pair_1, rest_0, behind_0)
    sources_0 = both(own_0, ahead_0) + both(behind_0, pair_0) + both(rest_0)
    sources_1 = both(own_1, ahead_1) + both(pair_1)
    sources_1 += both(behind_1, rest_1)
    out = make_tiles(0, windows, place_0, present, sources_0, None)
    return make_tiles(1, windows, place_1, present, sources_1, out)


def solution(mesh):
    in_specs = (P("subj", None, "row", "col", None), P(("row", "col")), P(("row", "col"), None))
    out_specs = P(("row", "col"), None, "subj", None, None)
    return jax.shard_map(
        on_device, mesh=mesh, in_specs=in_specs, out_specs=out_specs, check_vma=False
    )
```

```python
import functools
import math

import jax
import jax.numpy as jnp
from jax import lax
from jax.experimental import pallas as pl
from jax.experimental.pallas import tpu as pltpu
from jax.sharding import PartitionSpec as P

BLOCK = 128
SIDE = math.exp(-0.5) / (1.0 + 2.0 * math.exp(-0.5))
CENTRE = 1.0 / (1.0 + 2.0 * math.exp(-0.5))
SMALL = pl.CostEstimate(flops=1, bytes_accessed=1, transcendentals=0)
VMEM_BYTES = 20 * 1024 * 1024


def faces_kernel(place_ref, bold_ref, *refs):
    windows, frames, slab_x, slab_y, slab_z = bold_ref.shape
    per_frame = slab_x * slab_y
    wide = refs[-1]
    for window in range(windows):
        near_ref, outer_ref, edge_ref = refs[3 * window : 3 * window + 3]
        wide[...] = bold_ref[window].reshape(frames * per_frame, slab_z).astype(jnp.float32)

        def plane(x, y):
            taken = wide[pl.ds(x * slab_y + y, frames, stride=per_frame), :]
            return taken.astype(jnp.bfloat16)

        def layers(first_ref, last_ref):
            for y in range(slab_y):
                first_ref[y] = plane(0, y)
                last_ref[y] = plane(1, y)

        pl.when(place_ref[1] == 0)(functools.partial(layers, outer_ref, near_ref))
        pl.when(place_ref[1] != 0)(functools.partial(layers, near_ref, outer_ref))

        def edges(y):
            for x in range(slab_x):
                edge_ref[x] = plane(x, y)

        pl.when(place_ref[0] == 0)(functools.partial(edges, slab_y - 1))
        pl.when(place_ref[0] != 0)(functools.partial(edges, 0))


def make_faces(place, bold):
    windows, frames, slab_x, slab_y, slab_z = bold.shape
    layer = jax.ShapeDtypeStruct((slab_y, frames, slab_z), jnp.bfloat16)
    edge = jax.ShapeDtypeStruct((slab_x, frames, slab_z), jnp.bfloat16)
    whole = lambda array: pl.BlockSpec(array.shape, lambda _: (0,) * len(array.shape))
    return pl.pallas_call(
        faces_kernel,
        grid=(1,),
        in_specs=[pl.BlockSpec(memory_space=pltpu.SMEM), whole(bold)],
        out_specs=[whole(layer), whole(layer), whole(edge)] * windows,
        out_shape=[layer, layer, edge] * windows,
        scratch_shapes=[pltpu.VMEM((frames * slab_x * slab_y, slab_z), jnp.float32)],
        compiler_params=pltpu.CompilerParams(vmem_limit_bytes=VMEM_BYTES),
        cost_estimate=SMALL,
        name="faces",
    )(place, bold)


def three_taps(before, here, after):
    return SIDE * before + CENTRE * here + SIDE * after


def along_z(part):
    lane = lax.broadcasted_iota(jnp.int32, part.shape, 1)
    last = part.shape[1] - 1
    before = jnp.where(lane == 0, 0.0, pltpu.roll(part, 1, 1))
    after = jnp.where(lane == last, 0.0, pltpu.roll(part, last, 1))
    return three_taps(before, part, after)


def place_edge(planes, x, edge, col):
    planes[x, 0] = jnp.where(col == 0, 0.0, edge)
    planes[x, planes.shape[1] - 1] = jnp.where(col == 0, edge, 0.0)


def standardise(smooth):
    frames = smooth.shape[0]
    centred = smooth - jnp.mean(smooth, axis=0, keepdims=True)
    spread = jnp.mean(centred * centred, axis=0, keepdims=True)
    return (centred * lax.rsqrt((spread + 1e-05) * frames)).astype(jnp.bfloat16)


def pick(parts, gm_ref, out_ref):
    voxels = parts[0].shape[1]
    rows = gm_ref.shape[1]
    step = 2 * BLOCK
    for start in range(0, rows, step):
        wanted = gm_ref[:, start : start + step]
        voxel = lax.broadcasted_iota(jnp.int32, (voxels, step), 0)
        chosen = jnp.where(voxel == wanted, 1.0, 0.0).astype(jnp.bfloat16)
        total = jnp.dot(parts[0][...], chosen, preferred_element_type=jnp.float32)
        for part in parts[1:]:
            total += jnp.dot(part[...], chosen, preferred_element_type=jnp.float32)
        out_ref[:, start : start + step] = total.astype(out_ref.dtype)


def inner_kernel(
    place_ref, near_ref, outer_ref, edge_ref, gm_ref, out_ref, planes, high, middle, low
):
    slab_y, frames, slab_z = near_ref.shape
    slab_x = edge_ref.shape[0]
    even = place_ref[1] == 0

    def two_taps(here, other):
        return CENTRE * here + SIDE * other

    for y in range(slab_y):
        near, outer = near_ref[y].astype(jnp.float32), outer_ref[y].astype(jnp.float32)
        first, last = jnp.where(even, outer, near), jnp.where(even, near, outer)
        planes[0, y + 1] = two_taps(first, last)
        planes[1, y + 1] = two_taps(last, first)
    edges = [edge_ref[x].astype(jnp.float32) for x in range(slab_x)]
    for x in range(slab_x):
        place_edge(planes, x, two_taps(edges[x], edges[1 - x]), place_ref[0])
    for x in range(slab_x):
        for y in range(slab_y):
            part = along_z(three_taps(planes[x, y], planes[x, y + 1], planes[x, y + 2]))
            start = (x * slab_y + y) * slab_z
            for term in (high, middle, low):
                rounded = part.astype(jnp.bfloat16)
                term[:, start : start + slab_z] = rounded
                part = part - rounded.astype(jnp.float32)
    pick([high, middle, low], gm_ref, out_ref)


def halo_kernel(
    place_ref, near_ref, beyond_ref, edge_ref, corner_ref, gm_ref, out_ref, planes, scored
):
    slab_y, frames, slab_z = near_ref.shape
    even = place_ref[1] == 0

    def sides(own, beyond):
        own, beyond = own.astype(jnp.float32), beyond.astype(jnp.float32)
        return jnp.where(even, own, beyond), jnp.where(even, beyond, own)

    for y in range(slab_y):
        planes[0, y + 1], planes[1, y + 1] = sides(near_ref[y], beyond_ref[y])
    own = jnp.where(even, edge_ref[1], edge_ref[0])
    for x, edge in enumerate(sides(own, corner_ref[...])):
        place_edge(planes, x, edge, place_ref[0])
    for x in range(2):
        for y in range(slab_y):
            part = three_taps(planes[x, y], planes[x, y + 1], planes[x, y + 2])
            start = (x * slab_y + y) * slab_z
            scored[:, start : start + slab_z] = along_z(part).astype(jnp.bfloat16)
    pick([scored], gm_ref, out_ref)


def join_kernel(inner_ref, halo_ref, out_ref):
    for start in range(0, out_ref.shape[1], BLOCK):
        span = slice(start, start + BLOCK)
        smooth = inner_ref[:, span] + SIDE * halo_ref[:, span].astype(jnp.float32)
        out_ref[:, span] = standardise(smooth)


def call_on_rows(kernel, dtype, frames, place, operands, scratch, name):
    rows = operands[-1].shape[1]
    whole = lambda array: pl.BlockSpec(array.shape, lambda _: (0,) * array.ndim)
    scalars = [] if place is None else [place]
    return pl.pallas_call(
        kernel,
        grid=(1,),
        in_specs=[pl.BlockSpec(memory_space=pltpu.SMEM)] * len(scalars)
        + [whole(value) for value in operands],
        out_specs=pl.BlockSpec((frames, rows), lambda _: (0, 0)),
        out_shape=jax.ShapeDtypeStruct((frames, rows), dtype),
        scratch_shapes=scratch,
        compiler_params=pltpu.CompilerParams(vmem_limit_bytes=VMEM_BYTES),
        cost_estimate=SMALL,
        name=name,
    )(*scalars, *operands)


def blur_scratch(first, terms):
    slab_y, frames, slab_z = first.shape
    planes = pltpu.VMEM((2, slab_y + 2, frames, slab_z), jnp.float32)
    return [planes] + [pltpu.VMEM((frames, 2 * slab_y * slab_z), jnp.bfloat16)] * terms


def make_inner(place, near, outer, edge, gm):
    operands = (near, outer, edge, gm)
    scratch = blur_scratch(near, 3)
    return call_on_rows(
        inner_kernel, jnp.float32, near.shape[1], place, operands, scratch, "inner_blur"
    )


def make_halo(place, near, beyond, edge, corner, gm):
    operands = (near, beyond, edge, corner, gm)
    scratch = blur_scratch(near, 1)
    return call_on_rows(
        halo_kernel, jnp.bfloat16, near.shape[1], place, operands, scratch, "halo_blur"
    )


def join(inner, halo):
    return call_on_rows(
        join_kernel, jnp.bfloat16, inner.shape[0], None, (inner, halo), [], "join_score"
    )


def tiles_kernel(place_ref, present_ref, *refs, sources, window):
    parts = refs[:sources]
    out_ref, held, tiles, sems, out_sems = refs[-5:]
    blocks, slots = out_ref.shape[:2]

    loads = []
    first = 0
    for n, part in enumerate(parts):
        target = held.at[pl.ds(first, part.shape[0])]
        first += part.shape[0]
        loads.append(pltpu.make_async_copy(part, target, sems.at[n]))
        loads[-1].start()
    for load in loads:
        load.wait()

    def partner(block, slot):
        place = place_ref[block, slot]
        start = pl.multiple_of(lax.rem(place, blocks) * BLOCK, BLOCK)
        return held[lax.div(place, blocks), :, pl.ds(start, BLOCK)]

    stores = []
    for block in range(blocks):
        own = held[0, :, block * BLOCK : (block + 1) * BLOCK].T
        for slot in range(0, slots, 2):
            pair = jnp.concatenate([partner(block, slot), partner(block, slot + 1)], axis=1)
            both = jnp.dot(own, pair, preferred_element_type=jnp.float32)
            for n in range(2):
                tile = both[:, n * BLOCK : (n + 1) * BLOCK]
                tile = jnp.where(present_ref[block, slot + n] != 0, tile, 0.0)
                tiles[block, slot + n] = tile.astype(jnp.bfloat16)
        stores.append(
            pltpu.make_async_copy(tiles.at[block], out_ref.at[block, :, window], out_sems.at[block])
        )
        stores[-1].start()
    for store in stores:
        store.wait()


def make_tiles(window, windows, place, present, sources, earlier):
    frames, rows = sources[0].shape[1:]
    total = sum(source.shape[0] for source in sources)
    blocks = rows // BLOCK
    slots = place.shape[1]
    count = len(sources)
    anywhere = pl.BlockSpec(memory_space=pl.ANY)
    operands = list(sources) + ([] if earlier is None else [earlier])
    return pl.pallas_call(
        functools.partial(tiles_kernel, sources=count, window=window),
        grid_spec=pltpu.PrefetchScalarGridSpec(
            num_scalar_prefetch=2,
            grid=(1,),
            in_specs=[anywhere] * len(operands),
            out_specs=anywhere,
            scratch_shapes=[
                pltpu.VMEM((total, frames, rows), jnp.bfloat16),
                pltpu.VMEM((blocks, slots, BLOCK, BLOCK), jnp.bfloat16),
                pltpu.SemaphoreType.DMA((count,)),
                pltpu.SemaphoreType.DMA((blocks,)),
            ],
        ),
        out_shape=jax.ShapeDtypeStruct((blocks, slots, windows, BLOCK, BLOCK), jnp.bfloat16),
        input_output_aliases={} if earlier is None else {2 + count: 0},
        compiler_params=pltpu.CompilerParams(vmem_limit_bytes=VMEM_BYTES),
        cost_estimate=SMALL,
        name="tiles",
    )(place, present, *operands)


def after(value, *earlier):
    return lax.optimization_barrier((value,) + earlier)[0]


def on_device(bold, gm_index, partners):
    row_total = lax.axis_size("row")
    col_total = lax.axis_size("col")
    row = lax.axis_index("row")
    col = lax.axis_index("col")
    even = row % 2 == 0

    def other_col(value):
        return lax.ppermute(value, "col", [(0, 1), (1, 0)])

    ahead = [((i + 2 * (-1) ** i) % row_total, i) for i in range(row_total)]
    behind = [(i, source) for source, i in ahead]
    two_on = [(i, i + 2 * (-1) ** (i + 1)) for i in range(row_total)]
    two_on = [(i, target) for i, target in two_on if 0 <= target < row_total]
    in_pair = [(i, i ^ 1) for i in range(row_total)]

    gm = gm_index.reshape(1, -1)
    here = jnp.stack([col, row % 2]).astype(jnp.int32)

    blocks, slots = partners.shape
    ids = jnp.maximum(partners, 0)
    slab = ids // blocks
    hop = (slab // col_total - row + 2 + row_total) % row_total
    kind = jnp.where((hop == 1) == even, 4, 3)
    kind = jnp.where(hop == 2, 0, jnp.where((hop == 0) | (hop >= 4), 2 - (even == (hop >= 4)), kind))
    away = (slab % col_total != col).astype(jnp.int32)
    within = ids % blocks
    present = partners >= 0
    part = jnp.where(kind == 4, 8 + away, kind // 2 * 4 + kind % 2 + 2 * away)
    place = jnp.where(present, part * blocks + within, 0).astype(jnp.int32)
    present = present.astype(jnp.int32)

    def both(*parts):
        near = jnp.stack(parts, 0)
        return [near, other_col(near)]

    windows = bold.shape[0]
    gm_pair = lax.ppermute(gm, "row", in_pair)

    def give_halo(near, beyond, edge):
        corner = other_col(jnp.where(col == 0, beyond[-1], beyond[0]))
        return make_halo(here, near, beyond, edge, corner, gm_pair)

    near_0, outer_0, face_0, near_1, outer_1, face_1 = make_faces(after(here, gm_pair), bold)
    beyond_0 = lax.ppermute(outer_0, "row", two_on)
    edge_0, edge_1 = other_col(face_0), other_col(face_1)
    inner_0 = make_inner(here, near_0, outer_0, edge_0, after(gm, edge_1))
    beyond_0 = after(beyond_0, inner_0)
    beyond_1 = lax.ppermute(after(outer_1, beyond_0), "row", two_on)
    given_0 = give_halo(near_0, beyond_0, edge_0)
    halo_0 = lax.ppermute(given_0, "row", in_pair)
    inner_1 = make_inner(here, near_1, outer_1, edge_1, after(gm, given_0))
    given_1 = give_halo(near_1, after(beyond_1, inner_1), edge_1)
    halo_1 = lax.ppermute(given_1, "row", in_pair)
    own_0 = join(inner_0, after(halo_0, given_1))
    ahead_0 = lax.ppermute(own_0, "row", ahead)
    behind_0 = lax.ppermute(own_0, "row", behind)
    halo_1 = after(halo_1, own_0)
    own_1 = join(inner_1, halo_1)
    pair_0 = lax.ppermute(after(own_0, halo_1), "row", in_pair)
    pair_1 = lax.ppermute(own_1, "row", in_pair)
    ahead_1 = lax.ppermute(own_1, "row", ahead)
    behind_1 = lax.ppermute(own_1, "row", behind)
    ahead_0, behind_0 = after(ahead_0, own_1), after(behind_0, own_1)
    rest_0 = lax.ppermute(ahead_0, "row", in_pair)
    pair_0, pair_1 = after(pair_0, ahead_0, behind_0), after(pair_1, ahead_0, behind_0)
    ahead_1 = after(ahead_1, pair_0, pair_1)
    behind_1 = after(behind_1, ahead_1)
    rest_1 = lax.ppermute(ahead_1, "row", in_pair)
    rest_0 = after(rest_0, ahead_1, behind_1)
    sources_0 = both(own_0, ahead_0) + both(behind_0, pair_0) + both(rest_0)
    out = make_tiles(0, windows, place, present, sources_0, None)
    rest_1 = after(rest_1, out)
    sources_1 = both(own_1, ahead_1) + both(behind_1, pair_1) + both(rest_1)
    return make_tiles(1, windows, place, present, sources_1, out)


def solution(mesh):
    in_specs = (P("subj", None, "row", "col", None), P(("row", "col")), P(("row", "col"), None))
    out_specs = P(("row", "col"), None, "subj", None, None)
    return jax.shard_map(
        on_device, mesh=mesh, in_specs=in_specs, out_specs=out_specs, check_vma=False
    )
```

```python
import functools
import math

import jax
import jax.numpy as jnp
from jax import lax
from jax.experimental import pallas as pl
from jax.experimental.pallas import tpu as pltpu
from jax.sharding import PartitionSpec as P

BLOCK = 128
SIDE = math.exp(-0.5) / (1.0 + 2.0 * math.exp(-0.5))
CENTRE = 1.0 / (1.0 + 2.0 * math.exp(-0.5))
SMALL = pl.CostEstimate(flops=1, bytes_accessed=1, transcendentals=0)
VMEM_BYTES = 20 * 1024 * 1024
OUTER_VMEM_BYTES = 60 * 1024 * 1024


def outer_kernel(place_ref, bold_ref, out_ref, wide):
    frames, _, slab_y, slab_z = bold_ref.shape[1:]
    wide[...] = bold_ref[0].reshape(frames * slab_y, slab_z).astype(jnp.float32)
    for y in range(slab_y):
        out_ref[y] = wide[pl.ds(y, frames, stride=slab_y), :].astype(jnp.bfloat16)


def make_outer(place, bold):
    _, frames, _, slab_y, slab_z = bold.shape
    return pl.pallas_call(
        outer_kernel,
        grid_spec=pltpu.PrefetchScalarGridSpec(
            num_scalar_prefetch=1,
            grid=(1,),
            in_specs=[
                pl.BlockSpec((1, frames, 1, slab_y, slab_z), lambda _, at: (0, 0, at[1], 0, 0))
            ],
            out_specs=pl.BlockSpec((slab_y, frames, slab_z), lambda _, at: (0, 0, 0)),
            scratch_shapes=[pltpu.VMEM((frames * slab_y, slab_z), jnp.float32)],
        ),
        out_shape=jax.ShapeDtypeStruct((slab_y, frames, slab_z), jnp.bfloat16),
        compiler_params=pltpu.CompilerParams(vmem_limit_bytes=OUTER_VMEM_BYTES),
        cost_estimate=SMALL,
        name="outer_layer",
    )(place, bold)


def faces_kernel(place_ref, bold_ref, *refs):
    windows, frames, slab_x, slab_y, slab_z = bold_ref.shape
    per_frame = slab_x * slab_y
    wide = refs[-1]
    for window in range(windows):
        near_ref, outer_ref, edge_ref = refs[3 * window : 3 * window + 3]
        wide[...] = bold_ref[window].reshape(frames * per_frame, slab_z).astype(jnp.float32)

        def plane(x, y):
            taken = wide[pl.ds(x * slab_y + y, frames, stride=per_frame), :]
            return taken.astype(jnp.bfloat16)

        def layers(first_ref, last_ref):
            for y in range(slab_y):
                first_ref[y] = plane(0, y)
                last_ref[y] = plane(1, y)

        pl.when(place_ref[1] == 0)(functools.partial(layers, outer_ref, near_ref))
        pl.when(place_ref[1] != 0)(functools.partial(layers, near_ref, outer_ref))

        def edges(y):
            for x in range(slab_x):
                edge_ref[x] = plane(x, y)

        pl.when(place_ref[0] == 0)(functools.partial(edges, slab_y - 1))
        pl.when(place_ref[0] != 0)(functools.partial(edges, 0))


def make_faces(place, bold):
    windows, frames, slab_x, slab_y, slab_z = bold.shape
    layer = jax.ShapeDtypeStruct((slab_y, frames, slab_z), jnp.bfloat16)
    edge = jax.ShapeDtypeStruct((slab_x, frames, slab_z), jnp.bfloat16)
    whole = lambda array: pl.BlockSpec(array.shape, lambda _: (0,) * len(array.shape))
    return pl.pallas_call(
        faces_kernel,
        grid=(1,),
        in_specs=[pl.BlockSpec(memory_space=pltpu.SMEM), whole(bold)],
        out_specs=[whole(layer), whole(layer), whole(edge)] * windows,
        out_shape=[layer, layer, edge] * windows,
        scratch_shapes=[pltpu.VMEM((frames * slab_x * slab_y, slab_z), jnp.float32)],
        compiler_params=pltpu.CompilerParams(vmem_limit_bytes=VMEM_BYTES),
        cost_estimate=SMALL,
        name="faces",
    )(place, bold)


def three_taps(before, here, after):
    return SIDE * before + CENTRE * here + SIDE * after


def along_z(part):
    lane = lax.broadcasted_iota(jnp.int32, part.shape, 1)
    last = part.shape[1] - 1
    before = jnp.where(lane == 0, 0.0, pltpu.roll(part, 1, 1))
    after = jnp.where(lane == last, 0.0, pltpu.roll(part, last, 1))
    return three_taps(before, part, after)


def place_edge(planes, x, edge, col):
    planes[x, 0] = jnp.where(col == 0, 0.0, edge)
    planes[x, planes.shape[1] - 1] = jnp.where(col == 0, edge, 0.0)


def standardise(smooth):
    frames = smooth.shape[0]
    centred = smooth - jnp.mean(smooth, axis=0, keepdims=True)
    spread = jnp.mean(centred * centred, axis=0, keepdims=True)
    return (centred * lax.rsqrt((spread + 1e-05) * frames)).astype(jnp.bfloat16)


def pick(parts, gm_ref, out_ref):
    voxels = parts[0].shape[1]
    rows = gm_ref.shape[1]
    step = 2 * BLOCK
    for start in range(0, rows, step):
        wanted = gm_ref[:, start : start + step]
        voxel = lax.broadcasted_iota(jnp.int32, (voxels, step), 0)
        chosen = jnp.where(voxel == wanted, 1.0, 0.0).astype(jnp.bfloat16)
        total = jnp.dot(parts[0][...], chosen, preferred_element_type=jnp.float32)
        for part in parts[1:]:
            total += jnp.dot(part[...], chosen, preferred_element_type=jnp.float32)
        out_ref[:, start : start + step] = total.astype(out_ref.dtype)


def inner_kernel(
    place_ref, near_ref, outer_ref, edge_ref, gm_ref, out_ref, planes, high, middle, low
):
    slab_y, frames, slab_z = near_ref.shape
    slab_x = edge_ref.shape[0]
    even = place_ref[1] == 0

    def two_taps(here, other):
        return CENTRE * here + SIDE * other

    for y in range(slab_y):
        near, outer = near_ref[y].astype(jnp.float32), outer_ref[y].astype(jnp.float32)
        first, last = jnp.where(even, outer, near), jnp.where(even, near, outer)
        planes[0, y + 1] = two_taps(first, last)
        planes[1, y + 1] = two_taps(last, first)
    edges = [edge_ref[x].astype(jnp.float32) for x in range(slab_x)]
    for x in range(slab_x):
        place_edge(planes, x, two_taps(edges[x], edges[1 - x]), place_ref[0])
    for x in range(slab_x):
        for y in range(slab_y):
            part = along_z(three_taps(planes[x, y], planes[x, y + 1], planes[x, y + 2]))
            start = (x * slab_y + y) * slab_z
            for term in (high, middle, low):
                rounded = part.astype(jnp.bfloat16)
                term[:, start : start + slab_z] = rounded
                part = part - rounded.astype(jnp.float32)
    pick([high, middle, low], gm_ref, out_ref)


def halo_kernel(
    place_ref, near_ref, beyond_ref, edge_ref, corner_ref, gm_ref, out_ref, planes, scored
):
    slab_y, frames, slab_z = near_ref.shape
    even = place_ref[1] == 0

    def sides(own, beyond):
        own, beyond = own.astype(jnp.float32), beyond.astype(jnp.float32)
        return jnp.where(even, own, beyond), jnp.where(even, beyond, own)

    for y in range(slab_y):
        planes[0, y + 1], planes[1, y + 1] = sides(near_ref[y], beyond_ref[y])
    own = jnp.where(even, edge_ref[1], edge_ref[0])
    for x, edge in enumerate(sides(own, corner_ref[...])):
        place_edge(planes, x, edge, place_ref[0])
    for x in range(2):
        for y in range(slab_y):
            part = three_taps(planes[x, y], planes[x, y + 1], planes[x, y + 2])
            start = (x * slab_y + y) * slab_z
            scored[:, start : start + slab_z] = along_z(part).astype(jnp.bfloat16)
    pick([scored], gm_ref, out_ref)


def join_kernel(inner_ref, halo_ref, out_ref):
    for start in range(0, out_ref.shape[1], BLOCK):
        span = slice(start, start + BLOCK)
        smooth = inner_ref[:, span] + SIDE * halo_ref[:, span].astype(jnp.float32)
        out_ref[:, span] = standardise(smooth)


def call_on_rows(kernel, dtype, frames, place, operands, scratch, name):
    rows = operands[-1].shape[1]
    whole = lambda array: pl.BlockSpec(array.shape, lambda _: (0,) * array.ndim)
    scalars = [] if place is None else [place]
    return pl.pallas_call(
        kernel,
        grid=(1,),
        in_specs=[pl.BlockSpec(memory_space=pltpu.SMEM)] * len(scalars)
        + [whole(value) for value in operands],
        out_specs=pl.BlockSpec((frames, rows), lambda _: (0, 0)),
        out_shape=jax.ShapeDtypeStruct((frames, rows), dtype),
        scratch_shapes=scratch,
        compiler_params=pltpu.CompilerParams(vmem_limit_bytes=VMEM_BYTES),
        cost_estimate=SMALL,
        name=name,
    )(*scalars, *operands)


def blur_scratch(first, terms):
    slab_y, frames, slab_z = first.shape
    planes = pltpu.VMEM((2, slab_y + 2, frames, slab_z), jnp.float32)
    return [planes] + [pltpu.VMEM((frames, 2 * slab_y * slab_z), jnp.bfloat16)] * terms


def make_inner(place, near, outer, edge, gm):
    operands = (near, outer, edge, gm)
    scratch = blur_scratch(near, 3)
    return call_on_rows(
        inner_kernel, jnp.float32, near.shape[1], place, operands, scratch, "inner_blur"
    )


def make_halo(place, near, beyond, edge, corner, gm):
    operands = (near, beyond, edge, corner, gm)
    scratch = blur_scratch(near, 1)
    return call_on_rows(
        halo_kernel, jnp.bfloat16, near.shape[1], place, operands, scratch, "halo_blur"
    )


def join(inner, halo):
    return call_on_rows(
        join_kernel, jnp.bfloat16, inner.shape[0], None, (inner, halo), [], "join_score"
    )


def tiles_kernel(place_ref, present_ref, *refs, sources, window):
    parts = refs[:sources]
    out_ref, held, tiles, sems, out_sems = refs[-5:]
    blocks, slots = out_ref.shape[:2]

    loads = []
    first = 0
    for n, part in enumerate(parts):
        target = held.at[pl.ds(first, part.shape[0])]
        first += part.shape[0]
        loads.append(pltpu.make_async_copy(part, target, sems.at[n]))
        loads[-1].start()
    for load in loads:
        load.wait()

    def partner(block, slot):
        place = place_ref[block, slot]
        start = pl.multiple_of(lax.rem(place, blocks) * BLOCK, BLOCK)
        return held[lax.div(place, blocks), :, pl.ds(start, BLOCK)]

    stores = []
    for block in range(blocks):
        own = held[0, :, block * BLOCK : (block + 1) * BLOCK].T
        for slot in range(0, slots, 2):
            pair = jnp.concatenate([partner(block, slot), partner(block, slot + 1)], axis=1)
            both = jnp.dot(own, pair, preferred_element_type=jnp.float32)
            for n in range(2):
                tile = both[:, n * BLOCK : (n + 1) * BLOCK]
                tile = jnp.where(present_ref[block, slot + n] != 0, tile, 0.0)
                tiles[block, slot + n] = tile.astype(jnp.bfloat16)
        stores.append(
            pltpu.make_async_copy(tiles.at[block], out_ref.at[block, :, window], out_sems.at[block])
        )
        stores[-1].start()
    for store in stores:
        store.wait()


def make_tiles(window, windows, place, present, sources, earlier):
    frames, rows = sources[0].shape[1:]
    total = sum(source.shape[0] for source in sources)
    blocks = rows // BLOCK
    slots = place.shape[1]
    count = len(sources)
    anywhere = pl.BlockSpec(memory_space=pl.ANY)
    operands = list(sources) + ([] if earlier is None else [earlier])
    return pl.pallas_call(
        functools.partial(tiles_kernel, sources=count, window=window),
        grid_spec=pltpu.PrefetchScalarGridSpec(
            num_scalar_prefetch=2,
            grid=(1,),
            in_specs=[anywhere] * len(operands),
            out_specs=anywhere,
            scratch_shapes=[
                pltpu.VMEM((total, frames, rows), jnp.bfloat16),
                pltpu.VMEM((blocks, slots, BLOCK, BLOCK), jnp.bfloat16),
                pltpu.SemaphoreType.DMA((count,)),
                pltpu.SemaphoreType.DMA((blocks,)),
            ],
        ),
        out_shape=jax.ShapeDtypeStruct((blocks, slots, windows, BLOCK, BLOCK), jnp.bfloat16),
        input_output_aliases={} if earlier is None else {2 + count: 0},
        compiler_params=pltpu.CompilerParams(vmem_limit_bytes=VMEM_BYTES),
        cost_estimate=SMALL,
        name="tiles",
    )(place, present, *operands)


def after(value, *earlier):
    return lax.optimization_barrier((value,) + earlier)[0]


def on_device(bold, gm_index, partners):
    row_total = lax.axis_size("row")
    col_total = lax.axis_size("col")
    row = lax.axis_index("row")
    col = lax.axis_index("col")
    even = row % 2 == 0

    def other_col(value):
        return lax.ppermute(value, "col", [(0, 1), (1, 0)])

    ahead = [((i + 2 * (-1) ** i) % row_total, i) for i in range(row_total)]
    behind = [(i, source) for source, i in ahead]
    two_on = [(i, i + 2 * (-1) ** (i + 1)) for i in range(row_total)]
    two_on = [(i, target) for i, target in two_on if 0 <= target < row_total]
    in_pair = [(i, i ^ 1) for i in range(row_total)]

    gm = gm_index.reshape(1, -1)
    here = jnp.stack([col, row % 2]).astype(jnp.int32)

    blocks, slots = partners.shape
    ids = jnp.maximum(partners, 0)
    slab = ids // blocks
    hop = (slab // col_total - row + 2 + row_total) % row_total
    kind = jnp.where((hop == 1) == even, 4, 3)
    kind = jnp.where(hop == 2, 0, jnp.where((hop == 0) | (hop >= 4), 2 - (even == (hop >= 4)), kind))
    away = (slab % col_total != col).astype(jnp.int32)
    within = ids % blocks
    present = partners >= 0
    order = jnp.where(kind == 3, 2, jnp.where(kind == 2, 6, jnp.where(kind == 4, 8, kind)))
    part = order + away * jnp.where(order < 3, 3, 1)
    place = jnp.where(present, part * blocks + within, 0).astype(jnp.int32)
    present = present.astype(jnp.int32)

    def both(*parts):
        near = jnp.stack(parts, 0)
        return [near, other_col(near)]

    windows = bold.shape[0]
    gm_pair = lax.ppermute(gm, "row", in_pair)

    def give_halo(near, beyond, edge):
        corner = other_col(jnp.where(col == 0, beyond[-1], beyond[0]))
        return make_halo(here, near, beyond, edge, corner, gm_pair)

    beyond_0 = lax.ppermute(after(make_outer(here, bold), gm_pair), "row", two_on)
    near_0, outer_0, face_0, near_1, outer_1, face_1 = make_faces(after(here, gm_pair), bold)
    edge_0, edge_1 = other_col(face_0), other_col(face_1)
    inner_0 = make_inner(here, near_0, outer_0, edge_0, after(gm, edge_1))
    beyond_0 = after(beyond_0, inner_0)
    beyond_1 = lax.ppermute(after(outer_1, beyond_0), "row", two_on)
    given_0 = give_halo(near_0, beyond_0, edge_0)
    halo_0 = lax.ppermute(given_0, "row", in_pair)
    inner_1 = make_inner(here, near_1, outer_1, edge_1, after(gm, given_0))
    own_0 = join(inner_0, after(halo_0, inner_1))
    ahead_0 = lax.ppermute(own_0, "row", ahead)
    behind_0 = lax.ppermute(own_0, "row", behind)
    pair_0 = lax.ppermute(own_0, "row", in_pair)
    given_1 = give_halo(near_1, after(beyond_1, own_0), edge_1)
    halo_1 = lax.ppermute(given_1, "row", in_pair)
    pair_0 = after(pair_0, given_1)
    ahead_0, behind_0 = after(ahead_0, pair_0), after(behind_0, pair_0)
    own_1 = join(inner_1, after(halo_1, ahead_0, behind_0))
    pair_1 = lax.ppermute(own_1, "row", in_pair)
    ahead_1 = lax.ppermute(own_1, "row", ahead)
    behind_1 = lax.ppermute(own_1, "row", behind)
    rest_0 = lax.ppermute(after(ahead_0, own_1), "row", in_pair)
    ahead_1 = after(ahead_1, pair_1)
    behind_1 = after(behind_1, ahead_1)
    rest_1 = lax.ppermute(ahead_1, "row", in_pair)
    rest_0 = after(rest_0, ahead_1, behind_1)
    sources_0 = both(own_0, ahead_0, pair_0) + both(behind_0) + both(rest_0)
    out = make_tiles(0, windows, place, present, sources_0, None)
    rest_1 = after(rest_1, out)
    sources_1 = both(own_1, ahead_1, pair_1) + both(behind_1) + both(rest_1)
    return make_tiles(1, windows, place, present, sources_1, out)


def solution(mesh):
    in_specs = (P("subj", None, "row", "col", None), P(("row", "col")), P(("row", "col"), None))
    out_specs = P(("row", "col"), None, "subj", None, None)
    return jax.shard_map(
        on_device, mesh=mesh, in_specs=in_specs, out_specs=out_specs, check_vma=False
    )
```

```python
import functools
import math

import jax
import jax.numpy as jnp
from jax import lax
from jax.experimental import pallas as pl
from jax.experimental.pallas import tpu as pltpu
from jax.sharding import PartitionSpec as P

BLOCK = 128
SIDE = math.exp(-0.5) / (1.0 + 2.0 * math.exp(-0.5))
CENTRE = 1.0 / (1.0 + 2.0 * math.exp(-0.5))
SMALL = pl.CostEstimate(flops=1, bytes_accessed=1, transcendentals=0)
VMEM_BYTES = 20 * 1024 * 1024
OUTER_VMEM_BYTES = 60 * 1024 * 1024


def outer_kernel(place_ref, bold_ref, out_ref, wide):
    frames, _, slab_y, slab_z = bold_ref.shape[1:]
    wide[...] = bold_ref[0].reshape(frames * slab_y, slab_z).astype(jnp.float32)
    for y in range(slab_y):
        out_ref[y] = wide[pl.ds(y, frames, stride=slab_y), :].astype(jnp.bfloat16)


def make_outer(window, place, bold):
    _, frames, _, slab_y, slab_z = bold.shape
    return pl.pallas_call(
        outer_kernel,
        grid_spec=pltpu.PrefetchScalarGridSpec(
            num_scalar_prefetch=1,
            grid=(1,),
            in_specs=[
                pl.BlockSpec((1, frames, 1, slab_y, slab_z), lambda _, at: (window, 0, at[1], 0, 0))
            ],
            out_specs=pl.BlockSpec((slab_y, frames, slab_z), lambda _, at: (0, 0, 0)),
            scratch_shapes=[pltpu.VMEM((frames * slab_y, slab_z), jnp.float32)],
        ),
        out_shape=jax.ShapeDtypeStruct((slab_y, frames, slab_z), jnp.bfloat16),
        compiler_params=pltpu.CompilerParams(vmem_limit_bytes=OUTER_VMEM_BYTES),
        cost_estimate=SMALL,
        name="outer_layer",
    )(place, bold)


def faces_kernel(place_ref, bold_ref, *refs):
    windows, frames, slab_x, slab_y, slab_z = bold_ref.shape
    per_frame = slab_x * slab_y
    wide = refs[-1]
    for window in range(windows):
        near_ref, outer_ref, edge_ref = refs[3 * window : 3 * window + 3]
        wide[...] = bold_ref[window].reshape(frames * per_frame, slab_z).astype(jnp.float32)

        def plane(x, y):
            taken = wide[pl.ds(x * slab_y + y, frames, stride=per_frame), :]
            return taken.astype(jnp.bfloat16)

        def layers(first_ref, last_ref):
            for y in range(slab_y):
                first_ref[y] = plane(0, y)
                last_ref[y] = plane(1, y)

        pl.when(place_ref[1] == 0)(functools.partial(layers, outer_ref, near_ref))
        pl.when(place_ref[1] != 0)(functools.partial(layers, near_ref, outer_ref))

        def edges(y):
            for x in range(slab_x):
                edge_ref[x] = plane(x, y)

        pl.when(place_ref[0] == 0)(functools.partial(edges, slab_y - 1))
        pl.when(place_ref[0] != 0)(functools.partial(edges, 0))


def make_faces(place, bold):
    windows, frames, slab_x, slab_y, slab_z = bold.shape
    layer = jax.ShapeDtypeStruct((slab_y, frames, slab_z), jnp.bfloat16)
    edge = jax.ShapeDtypeStruct((slab_x, frames, slab_z), jnp.bfloat16)
    whole = lambda array: pl.BlockSpec(array.shape, lambda _: (0,) * len(array.shape))
    return pl.pallas_call(
        faces_kernel,
        grid=(1,),
        in_specs=[pl.BlockSpec(memory_space=pltpu.SMEM), whole(bold)],
        out_specs=[whole(layer), whole(layer), whole(edge)] * windows,
        out_shape=[layer, layer, edge] * windows,
        scratch_shapes=[pltpu.VMEM((frames * slab_x * slab_y, slab_z), jnp.float32)],
        compiler_params=pltpu.CompilerParams(vmem_limit_bytes=VMEM_BYTES),
        cost_estimate=SMALL,
        name="faces",
    )(place, bold)


def three_taps(before, here, after):
    return SIDE * before + CENTRE * here + SIDE * after


def along_z(part):
    lane = lax.broadcasted_iota(jnp.int32, part.shape, 1)
    last = part.shape[1] - 1
    before = jnp.where(lane == 0, 0.0, pltpu.roll(part, 1, 1))
    after = jnp.where(lane == last, 0.0, pltpu.roll(part, last, 1))
    return three_taps(before, part, after)


def place_edge(planes, x, edge, col):
    planes[x, 0] = jnp.where(col == 0, 0.0, edge)
    planes[x, planes.shape[1] - 1] = jnp.where(col == 0, edge, 0.0)


def standardise(smooth):
    frames = smooth.shape[0]
    centred = smooth - jnp.mean(smooth, axis=0, keepdims=True)
    spread = jnp.mean(centred * centred, axis=0, keepdims=True)
    return (centred * lax.rsqrt((spread + 1e-05) * frames)).astype(jnp.bfloat16)


def pick(parts, gm_ref, out_ref):
    voxels = parts[0].shape[1]
    rows = gm_ref.shape[1]
    step = 2 * BLOCK
    for start in range(0, rows, step):
        wanted = gm_ref[:, start : start + step]
        voxel = lax.broadcasted_iota(jnp.int32, (voxels, step), 0)
        chosen = jnp.where(voxel == wanted, 1.0, 0.0).astype(jnp.bfloat16)
        total = jnp.dot(parts[0][...], chosen, preferred_element_type=jnp.float32)
        for part in parts[1:]:
            total += jnp.dot(part[...], chosen, preferred_element_type=jnp.float32)
        out_ref[:, start : start + step] = total.astype(out_ref.dtype)


def panel_kernel(
    place_ref, near_ref, outer_ref, facing_ref, across_ref, edge_ref, corner_ref, gm_ref, out_ref,
    planes, scored,
):
    slab_y, frames, slab_z = near_ref.shape
    even = place_ref[1] == 0

    def along_x(across, outer, near, facing):
        layers = [part.astype(jnp.float32) for part in (across, outer, near, facing)]
        outer, near = three_taps(*layers[:3]), three_taps(*layers[1:])
        return jnp.where(even, outer, near), jnp.where(even, near, outer)

    for y in range(slab_y):
        planes[0, y + 1], planes[1, y + 1] = along_x(
            across_ref[y], outer_ref[y], near_ref[y], facing_ref[y]
        )
    outer = jnp.where(even, edge_ref[0], edge_ref[1])
    near = jnp.where(even, edge_ref[1], edge_ref[0])
    for x, edge in enumerate(along_x(corner_ref[0], outer, near, corner_ref[1])):
        place_edge(planes, x, edge, place_ref[0])
    for x in range(2):
        for y in range(slab_y):
            part = three_taps(planes[x, y], planes[x, y + 1], planes[x, y + 2])
            start = (x * slab_y + y) * slab_z
            scored[:, start : start + slab_z] = standardise(along_z(part))
    pick([scored], gm_ref, out_ref)


def inner_kernel(
    place_ref, near_ref, outer_ref, edge_ref, gm_ref, out_ref, planes, high, middle, low
):
    slab_y, frames, slab_z = near_ref.shape
    slab_x = edge_ref.shape[0]
    even = place_ref[1] == 0

    def two_taps(here, other):
        return CENTRE * here + SIDE * other

    for y in range(slab_y):
        near, outer = near_ref[y].astype(jnp.float32), outer_ref[y].astype(jnp.float32)
        first, last = jnp.where(even, outer, near), jnp.where(even, near, outer)
        planes[0, y + 1] = two_taps(first, last)
        planes[1, y + 1] = two_taps(last, first)
    edges = [edge_ref[x].astype(jnp.float32) for x in range(slab_x)]
    for x in range(slab_x):
        place_edge(planes, x, two_taps(edges[x], edges[1 - x]), place_ref[0])
    for x in range(slab_x):
        for y in range(slab_y):
            part = along_z(three_taps(planes[x, y], planes[x, y + 1], planes[x, y + 2]))
            start = (x * slab_y + y) * slab_z
            for term in (high, middle, low):
                rounded = part.astype(jnp.bfloat16)
                term[:, start : start + slab_z] = rounded
                part = part - rounded.astype(jnp.float32)
    pick([high, middle, low], gm_ref, out_ref)


def halo_kernel(
    place_ref, near_ref, beyond_ref, edge_ref, corner_ref, gm_ref, out_ref, planes, scored
):
    slab_y, frames, slab_z = near_ref.shape
    even = place_ref[1] == 0

    def sides(own, beyond):
        own, beyond = own.astype(jnp.float32), beyond.astype(jnp.float32)
        return jnp.where(even, own, beyond), jnp.where(even, beyond, own)

    for y in range(slab_y):
        planes[0, y + 1], planes[1, y + 1] = sides(near_ref[y], beyond_ref[y])
    own = jnp.where(even, edge_ref[1], edge_ref[0])
    for x, edge in enumerate(sides(own, corner_ref[...])):
        place_edge(planes, x, edge, place_ref[0])
    for x in range(2):
        for y in range(slab_y):
            part = three_taps(planes[x, y], planes[x, y + 1], planes[x, y + 2])
            start = (x * slab_y + y) * slab_z
            scored[:, start : start + slab_z] = along_z(part).astype(jnp.bfloat16)
    pick([scored], gm_ref, out_ref)


def join_kernel(inner_ref, halo_ref, out_ref):
    for start in range(0, out_ref.shape[1], BLOCK):
        span = slice(start, start + BLOCK)
        smooth = inner_ref[:, span] + SIDE * halo_ref[:, span].astype(jnp.float32)
        out_ref[:, span] = standardise(smooth)


def call_on_rows(kernel, dtype, frames, place, operands, scratch, name):
    rows = operands[-1].shape[1]
    whole = lambda array: pl.BlockSpec(array.shape, lambda _: (0,) * array.ndim)
    scalars = [] if place is None else [place]
    return pl.pallas_call(
        kernel,
        grid=(1,),
        in_specs=[pl.BlockSpec(memory_space=pltpu.SMEM)] * len(scalars)
        + [whole(value) for value in operands],
        out_specs=pl.BlockSpec((frames, rows), lambda _: (0, 0)),
        out_shape=jax.ShapeDtypeStruct((frames, rows), dtype),
        scratch_shapes=scratch,
        compiler_params=pltpu.CompilerParams(vmem_limit_bytes=VMEM_BYTES),
        cost_estimate=SMALL,
        name=name,
    )(*scalars, *operands)


def blur_scratch(first, terms):
    slab_y, frames, slab_z = first.shape
    planes = pltpu.VMEM((2, slab_y + 2, frames, slab_z), jnp.float32)
    return [planes] + [pltpu.VMEM((frames, 2 * slab_y * slab_z), jnp.bfloat16)] * terms


def make_panel(place, near, outer, facing, across, edge, corner, gm):
    operands = (near, outer, facing, across, edge, corner, gm)
    scratch = blur_scratch(near, 1)
    return call_on_rows(
        panel_kernel, jnp.bfloat16, near.shape[1], place, operands, scratch, "blur_score_pick"
    )


def make_inner(place, near, outer, edge, gm):
    operands = (near, outer, edge, gm)
    scratch = blur_scratch(near, 3)
    return call_on_rows(
        inner_kernel, jnp.float32, near.shape[1], place, operands, scratch, "inner_blur"
    )


def make_halo(place, near, beyond, edge, corner, gm):
    operands = (near, beyond, edge, corner, gm)
    scratch = blur_scratch(near, 1)
    return call_on_rows(
        halo_kernel, jnp.bfloat16, near.shape[1], place, operands, scratch, "halo_blur"
    )


def join(inner, halo):
    return call_on_rows(
        join_kernel, jnp.bfloat16, inner.shape[0], None, (inner, halo), [], "join_score"
    )


def tiles_kernel(place_ref, present_ref, *refs, sources, window):
    parts = refs[:sources]
    out_ref, held, tiles, sems, out_sems = refs[-5:]
    blocks, slots = out_ref.shape[:2]

    loads = []
    for n, part in enumerate(parts):
        mine = part.at[window] if len(part.shape) == 3 else part
        loads.append(pltpu.make_async_copy(mine, held.at[n], sems.at[n]))
        loads[-1].start()
    for load in loads:
        load.wait()

    def partner(block, slot):
        place = place_ref[block, slot]
        start = pl.multiple_of(lax.rem(place, blocks) * BLOCK, BLOCK)
        return held[lax.div(place, blocks), :, pl.ds(start, BLOCK)]

    stores = []
    for block in range(blocks):
        own = held[0, :, block * BLOCK : (block + 1) * BLOCK].T
        for slot in range(0, slots, 2):
            pair = jnp.concatenate([partner(block, slot), partner(block, slot + 1)], axis=1)
            both = jnp.dot(own, pair, preferred_element_type=jnp.float32)
            for n in range(2):
                tile = both[:, n * BLOCK : (n + 1) * BLOCK]
                tile = jnp.where(present_ref[block, slot + n] != 0, tile, 0.0)
                tiles[block, slot + n] = tile.astype(jnp.bfloat16)
        stores.append(
            pltpu.make_async_copy(tiles.at[block], out_ref.at[block, :, window], out_sems.at[block])
        )
        stores[-1].start()
    for store in stores:
        store.wait()


def make_tiles(window, windows, place, present, sources, earlier):
    frames, rows = sources[0].shape[-2:]
    blocks = rows // BLOCK
    slots = place.shape[1]
    count = len(sources)
    anywhere = pl.BlockSpec(memory_space=pl.ANY)
    operands = list(sources) + ([] if earlier is None else [earlier])
    return pl.pallas_call(
        functools.partial(tiles_kernel, sources=count, window=window),
        grid_spec=pltpu.PrefetchScalarGridSpec(
            num_scalar_prefetch=2,
            grid=(1,),
            in_specs=[anywhere] * len(operands),
            out_specs=anywhere,
            scratch_shapes=[
                pltpu.VMEM((count, frames, rows), jnp.bfloat16),
                pltpu.VMEM((blocks, slots, BLOCK, BLOCK), jnp.bfloat16),
                pltpu.SemaphoreType.DMA((count,)),
                pltpu.SemaphoreType.DMA((blocks,)),
            ],
        ),
        out_shape=jax.ShapeDtypeStruct((blocks, slots, windows, BLOCK, BLOCK), jnp.bfloat16),
        input_output_aliases={} if earlier is None else {2 + count: 0},
        compiler_params=pltpu.CompilerParams(vmem_limit_bytes=VMEM_BYTES),
        cost_estimate=SMALL,
        name="tiles",
    )(place, present, *operands)


def after(value, *earlier):
    return lax.optimization_barrier((value,) + earlier)[0]


def on_device(bold, gm_index, partners):
    row_total = lax.axis_size("row")
    col_total = lax.axis_size("col")
    row = lax.axis_index("row")
    col = lax.axis_index("col")
    even = row % 2 == 0

    def other_col(value):
        return lax.ppermute(value, "col", [(0, 1), (1, 0)])

    ahead = [((i + 2 * (-1) ** i) % row_total, i) for i in range(row_total)]
    behind_pairs = [(i, source) for source, i in ahead]
    two_on = [(i, i + 2 * (-1) ** (i + 1)) for i in range(row_total)]
    two_on = [(i, target) for i, target in two_on if 0 <= target < row_total]
    across_pairs = [(i, i - (-1) ** i) for i in range(row_total)]
    across_pairs = [(i, target) for i, target in across_pairs if 0 <= target < row_total]
    in_pair = [(i, i ^ 1) for i in range(row_total)]

    gm = gm_index.reshape(1, -1)
    here = jnp.stack([col, row % 2]).astype(jnp.int32)

    blocks, slots = partners.shape
    ids = jnp.maximum(partners, 0)
    slab = ids // blocks
    hop = (slab // col_total - row + 2 + row_total) % row_total
    kind = jnp.where((hop == 1) == even, 4, 3)
    kind = jnp.where(hop == 2, 0, jnp.where((hop == 0) | (hop >= 4), 2 - (even == (hop >= 4)), kind))
    away = (slab % col_total != col).astype(jnp.int32)
    within = ids % blocks
    present = partners >= 0
    place = jnp.where(present, (kind + 5 * away) * blocks + within, 0).astype(jnp.int32)
    present = present.astype(jnp.int32)

    windows = bold.shape[0]
    gm_pair = lax.ppermute(gm, "row", in_pair)

    def ends(*layers):
        return other_col(jnp.stack([jnp.where(col == 0, layer[-1], layer[0]) for layer in layers], 0))

    beyond_1 = lax.ppermute(make_outer(1, here, bold), "row", two_on)
    near_0, outer_0, face_0, near_1, outer_1, face_1 = make_faces(here, bold)
    facing_0 = lax.ppermute(after(near_0, gm_pair), "row", in_pair)
    across_0 = lax.ppermute(after(outer_0, gm_pair), "row", across_pairs)
    edge_0, edge_1 = other_col(face_0), other_col(face_1)
    inner_1 = make_inner(here, near_1, outer_1, edge_1, after(gm, edge_0))
    beyond_1 = after(beyond_1, inner_1)
    given_1 = make_halo(here, near_1, beyond_1, edge_1, ends(beyond_1)[0], gm_pair)
    facing_0, across_0 = after(facing_0, given_1), after(across_0, given_1)
    halo_1 = lax.ppermute(after(given_1, facing_0, across_0), "row", in_pair)
    corner_0 = ends(across_0, facing_0)
    own_0 = make_panel(here, near_0, outer_0, facing_0, across_0, edge_0, corner_0, gm)
    ahead_0 = lax.ppermute(own_0, "row", ahead)
    halo_1 = after(halo_1, own_0)
    own_1 = join(inner_1, halo_1)
    own = jnp.stack([own_0, own_1], 0)
    ahead_1 = lax.ppermute(own_1, "row", ahead)
    pair = lax.ppermute(own, "row", in_pair)
    behind = lax.ppermute(own, "row", behind_pairs)
    own_far = other_col(own)
    ahead_0 = after(ahead_0, own)
    rest_0 = lax.ppermute(ahead_0, "row", in_pair)
    ahead_1, pair = after(ahead_1, ahead_0), after(pair, ahead_0)
    rest_1 = lax.ppermute(ahead_1, "row", in_pair)
    rest_0 = after(rest_0, ahead_1)
    behind = after(behind, rest_0, pair)
    pair_far = other_col(pair)
    behind_far = [other_col(behind[window]) for window in range(windows)]
    ahead_far = [other_col(ahead_0), other_col(ahead_1)]
    rest_far_0 = other_col(rest_0)
    sources = [own, ahead_0, behind, pair, rest_0]
    sources += [own_far, ahead_far[0], behind_far[0], pair_far, rest_far_0]
    out = make_tiles(0, windows, place, present, sources, None)
    sources = [own, ahead_1, behind, pair, rest_1]
    sources += [own_far, ahead_far[1], behind_far[1], pair_far, other_col(rest_1)]
    return make_tiles(1, windows, place, present, sources, out)


def solution(mesh):
    in_specs = (P("subj", None, "row", "col", None), P(("row", "col")), P(("row", "col"), None))
    out_specs = P(("row", "col"), None, "subj", None, None)
    return jax.shard_map(
        on_device, mesh=mesh, in_specs=in_specs, out_specs=out_specs, check_vma=False
    )
```

```python
import functools
import math

import jax
import jax.numpy as jnp
from jax import lax
from jax.experimental import pallas as pl
from jax.experimental.pallas import tpu as pltpu
from jax.sharding import PartitionSpec as P

BLOCK = 128
SIDE = math.exp(-0.5) / (1.0 + 2.0 * math.exp(-0.5))
CENTRE = 1.0 / (1.0 + 2.0 * math.exp(-0.5))
SMALL = pl.CostEstimate(flops=1, bytes_accessed=1, transcendentals=0)
VMEM_BYTES = 20 * 1024 * 1024


def is_even():
    return lax.axis_index("row") % 2 == 0


def is_first():
    return lax.axis_index("col") == 0


def faces_kernel(bold_ref, *refs):
    windows, frames, slab_x, slab_y, slab_z = bold_ref.shape
    per_frame = slab_x * slab_y
    wide = refs[-1]
    for window in range(windows):
        near_ref, outer_ref, edge_ref = refs[3 * window : 3 * window + 3]
        wide[...] = bold_ref[window].reshape(frames * per_frame, slab_z).astype(jnp.float32)

        def plane(x, y):
            taken = wide[pl.ds(x * slab_y + y, frames, stride=per_frame), :]
            return taken.astype(jnp.bfloat16)

        def layers(first_ref, last_ref):
            for y in range(slab_y):
                first_ref[y] = plane(0, y)
                last_ref[y] = plane(1, y)

        pl.when(is_even())(functools.partial(layers, outer_ref, near_ref))
        pl.when(~is_even())(functools.partial(layers, near_ref, outer_ref))

        def edges(y):
            for x in range(slab_x):
                edge_ref[x] = plane(x, y)

        pl.when(is_first())(functools.partial(edges, slab_y - 1))
        pl.when(~is_first())(functools.partial(edges, 0))


def make_faces(bold):
    windows, frames, slab_x, slab_y, slab_z = bold.shape
    layer = jax.ShapeDtypeStruct((slab_y, frames, slab_z), jnp.bfloat16)
    edge = jax.ShapeDtypeStruct((slab_x, frames, slab_z), jnp.bfloat16)
    whole = lambda array: pl.BlockSpec(array.shape, lambda _: (0,) * len(array.shape))
    return pl.pallas_call(
        faces_kernel,
        grid=(1,),
        in_specs=[whole(bold)],
        out_specs=[whole(layer), whole(layer), whole(edge)] * windows,
        out_shape=[layer, layer, edge] * windows,
        scratch_shapes=[pltpu.VMEM((frames * slab_x * slab_y, slab_z), jnp.float32)],
        compiler_params=pltpu.CompilerParams(vmem_limit_bytes=VMEM_BYTES),
        cost_estimate=SMALL,
        name="faces",
    )(bold)


def three_taps(before, here, after):
    return SIDE * before + CENTRE * here + SIDE * after


def along_z(part):
    lane = lax.broadcasted_iota(jnp.int32, part.shape, 1)
    last = part.shape[1] - 1
    before = jnp.where(lane == 0, 0.0, pltpu.roll(part, 1, 1))
    after = jnp.where(lane == last, 0.0, pltpu.roll(part, last, 1))
    return three_taps(before, part, after)


def place_edge(planes, x, edge):
    planes[x, 0] = jnp.where(is_first(), 0.0, edge)
    planes[x, planes.shape[1] - 1] = jnp.where(is_first(), edge, 0.0)


def standardise(smooth):
    frames = smooth.shape[0]
    centred = smooth - jnp.mean(smooth, axis=0, keepdims=True)
    spread = jnp.mean(centred * centred, axis=0, keepdims=True)
    return (centred * lax.rsqrt((spread + 1e-05) * frames)).astype(jnp.bfloat16)


def pick(parts, gm_ref, out_ref):
    voxels = parts[0].shape[1]
    rows = gm_ref.shape[1]
    step = 2 * BLOCK
    for start in range(0, rows, step):
        wanted = gm_ref[:, start : start + step]
        voxel = lax.broadcasted_iota(jnp.int32, (voxels, step), 0)
        chosen = jnp.where(voxel == wanted, 1.0, 0.0).astype(jnp.bfloat16)
        total = jnp.dot(parts[0][...], chosen, preferred_element_type=jnp.float32)
        for part in parts[1:]:
            total += jnp.dot(part[...], chosen, preferred_element_type=jnp.float32)
        out_ref[:, start : start + step] = total.astype(out_ref.dtype)


def panel_kernel(
    near_ref, outer_ref, facing_ref, across_ref, edge_ref, corner_ref, gm_ref, out_ref,
    planes, scored,
):
    slab_y, frames, slab_z = near_ref.shape
    even = is_even()

    def along_x(across, outer, near, facing):
        layers = [part.astype(jnp.float32) for part in (across, outer, near, facing)]
        outer, near = three_taps(*layers[:3]), three_taps(*layers[1:])
        return jnp.where(even, outer, near), jnp.where(even, near, outer)

    for y in range(slab_y):
        planes[0, y + 1], planes[1, y + 1] = along_x(
            across_ref[y], outer_ref[y], near_ref[y], facing_ref[y]
        )
    outer = jnp.where(even, edge_ref[0], edge_ref[1])
    near = jnp.where(even, edge_ref[1], edge_ref[0])
    for x, edge in enumerate(along_x(corner_ref[0], outer, near, corner_ref[1])):
        place_edge(planes, x, edge)
    for x in range(2):
        for y in range(slab_y):
            part = three_taps(planes[x, y], planes[x, y + 1], planes[x, y + 2])
            start = (x * slab_y + y) * slab_z
            scored[:, start : start + slab_z] = standardise(along_z(part))
    pick([scored], gm_ref, out_ref)


def inner_kernel(
    near_ref, outer_ref, edge_ref, gm_ref, out_ref, planes, high, middle, low
):
    slab_y, frames, slab_z = near_ref.shape
    slab_x = edge_ref.shape[0]
    even = is_even()

    def two_taps(here, other):
        return CENTRE * here + SIDE * other

    for y in range(slab_y):
        near, outer = near_ref[y].astype(jnp.float32), outer_ref[y].astype(jnp.float32)
        first, last = jnp.where(even, outer, near), jnp.where(even, near, outer)
        planes[0, y + 1] = two_taps(first, last)
        planes[1, y + 1] = two_taps(last, first)
    edges = [edge_ref[x].astype(jnp.float32) for x in range(slab_x)]
    for x in range(slab_x):
        place_edge(planes, x, two_taps(edges[x], edges[1 - x]))
    for x in range(slab_x):
        for y in range(slab_y):
            part = along_z(three_taps(planes[x, y], planes[x, y + 1], planes[x, y + 2]))
            start = (x * slab_y + y) * slab_z
            for term in (high, middle, low):
                rounded = part.astype(jnp.bfloat16)
                term[:, start : start + slab_z] = rounded
                part = part - rounded.astype(jnp.float32)
    pick([high, middle, low], gm_ref, out_ref)


def halo_kernel(
    near_ref, beyond_ref, edge_ref, corner_ref, gm_ref, out_ref, planes, scored
):
    slab_y, frames, slab_z = near_ref.shape
    even = is_even()

    def sides(own, beyond):
        own, beyond = own.astype(jnp.float32), beyond.astype(jnp.float32)
        return jnp.where(even, own, beyond), jnp.where(even, beyond, own)

    for y in range(slab_y):
        planes[0, y + 1], planes[1, y + 1] = sides(near_ref[y], beyond_ref[y])
    own = jnp.where(even, edge_ref[1], edge_ref[0])
    for x, edge in enumerate(sides(own, corner_ref[...])):
        place_edge(planes, x, edge)
    for x in range(2):
        for y in range(slab_y):
            part = three_taps(planes[x, y], planes[x, y + 1], planes[x, y + 2])
            start = (x * slab_y + y) * slab_z
            scored[:, start : start + slab_z] = along_z(part).astype(jnp.bfloat16)
    pick([scored], gm_ref, out_ref)


def join_kernel(inner_ref, halo_ref, out_ref):
    for start in range(0, out_ref.shape[1], BLOCK):
        span = slice(start, start + BLOCK)
        smooth = inner_ref[:, span] + SIDE * halo_ref[:, span].astype(jnp.float32)
        out_ref[:, span] = standardise(smooth)


def call_on_rows(kernel, dtype, frames, operands, scratch, name):
    rows = operands[-1].shape[1]
    whole = lambda array: pl.BlockSpec(array.shape, lambda _: (0,) * array.ndim)
    return pl.pallas_call(
        kernel,
        grid=(1,),
        in_specs=[whole(value) for value in operands],
        out_specs=pl.BlockSpec((frames, rows), lambda _: (0, 0)),
        out_shape=jax.ShapeDtypeStruct((frames, rows), dtype),
        scratch_shapes=scratch,
        compiler_params=pltpu.CompilerParams(vmem_limit_bytes=VMEM_BYTES),
        cost_estimate=SMALL,
        name=name,
    )(*operands)


def blur_scratch(first, terms):
    slab_y, frames, slab_z = first.shape
    planes = pltpu.VMEM((2, slab_y + 2, frames, slab_z), jnp.float32)
    return [planes] + [pltpu.VMEM((frames, 2 * slab_y * slab_z), jnp.bfloat16)] * terms


def make_panel(near, outer, facing, across, edge, corner, gm):
    operands = (near, outer, facing, across, edge, corner, gm)
    scratch = blur_scratch(near, 1)
    return call_on_rows(
        panel_kernel, jnp.bfloat16, near.shape[1], operands, scratch, "blur_score_pick"
    )


def make_inner(near, outer, edge, gm):
    operands = (near, outer, edge, gm)
    scratch = blur_scratch(near, 3)
    return call_on_rows(
        inner_kernel, jnp.float32, near.shape[1], operands, scratch, "inner_blur"
    )


def make_halo(near, beyond, edge, corner, gm):
    operands = (near, beyond, edge, corner, gm)
    scratch = blur_scratch(near, 1)
    return call_on_rows(
        halo_kernel, jnp.bfloat16, near.shape[1], operands, scratch, "halo_blur"
    )


def join(inner, halo):
    return call_on_rows(
        join_kernel, jnp.bfloat16, inner.shape[0], (inner, halo), [], "join_score"
    )


def tiles_kernel(place_ref, present_ref, *refs, sources, window):
    parts = refs[:sources]
    out_ref, held, tiles, sems, out_sems = refs[-5:]
    blocks, slots = out_ref.shape[:2]

    loads = []
    first = 0
    for n, part in enumerate(parts):
        target = held.at[pl.ds(first, part.shape[0])]
        first += part.shape[0]
        loads.append(pltpu.make_async_copy(part, target, sems.at[n]))
        loads[-1].start()
    for load in loads:
        load.wait()

    def partner(block, slot):
        place = place_ref[block, slot]
        start = pl.multiple_of(lax.rem(place, blocks) * BLOCK, BLOCK)
        return held[lax.div(place, blocks), :, pl.ds(start, BLOCK)]

    stores = []
    for block in range(blocks):
        own = held[0, :, block * BLOCK : (block + 1) * BLOCK].T
        for slot in range(0, slots, 2):
            pair = jnp.concatenate([partner(block, slot), partner(block, slot + 1)], axis=1)
            both = jnp.dot(own, pair, preferred_element_type=jnp.float32)
            for n in range(2):
                tile = both[:, n * BLOCK : (n + 1) * BLOCK]
                tile = jnp.where(present_ref[block, slot + n] != 0, tile, 0.0)
                tiles[block, slot + n] = tile.astype(jnp.bfloat16)
        stores.append(
            pltpu.make_async_copy(tiles.at[block], out_ref.at[block, :, window], out_sems.at[block])
        )
        stores[-1].start()
    for store in stores:
        store.wait()


def make_tiles(window, windows, place, present, sources, earlier):
    frames, rows = sources[0].shape[1:]
    total = sum(source.shape[0] for source in sources)
    blocks = rows // BLOCK
    slots = place.shape[1]
    count = len(sources)
    anywhere = pl.BlockSpec(memory_space=pl.ANY)
    operands = list(sources) + ([] if earlier is None else [earlier])
    return pl.pallas_call(
        functools.partial(tiles_kernel, sources=count, window=window),
        grid_spec=pltpu.PrefetchScalarGridSpec(
            num_scalar_prefetch=2,
            grid=(1,),
            in_specs=[anywhere] * len(operands),
            out_specs=anywhere,
            scratch_shapes=[
                pltpu.VMEM((total, frames, rows), jnp.bfloat16),
                pltpu.VMEM((blocks, slots, BLOCK, BLOCK), jnp.bfloat16),
                pltpu.SemaphoreType.DMA((count,)),
                pltpu.SemaphoreType.DMA((blocks,)),
            ],
        ),
        out_shape=jax.ShapeDtypeStruct((blocks, slots, windows, BLOCK, BLOCK), jnp.bfloat16),
        input_output_aliases={} if earlier is None else {2 + count: 0},
        compiler_params=pltpu.CompilerParams(vmem_limit_bytes=VMEM_BYTES),
        cost_estimate=SMALL,
        name="tiles",
    )(place, present, *operands)


def after(value, *earlier):
    return lax.optimization_barrier((value,) + earlier)[0]


def on_device(bold, gm_index, partners):
    row_total = lax.axis_size("row")
    col_total = lax.axis_size("col")
    row = lax.axis_index("row")
    col = lax.axis_index("col")
    even = row % 2 == 0

    def other_col(value):
        return lax.ppermute(value, "col", [(0, 1), (1, 0)])

    ahead = [((i + 2 * (-1) ** i) % row_total, i) for i in range(row_total)]
    behind = [(i, source) for source, i in ahead]
    two_on = [(i, i + 2 * (-1) ** (i + 1)) for i in range(row_total)]
    two_on = [(i, target) for i, target in two_on if 0 <= target < row_total]
    across_pairs = [(i, i - (-1) ** i) for i in range(row_total)]
    across_pairs = [(i, target) for i, target in across_pairs if 0 <= target < row_total]
    in_pair = [(i, i ^ 1) for i in range(row_total)]

    gm = gm_index.reshape(1, -1)
    blocks, slots = partners.shape
    ids = jnp.maximum(partners, 0)
    slab = ids // blocks
    hop = (slab // col_total - row + 2 + row_total) % row_total
    kind = jnp.where((hop == 1) == even, 4, 3)
    kind = jnp.where(hop == 2, 0, jnp.where((hop == 0) | (hop >= 4), 2 - (even == (hop >= 4)), kind))
    away = (slab % col_total != col).astype(jnp.int32)
    within = ids % blocks
    present = partners >= 0
    parts_0 = jnp.where(kind == 4, 8 + away, kind // 2 * 4 + kind % 2 + 2 * away)
    parts_1 = jnp.where(kind == 3, 4 + away, jnp.where(kind < 2, kind, kind // 2 + 5) + 2 * away)
    place_0, place_1 = (
        jnp.where(present, part * blocks + within, 0).astype(jnp.int32)
        for part in (parts_0, parts_1)
    )
    present = present.astype(jnp.int32)

    def both(*parts):
        near = jnp.stack(parts, 0)
        return [near, other_col(near)]

    windows = bold.shape[0]
    gm_pair = lax.ppermute(gm, "row", in_pair)

    def ends(*layers):
        return other_col(jnp.stack([jnp.where(col == 0, layer[-1], layer[0]) for layer in layers], 0))

    near_0, outer_0, face_0, near_1, outer_1, face_1 = make_faces(bold)
    beyond_1 = lax.ppermute(outer_1, "row", two_on)
    facing_0 = lax.ppermute(after(near_0, gm_pair), "row", in_pair)
    across_0 = lax.ppermute(after(outer_0, gm_pair), "row", across_pairs)
    edge_0, edge_1 = other_col(face_0), other_col(face_1)
    inner_1 = make_inner(near_1, outer_1, edge_1, after(gm, edge_0))
    beyond_1 = after(beyond_1, inner_1)
    given_1 = make_halo(near_1, beyond_1, edge_1, ends(beyond_1)[0], gm_pair)
    facing_0, across_0 = after(facing_0, given_1), after(across_0, given_1)
    halo_1 = lax.ppermute(after(given_1, facing_0, across_0), "row", in_pair)
    corner_0 = ends(across_0, facing_0)
    own_0 = make_panel(near_0, outer_0, facing_0, across_0, edge_0, corner_0, gm)
    ahead_0 = lax.ppermute(own_0, "row", ahead)
    halo_1 = after(halo_1, own_0)
    own_1 = join(inner_1, halo_1)
    pair_0 = lax.ppermute(after(own_0, halo_1), "row", in_pair)
    pair_1 = lax.ppermute(own_1, "row", in_pair)
    ahead_1 = lax.ppermute(own_1, "row", ahead)
    ahead_0 = after(ahead_0, own_1)
    behind_0 = lax.ppermute(after(own_0, ahead_0), "row", behind)
    rest_0 = lax.ppermute(ahead_0, "row", in_pair)
    pair_0 = after(pair_0, ahead_0)
    pair_1 = after(pair_1, pair_0)
    ahead_1 = after(ahead_1, pair_1)
    behind_1 = lax.ppermute(after(own_1, ahead_1), "row", behind)
    rest_1 = lax.ppermute(ahead_1, "row", in_pair)
    behind_0, rest_0 = after(behind_0, ahead_1), after(rest_0, ahead_1)
    sources_0 = both(own_0, ahead_0) + both(behind_0, pair_0) + both(rest_0)
    sources_1 = both(own_1, ahead_1) + both(pair_1) + both(behind_1, rest_1)
    out = make_tiles(0, windows, place_0, present, sources_0, None)
    return make_tiles(1, windows, place_1, present, sources_1, out)


def solution(mesh):
    in_specs = (P("subj", None, "row", "col", None), P(("row", "col")), P(("row", "col"), None))
    out_specs = P(("row", "col"), None, "subj", None, None)
    return jax.shard_map(
        on_device, mesh=mesh, in_specs=in_specs, out_specs=out_specs, check_vma=False
    )
```

```python
import functools
import math

import jax
import jax.numpy as jnp
from jax import lax
from jax.experimental import pallas as pl
from jax.experimental.pallas import tpu as pltpu
from jax.sharding import PartitionSpec as P

BLOCK = 128
SIDE = math.exp(-0.5) / (1.0 + 2.0 * math.exp(-0.5))
CENTRE = 1.0 / (1.0 + 2.0 * math.exp(-0.5))
SMALL = pl.CostEstimate(flops=1, bytes_accessed=1, transcendentals=0)
VMEM_BYTES = 20 * 1024 * 1024


def is_even():
    return lax.axis_index("row") % 2 == 0


def is_first():
    return lax.axis_index("col") == 0


def faces_kernel(bold_ref, *refs):
    windows, frames, slab_x, slab_y, slab_z = bold_ref.shape
    per_frame = slab_x * slab_y
    wide = refs[-1]
    for window in range(windows):
        near_ref, outer_ref, edge_ref = refs[3 * window : 3 * window + 3]
        wide[...] = bold_ref[window].reshape(frames * per_frame, slab_z).astype(jnp.float32)

        def plane(x, y):
            taken = wide[pl.ds(x * slab_y + y, frames, stride=per_frame), :]
            return taken.astype(jnp.bfloat16)

        def layers(first_ref, last_ref):
            for y in range(slab_y):
                first_ref[y] = plane(0, y)
                last_ref[y] = plane(1, y)

        pl.when(is_even())(functools.partial(layers, outer_ref, near_ref))
        pl.when(~is_even())(functools.partial(layers, near_ref, outer_ref))

        def edges(y):
            for x in range(slab_x):
                edge_ref[x] = plane(x, y)

        pl.when(is_first())(functools.partial(edges, slab_y - 1))
        pl.when(~is_first())(functools.partial(edges, 0))


def make_faces(bold):
    windows, frames, slab_x, slab_y, slab_z = bold.shape
    layer = jax.ShapeDtypeStruct((slab_y, frames, slab_z), jnp.bfloat16)
    edge = jax.ShapeDtypeStruct((slab_x, frames, slab_z), jnp.bfloat16)
    whole = lambda array: pl.BlockSpec(array.shape, lambda _: (0,) * len(array.shape))
    return pl.pallas_call(
        faces_kernel,
        grid=(1,),
        in_specs=[whole(bold)],
        out_specs=[whole(layer), whole(layer), whole(edge)] * windows,
        out_shape=[layer, layer, edge] * windows,
        scratch_shapes=[pltpu.VMEM((frames * slab_x * slab_y, slab_z), jnp.float32)],
        compiler_params=pltpu.CompilerParams(vmem_limit_bytes=VMEM_BYTES),
        cost_estimate=SMALL,
        name="faces",
    )(bold)


def three_taps(before, here, after):
    return SIDE * before + CENTRE * here + SIDE * after


def along_z(part):
    lane = lax.broadcasted_iota(jnp.int32, part.shape, 1)
    last = part.shape[1] - 1
    before = jnp.where(lane == 0, 0.0, pltpu.roll(part, 1, 1))
    after = jnp.where(lane == last, 0.0, pltpu.roll(part, last, 1))
    return three_taps(before, part, after)


def place_edge(planes, x, edge):
    planes[x, 0] = jnp.where(is_first(), 0.0, edge)
    planes[x, planes.shape[1] - 1] = jnp.where(is_first(), edge, 0.0)


def standardise(smooth):
    frames = smooth.shape[0]
    centred = smooth - jnp.mean(smooth, axis=0, keepdims=True)
    spread = jnp.mean(centred * centred, axis=0, keepdims=True)
    return (centred * lax.rsqrt((spread + 1e-05) * frames)).astype(jnp.bfloat16)


def pick(parts, gm_ref, out_ref):
    voxels = parts[0].shape[1]
    rows = gm_ref.shape[1]
    step = 2 * BLOCK
    for start in range(0, rows, step):
        wanted = gm_ref[:, start : start + step]
        voxel = lax.broadcasted_iota(jnp.int32, (voxels, step), 0)
        chosen = jnp.where(voxel == wanted, 1.0, 0.0).astype(jnp.bfloat16)
        total = jnp.dot(parts[0][...], chosen, preferred_element_type=jnp.float32)
        for part in parts[1:]:
            total += jnp.dot(part[...], chosen, preferred_element_type=jnp.float32)
        out_ref[:, start : start + step] = total.astype(out_ref.dtype)


def panel_kernel(
    near_ref, outer_ref, facing_ref, across_ref, edge_ref, corner_ref, gm_ref, out_ref,
    planes, scored,
):
    slab_y, frames, slab_z = near_ref.shape
    even = is_even()

    def along_x(across, outer, near, facing):
        layers = [part.astype(jnp.float32) for part in (across, outer, near, facing)]
        outer, near = three_taps(*layers[:3]), three_taps(*layers[1:])
        return jnp.where(even, outer, near), jnp.where(even, near, outer)

    for y in range(slab_y):
        planes[0, y + 1], planes[1, y + 1] = along_x(
            across_ref[y], outer_ref[y], near_ref[y], facing_ref[y]
        )
    outer = jnp.where(even, edge_ref[0], edge_ref[1])
    near = jnp.where(even, edge_ref[1], edge_ref[0])
    for x, edge in enumerate(along_x(corner_ref[0], outer, near, corner_ref[1])):
        place_edge(planes, x, edge)
    for x in range(2):
        for y in range(slab_y):
            part = three_taps(planes[x, y], planes[x, y + 1], planes[x, y + 2])
            start = (x * slab_y + y) * slab_z
            scored[:, start : start + slab_z] = standardise(along_z(part))
    pick([scored], gm_ref, out_ref)


def inner_kernel(
    near_ref, outer_ref, edge_ref, gm_ref, out_ref, planes, high, middle, low
):
    slab_y, frames, slab_z = near_ref.shape
    slab_x = edge_ref.shape[0]
    even = is_even()

    def two_taps(here, other):
        return CENTRE * here + SIDE * other

    for y in range(slab_y):
        near, outer = near_ref[y].astype(jnp.float32), outer_ref[y].astype(jnp.float32)
        first, last = jnp.where(even, outer, near), jnp.where(even, near, outer)
        planes[0, y + 1] = two_taps(first, last)
        planes[1, y + 1] = two_taps(last, first)
    edges = [edge_ref[x].astype(jnp.float32) for x in range(slab_x)]
    for x in range(slab_x):
        place_edge(planes, x, two_taps(edges[x], edges[1 - x]))
    for x in range(slab_x):
        for y in range(slab_y):
            part = along_z(three_taps(planes[x, y], planes[x, y + 1], planes[x, y + 2]))
            start = (x * slab_y + y) * slab_z
            for term in (high, middle, low):
                rounded = part.astype(jnp.bfloat16)
                term[:, start : start + slab_z] = rounded
                part = part - rounded.astype(jnp.float32)
    pick([high, middle, low], gm_ref, out_ref)


def halo_kernel(
    near_ref, beyond_ref, edge_ref, corner_ref, gm_ref, out_ref, planes, scored
):
    slab_y, frames, slab_z = near_ref.shape
    even = is_even()

    def sides(own, beyond):
        own, beyond = own.astype(jnp.float32), beyond.astype(jnp.float32)
        return jnp.where(even, own, beyond), jnp.where(even, beyond, own)

    for y in range(slab_y):
        planes[0, y + 1], planes[1, y + 1] = sides(near_ref[y], beyond_ref[y])
    own = jnp.where(even, edge_ref[1], edge_ref[0])
    for x, edge in enumerate(sides(own, corner_ref[...])):
        place_edge(planes, x, edge)
    for x in range(2):
        for y in range(slab_y):
            part = three_taps(planes[x, y], planes[x, y + 1], planes[x, y + 2])
            start = (x * slab_y + y) * slab_z
            scored[:, start : start + slab_z] = along_z(part).astype(jnp.bfloat16)
    pick([scored], gm_ref, out_ref)


def join_kernel(inner_ref, halo_ref, out_ref):
    for start in range(0, out_ref.shape[1], BLOCK):
        span = slice(start, start + BLOCK)
        smooth = inner_ref[:, span] + SIDE * halo_ref[:, span].astype(jnp.float32)
        out_ref[:, span] = standardise(smooth)


def call_on_rows(kernel, dtype, frames, operands, scratch, name):
    rows = operands[-1].shape[1]
    whole = lambda array: pl.BlockSpec(array.shape, lambda _: (0,) * array.ndim)
    return pl.pallas_call(
        kernel,
        grid=(1,),
        in_specs=[whole(value) for value in operands],
        out_specs=pl.BlockSpec((frames, rows), lambda _: (0, 0)),
        out_shape=jax.ShapeDtypeStruct((frames, rows), dtype),
        scratch_shapes=scratch,
        compiler_params=pltpu.CompilerParams(vmem_limit_bytes=VMEM_BYTES),
        cost_estimate=SMALL,
        name=name,
    )(*operands)


def blur_scratch(first, terms):
    slab_y, frames, slab_z = first.shape
    planes = pltpu.VMEM((2, slab_y + 2, frames, slab_z), jnp.float32)
    return [planes] + [pltpu.VMEM((frames, 2 * slab_y * slab_z), jnp.bfloat16)] * terms


def make_panel(near, outer, facing, across, edge, corner, gm):
    operands = (near, outer, facing, across, edge, corner, gm)
    scratch = blur_scratch(near, 1)
    return call_on_rows(
        panel_kernel, jnp.bfloat16, near.shape[1], operands, scratch, "blur_score_pick"
    )


def make_inner(near, outer, edge, gm):
    operands = (near, outer, edge, gm)
    scratch = blur_scratch(near, 3)
    return call_on_rows(
        inner_kernel, jnp.float32, near.shape[1], operands, scratch, "inner_blur"
    )


def make_halo(near, beyond, edge, corner, gm):
    operands = (near, beyond, edge, corner, gm)
    scratch = blur_scratch(near, 1)
    return call_on_rows(
        halo_kernel, jnp.bfloat16, near.shape[1], operands, scratch, "halo_blur"
    )


def join(inner, halo):
    return call_on_rows(
        join_kernel, jnp.bfloat16, inner.shape[0], (inner, halo), [], "join_score"
    )


def tiles_kernel(place_ref, present_ref, *refs, sources, window):
    parts = refs[:sources]
    out_ref, held, tiles, sems, out_sems = refs[-5:]
    blocks, slots = out_ref.shape[:2]

    loads = []
    first = 0
    for n, part in enumerate(parts):
        target = held.at[pl.ds(first, part.shape[0])]
        first += part.shape[0]
        loads.append(pltpu.make_async_copy(part, target, sems.at[n]))
        loads[-1].start()
    for load in loads:
        load.wait()

    def partner(block, slot):
        place = place_ref[block, slot]
        start = pl.multiple_of(lax.rem(place, blocks) * BLOCK, BLOCK)
        return held[lax.div(place, blocks), :, pl.ds(start, BLOCK)]

    stores = []
    for block in range(blocks):
        own = held[0, :, block * BLOCK : (block + 1) * BLOCK].T
        for slot in range(0, slots, 2):
            pair = jnp.concatenate([partner(block, slot), partner(block, slot + 1)], axis=1)
            both = jnp.dot(own, pair, preferred_element_type=jnp.float32)
            for n in range(2):
                tile = both[:, n * BLOCK : (n + 1) * BLOCK]
                tile = jnp.where(present_ref[block, slot + n] != 0, tile, 0.0)
                tiles[block, slot + n] = tile.astype(jnp.bfloat16)
        stores.append(
            pltpu.make_async_copy(tiles.at[block], out_ref.at[block, :, window], out_sems.at[block])
        )
        stores[-1].start()
    for store in stores:
        store.wait()


def make_tiles(window, windows, place, present, sources, earlier):
    frames, rows = sources[0].shape[1:]
    total = sum(source.shape[0] for source in sources)
    blocks = rows // BLOCK
    slots = place.shape[1]
    count = len(sources)
    anywhere = pl.BlockSpec(memory_space=pl.ANY)
    operands = list(sources) + ([] if earlier is None else [earlier])
    return pl.pallas_call(
        functools.partial(tiles_kernel, sources=count, window=window),
        grid_spec=pltpu.PrefetchScalarGridSpec(
            num_scalar_prefetch=2,
            grid=(1,),
            in_specs=[anywhere] * len(operands),
            out_specs=anywhere,
            scratch_shapes=[
                pltpu.VMEM((total, frames, rows), jnp.bfloat16),
                pltpu.VMEM((blocks, slots, BLOCK, BLOCK), jnp.bfloat16),
                pltpu.SemaphoreType.DMA((count,)),
                pltpu.SemaphoreType.DMA((blocks,)),
            ],
        ),
        out_shape=jax.ShapeDtypeStruct((blocks, slots, windows, BLOCK, BLOCK), jnp.bfloat16),
        input_output_aliases={} if earlier is None else {2 + count: 0},
        compiler_params=pltpu.CompilerParams(vmem_limit_bytes=VMEM_BYTES),
        cost_estimate=SMALL,
        name="tiles",
    )(place, present, *operands)


def after(value, *earlier):
    return lax.optimization_barrier((value,) + earlier)[0]


def on_device(bold, gm_index, partners):
    row_total = lax.axis_size("row")
    col_total = lax.axis_size("col")
    row = lax.axis_index("row")
    col = lax.axis_index("col")
    even = row % 2 == 0

    def other_col(value):
        return lax.ppermute(value, "col", [(0, 1), (1, 0)])

    ahead = [((i + 2 * (-1) ** i) % row_total, i) for i in range(row_total)]
    behind = [(i, source) for source, i in ahead]
    two_on = [(i, i + 2 * (-1) ** (i + 1)) for i in range(row_total)]
    two_on = [(i, target) for i, target in two_on if 0 <= target < row_total]
    across_pairs = [(i, i - (-1) ** i) for i in range(row_total)]
    across_pairs = [(i, target) for i, target in across_pairs if 0 <= target < row_total]
    in_pair = [(i, i ^ 1) for i in range(row_total)]

    gm = gm_index.reshape(1, -1)
    blocks, slots = partners.shape
    ids = jnp.maximum(partners, 0)
    slab = ids // blocks
    hop = (slab // col_total - row + 2 + row_total) % row_total
    kind = jnp.where((hop == 1) == even, 4, 3)
    kind = jnp.where(hop == 2, 0, jnp.where((hop == 0) | (hop >= 4), 2 - (even == (hop >= 4)), kind))
    away = (slab % col_total != col).astype(jnp.int32)
    within = ids % blocks
    present = partners >= 0
    parts_0 = jnp.where(kind == 4, 8 + away, kind // 2 * 4 + kind % 2 + 2 * away)
    alone = jnp.where(kind == 3, 4, jnp.where(kind == 4, 6, 8)) + away
    parts_1 = jnp.where(kind < 2, kind + 2 * away, alone)
    place_0, place_1 = (
        jnp.where(present, part * blocks + within, 0).astype(jnp.int32)
        for part in (parts_0, parts_1)
    )
    present = present.astype(jnp.int32)

    def both(*parts):
        near = jnp.stack(parts, 0)
        return [near, other_col(near)]

    windows = bold.shape[0]
    gm_pair = lax.ppermute(gm, "row", in_pair)

    def ends(*layers):
        return other_col(jnp.stack([jnp.where(col == 0, layer[-1], layer[0]) for layer in layers], 0))

    near_0, outer_0, face_0, near_1, outer_1, face_1 = make_faces(bold)
    beyond_1 = lax.ppermute(outer_1, "row", two_on)
    facing_0 = lax.ppermute(after(near_0, gm_pair), "row", in_pair)
    across_0 = lax.ppermute(after(outer_0, gm_pair), "row", across_pairs)
    edge_0, edge_1 = other_col(face_0), other_col(face_1)
    inner_1 = make_inner(near_1, outer_1, edge_1, after(gm, edge_0))
    beyond_1 = after(beyond_1, inner_1)
    given_1 = make_halo(near_1, beyond_1, edge_1, ends(beyond_1)[0], gm_pair)
    facing_0, across_0 = after(facing_0, given_1), after(across_0, given_1)
    halo_1 = lax.ppermute(after(given_1, facing_0, across_0), "row", in_pair)
    corner_0 = ends(across_0, facing_0)
    own_0 = make_panel(near_0, outer_0, facing_0, across_0, edge_0, corner_0, gm)
    ahead_0 = lax.ppermute(own_0, "row", ahead)
    halo_1 = after(halo_1, own_0)
    own_1 = join(inner_1, halo_1)
    pair_0 = lax.ppermute(after(own_0, halo_1), "row", in_pair)
    pair_1 = lax.ppermute(own_1, "row", in_pair)
    ahead_1 = lax.ppermute(own_1, "row", ahead)
    ahead_0 = after(ahead_0, own_1)
    behind_0 = lax.ppermute(after(own_0, ahead_0), "row", behind)
    rest_0 = lax.ppermute(ahead_0, "row", in_pair)
    pair_0 = after(pair_0, ahead_0)
    pair_1 = after(pair_1, pair_0)
    ahead_1 = after(ahead_1, pair_1)
    rest_0 = after(rest_0, ahead_1)
    behind_0 = after(behind_0, rest_0)
    rest_1 = lax.ppermute(after(ahead_1, rest_0), "row", in_pair)
    behind_1 = lax.ppermute(after(own_1, rest_0), "row", behind)
    sources_0 = both(own_0, ahead_0) + both(behind_0, pair_0) + both(rest_0)
    out = make_tiles(0, windows, place_0, present, sources_0, None)
    rest_1, behind_1 = after(rest_1, out), after(behind_1, out)
    sources_1 = both(own_1, ahead_1) + both(pair_1) + both(rest_1) + both(behind_1)
    return make_tiles(1, windows, place_1, present, sources_1, out)


def solution(mesh):
    in_specs = (P("subj", None, "row", "col", None), P(("row", "col")), P(("row", "col"), None))
    out_specs = P(("row", "col"), None, "subj", None, None)
    return jax.shard_map(
        on_device, mesh=mesh, in_specs=in_specs, out_specs=out_specs, check_vma=False
    )
```

```python
import functools
import math

import jax
import jax.numpy as jnp
from jax import lax
from jax.experimental import pallas as pl
from jax.experimental.pallas import tpu as pltpu
from jax.sharding import PartitionSpec as P

BLOCK = 128
SIDE = math.exp(-0.5) / (1.0 + 2.0 * math.exp(-0.5))
CENTRE = 1.0 / (1.0 + 2.0 * math.exp(-0.5))
SMALL = pl.CostEstimate(flops=1, bytes_accessed=1, transcendentals=0)
VMEM_BYTES = 20 * 1024 * 1024


def is_even():
    return lax.axis_index("row") % 2 == 0


def is_first():
    return lax.axis_index("col") == 0


def plane_of(layer, y, frames):
    return layer[y] if len(layer.shape) == 3 else layer[y * frames : (y + 1) * frames]


def faces_kernel(bold_ref, gm_ref, *refs):
    windows, frames, slab_x, slab_y, slab_z = bold_ref.shape
    per_frame = slab_x * slab_y
    wide = refs[-1]
    for window in range(windows):
        near_ref, outer_ref, edge_ref = refs[3 * window : 3 * window + 3]
        wide[...] = bold_ref[window].reshape(frames * per_frame, slab_z).astype(jnp.float32)

        def plane(x, y):
            taken = wide[pl.ds(x * slab_y + y, frames, stride=per_frame), :]
            return taken.astype(jnp.bfloat16)

        def store(layer_ref, y, value):
            if len(layer_ref.shape) == 3:
                layer_ref[y] = value
            else:
                layer_ref[y * frames : (y + 1) * frames] = value

        def layers(first_ref, last_ref):
            for y in range(slab_y):
                store(first_ref, y, plane(0, y))
                store(last_ref, y, plane(1, y))

        pl.when(is_even())(functools.partial(layers, outer_ref, near_ref))
        pl.when(~is_even())(functools.partial(layers, near_ref, outer_ref))

        def edges(y):
            for x in range(slab_x):
                edge_ref[x] = plane(x, y)

        if len(near_ref.shape) == 2:
            number = gm_ref[...] + 1
            parts = jnp.concatenate([lax.shift_right_logical(number, 6), number & 63], axis=0)
            near_ref[slab_y * frames :] = parts.astype(jnp.float32).astype(jnp.bfloat16)

        pl.when(is_first())(functools.partial(edges, slab_y - 1))
        pl.when(~is_first())(functools.partial(edges, 0))


def make_faces(bold, gm):
    windows, frames, slab_x, slab_y, slab_z = bold.shape
    layer = jax.ShapeDtypeStruct((slab_y, frames, slab_z), jnp.bfloat16)
    edge = jax.ShapeDtypeStruct((slab_x, frames, slab_z), jnp.bfloat16)
    with_gm = jax.ShapeDtypeStruct(
        (slab_y * frames + 2 * gm.shape[0], slab_z), jnp.bfloat16
    )
    outs = [with_gm, layer, edge] + [layer, layer, edge] * (windows - 1)
    whole = lambda array: pl.BlockSpec(array.shape, lambda _: (0,) * len(array.shape))
    return pl.pallas_call(
        faces_kernel,
        grid=(1,),
        in_specs=[whole(bold), whole(gm)],
        out_specs=[whole(value) for value in outs],
        out_shape=outs,
        scratch_shapes=[pltpu.VMEM((frames * slab_x * slab_y, slab_z), jnp.float32)],
        compiler_params=pltpu.CompilerParams(vmem_limit_bytes=VMEM_BYTES),
        cost_estimate=SMALL,
        name="faces",
    )(bold, gm)


def three_taps(before, here, after):
    return SIDE * before + CENTRE * here + SIDE * after


def along_z(part):
    lane = lax.broadcasted_iota(jnp.int32, part.shape, 1)
    last = part.shape[1] - 1
    before = jnp.where(lane == 0, 0.0, pltpu.roll(part, 1, 1))
    after = jnp.where(lane == last, 0.0, pltpu.roll(part, last, 1))
    return three_taps(before, part, after)


def place_edge(planes, x, edge):
    planes[x, 0] = jnp.where(is_first(), 0.0, edge)
    planes[x, planes.shape[1] - 1] = jnp.where(is_first(), edge, 0.0)


def standardise(smooth):
    frames = smooth.shape[0]
    centred = smooth - jnp.mean(smooth, axis=0, keepdims=True)
    spread = jnp.mean(centred * centred, axis=0, keepdims=True)
    return (centred * lax.rsqrt((spread + 1e-05) * frames)).astype(jnp.bfloat16)


def pick(parts, gm, out_ref):
    voxels = parts[0].shape[1]
    for line in range(0, gm.shape[0], 2):
        wanted = jnp.concatenate([gm[line : line + 1], gm[line + 1 : line + 2]], axis=1)
        voxel = lax.broadcasted_iota(jnp.int32, (voxels, 2 * BLOCK), 0)
        chosen = jnp.where(voxel == wanted, 1.0, 0.0).astype(jnp.bfloat16)
        total = jnp.dot(parts[0][...], chosen, preferred_element_type=jnp.float32)
        for part in parts[1:]:
            total += jnp.dot(part[...], chosen, preferred_element_type=jnp.float32)
        start = line * BLOCK
        out_ref[:, start : start + 2 * BLOCK] = total.astype(out_ref.dtype)


def panel_kernel(
    near_ref, outer_ref, facing_ref, across_ref, edge_ref, corner_ref, gm_ref, out_ref,
    planes, scored,
):
    slab_y, frames, slab_z = outer_ref.shape
    even = is_even()

    def along_x(across, outer, near, facing):
        layers = [part.astype(jnp.float32) for part in (across, outer, near, facing)]
        outer, near = three_taps(*layers[:3]), three_taps(*layers[1:])
        return jnp.where(even, outer, near), jnp.where(even, near, outer)

    for y in range(slab_y):
        planes[0, y + 1], planes[1, y + 1] = along_x(
            across_ref[y],
            outer_ref[y],
            plane_of(near_ref, y, frames),
            plane_of(facing_ref, y, frames),
        )
    outer = jnp.where(even, edge_ref[0], edge_ref[1])
    near = jnp.where(even, edge_ref[1], edge_ref[0])
    for x, edge in enumerate(along_x(corner_ref[0], outer, near, corner_ref[1])):
        place_edge(planes, x, edge)
    for x in range(2):
        for y in range(slab_y):
            part = three_taps(planes[x, y], planes[x, y + 1], planes[x, y + 2])
            start = (x * slab_y + y) * slab_z
            scored[:, start : start + slab_z] = standardise(along_z(part))
    pick([scored], gm_ref[...], out_ref)


def inner_kernel(
    near_ref, outer_ref, edge_ref, gm_ref, out_ref, planes, high, middle, low
):
    slab_y, frames, slab_z = near_ref.shape
    slab_x = edge_ref.shape[0]
    even = is_even()

    def two_taps(here, other):
        return CENTRE * here + SIDE * other

    for y in range(slab_y):
        near, outer = near_ref[y].astype(jnp.float32), outer_ref[y].astype(jnp.float32)
        first, last = jnp.where(even, outer, near), jnp.where(even, near, outer)
        planes[0, y + 1] = two_taps(first, last)
        planes[1, y + 1] = two_taps(last, first)
    edges = [edge_ref[x].astype(jnp.float32) for x in range(slab_x)]
    for x in range(slab_x):
        place_edge(planes, x, two_taps(edges[x], edges[1 - x]))
    for x in range(slab_x):
        for y in range(slab_y):
            part = along_z(three_taps(planes[x, y], planes[x, y + 1], planes[x, y + 2]))
            start = (x * slab_y + y) * slab_z
            for term in (high, middle, low):
                rounded = part.astype(jnp.bfloat16)
                term[:, start : start + slab_z] = rounded
                part = part - rounded.astype(jnp.float32)
    pick([high, middle, low], gm_ref[...], out_ref)


def halo_kernel(
    near_ref, beyond_ref, edge_ref, corner_ref, gm_ref, out_ref, planes, scored
):
    slab_y, frames, slab_z = near_ref.shape
    even = is_even()

    def sides(own, beyond):
        own, beyond = own.astype(jnp.float32), beyond.astype(jnp.float32)
        return jnp.where(even, own, beyond), jnp.where(even, beyond, own)

    for y in range(slab_y):
        planes[0, y + 1], planes[1, y + 1] = sides(near_ref[y], beyond_ref[y])
    own = jnp.where(even, edge_ref[1], edge_ref[0])
    for x, edge in enumerate(sides(own, corner_ref[2])):
        place_edge(planes, x, edge)
    for x in range(2):
        for y in range(slab_y):
            part = three_taps(planes[x, y], planes[x, y + 1], planes[x, y + 2])
            start = (x * slab_y + y) * slab_z
            scored[:, start : start + slab_z] = along_z(part).astype(jnp.bfloat16)
    lines = gm_ref.shape[0] // 2
    number = gm_ref[...].astype(jnp.float32).astype(jnp.int32)
    pick([scored], number[:lines] * 64 + number[lines:] - 1, out_ref)


def join_kernel(inner_ref, halo_ref, out_ref):
    for start in range(0, out_ref.shape[1], BLOCK):
        span = slice(start, start + BLOCK)
        smooth = inner_ref[:, span] + SIDE * halo_ref[:, span].astype(jnp.float32)
        out_ref[:, span] = standardise(smooth)


def call_on_rows(kernel, dtype, frames, rows, operands, scratch, name):
    whole = lambda array: pl.BlockSpec(array.shape, lambda _: (0,) * array.ndim)
    return pl.pallas_call(
        kernel,
        grid=(1,),
        in_specs=[whole(value) for value in operands],
        out_specs=pl.BlockSpec((frames, rows), lambda _: (0, 0)),
        out_shape=jax.ShapeDtypeStruct((frames, rows), dtype),
        scratch_shapes=scratch,
        compiler_params=pltpu.CompilerParams(vmem_limit_bytes=VMEM_BYTES),
        cost_estimate=SMALL,
        name=name,
    )(*operands)


def blur_scratch(first, terms):
    slab_y, frames, slab_z = first.shape
    planes = pltpu.VMEM((2, slab_y + 2, frames, slab_z), jnp.float32)
    return [planes] + [pltpu.VMEM((frames, 2 * slab_y * slab_z), jnp.bfloat16)] * terms


def make_panel(near, outer, facing, across, edge, corner, gm):
    operands = (near, outer, facing, across, edge, corner, gm)
    scratch = blur_scratch(outer, 1)
    return call_on_rows(
        panel_kernel, jnp.bfloat16, outer.shape[1], gm.size, operands, scratch, "blur_score_pick"
    )


def make_inner(near, outer, edge, gm):
    operands = (near, outer, edge, gm)
    scratch = blur_scratch(near, 3)
    return call_on_rows(
        inner_kernel, jnp.float32, near.shape[1], gm.size, operands, scratch, "inner_blur"
    )


def make_halo(near, beyond, edge, corner, gm):
    operands = (near, beyond, edge, corner, gm)
    scratch = blur_scratch(near, 1)
    return call_on_rows(
        halo_kernel, jnp.bfloat16, near.shape[1], gm.size // 2, operands, scratch, "halo_blur"
    )


def join(inner, halo):
    return call_on_rows(
        join_kernel, jnp.bfloat16, *inner.shape, (inner, halo), [], "join_score"
    )


def tiles_kernel(place_ref, present_ref, *refs, sources, window):
    parts = refs[:sources]
    out_ref, held, tiles, sems, out_sems = refs[-5:]
    blocks, slots = out_ref.shape[:2]

    loads = []
    first = 0
    for n, part in enumerate(parts):
        target = held.at[pl.ds(first, part.shape[0])]
        first += part.shape[0]
        loads.append(pltpu.make_async_copy(part, target, sems.at[n]))
        loads[-1].start()
    for load in loads:
        load.wait()

    def partner(block, slot):
        place = place_ref[block, slot]
        start = pl.multiple_of(lax.rem(place, blocks) * BLOCK, BLOCK)
        return held[lax.div(place, blocks), :, pl.ds(start, BLOCK)]

    stores = []
    for block in range(blocks):
        own = held[0, :, block * BLOCK : (block + 1) * BLOCK].T
        for slot in range(0, slots, 2):
            pair = jnp.concatenate([partner(block, slot), partner(block, slot + 1)], axis=1)
            both = jnp.dot(own, pair, preferred_element_type=jnp.float32)
            for n in range(2):
                tile = both[:, n * BLOCK : (n + 1) * BLOCK]
                tile = jnp.where(present_ref[block, slot + n] != 0, tile, 0.0)
                tiles[block, slot + n] = tile.astype(jnp.bfloat16)
        stores.append(
            pltpu.make_async_copy(tiles.at[block], out_ref.at[block, :, window], out_sems.at[block])
        )
        stores[-1].start()
    for store in stores:
        store.wait()


def make_tiles(window, windows, place, present, sources, earlier):
    frames, rows = sources[0].shape[1:]
    total = sum(source.shape[0] for source in sources)
    blocks = rows // BLOCK
    slots = place.shape[1]
    count = len(sources)
    anywhere = pl.BlockSpec(memory_space=pl.ANY)
    operands = list(sources) + ([] if earlier is None else [earlier])
    return pl.pallas_call(
        functools.partial(tiles_kernel, sources=count, window=window),
        grid_spec=pltpu.PrefetchScalarGridSpec(
            num_scalar_prefetch=2,
            grid=(1,),
            in_specs=[anywhere] * len(operands),
            out_specs=anywhere,
            scratch_shapes=[
                pltpu.VMEM((total, frames, rows), jnp.bfloat16),
                pltpu.VMEM((blocks, slots, BLOCK, BLOCK), jnp.bfloat16),
                pltpu.SemaphoreType.DMA((count,)),
                pltpu.SemaphoreType.DMA((blocks,)),
            ],
        ),
        out_shape=jax.ShapeDtypeStruct((blocks, slots, windows, BLOCK, BLOCK), jnp.bfloat16),
        input_output_aliases={} if earlier is None else {2 + count: 0},
        compiler_params=pltpu.CompilerParams(vmem_limit_bytes=VMEM_BYTES),
        cost_estimate=SMALL,
        name="tiles",
    )(place, present, *operands)


def after(value, *earlier):
    return lax.optimization_barrier((value,) + earlier)[0]


def on_device(bold, gm_index, partners):
    row_total = lax.axis_size("row")
    col_total = lax.axis_size("col")
    row = lax.axis_index("row")
    col = lax.axis_index("col")
    even = row % 2 == 0

    def other_col(value):
        return lax.ppermute(value, "col", [(0, 1), (1, 0)])

    ahead = [((i + 2 * (-1) ** i) % row_total, i) for i in range(row_total)]
    behind = [(i, source) for source, i in ahead]
    two_on = [(i, i + 2 * (-1) ** (i + 1)) for i in range(row_total)]
    two_on = [(i, target) for i, target in two_on if 0 <= target < row_total]
    across_pairs = [(i, i - (-1) ** i) for i in range(row_total)]
    across_pairs = [(i, target) for i, target in across_pairs if 0 <= target < row_total]
    in_pair = [(i, i ^ 1) for i in range(row_total)]

    gm = gm_index.reshape(-1, BLOCK)
    blocks, slots = partners.shape
    ids = jnp.maximum(partners, 0)
    slab = ids // blocks
    hop = (slab // col_total - row + 2 + row_total) % row_total
    kind = jnp.where((hop == 1) == even, 4, 3)
    kind = jnp.where(hop == 2, 0, jnp.where((hop == 0) | (hop >= 4), 2 - (even == (hop >= 4)), kind))
    away = (slab % col_total != col).astype(jnp.int32)
    within = ids % blocks
    present = partners >= 0
    parts_0 = jnp.where(kind == 4, 8 + away, kind // 2 * 4 + kind % 2 + 2 * away)
    alone = jnp.where(kind == 3, 4, jnp.where(kind == 4, 6, 8)) + away
    parts_1 = jnp.where(kind < 2, kind + 2 * away, alone)
    place_0, place_1 = (
        jnp.where(present, part * blocks + within, 0).astype(jnp.int32)
        for part in (parts_0, parts_1)
    )
    present = present.astype(jnp.int32)

    def both(*parts):
        near = jnp.stack(parts, 0)
        return [near, other_col(near)]

    windows = bold.shape[0]
    frames, slab_y = bold.shape[1], bold.shape[3]

    def ends(*layers):
        planes = [
            jnp.where(col == 0, plane_of(layer, slab_y - 1, frames), plane_of(layer, 0, frames))
            for layer in layers
        ]
        return other_col(jnp.stack(planes, 0))

    near_0, outer_0, face_0, near_1, outer_1, face_1 = make_faces(bold, gm)
    facing_0 = lax.ppermute(near_0, "row", in_pair)
    across_0 = lax.ppermute(outer_0, "row", across_pairs)
    beyond_1 = lax.ppermute(outer_1, "row", two_on)
    edge_0, edge_1 = other_col(face_0), other_col(face_1)
    inner_1 = make_inner(near_1, outer_1, edge_1, after(gm, edge_0))
    facing_0, across_0 = after(facing_0, inner_1), after(across_0, inner_1)
    beyond_1 = after(beyond_1, facing_0, across_0)
    gm_pair = facing_0[slab_y * frames :]
    corner = ends(across_0, facing_0, beyond_1)
    given_1 = make_halo(near_1, beyond_1, edge_1, corner, gm_pair)
    halo_1 = lax.ppermute(given_1, "row", in_pair)
    corner = after(corner, given_1)
    own_0 = make_panel(near_0, outer_0, facing_0, across_0, edge_0, corner, gm)
    ahead_0 = lax.ppermute(own_0, "row", ahead)
    halo_1 = after(halo_1, own_0)
    own_1 = join(inner_1, halo_1)
    pair_0 = lax.ppermute(after(own_0, halo_1), "row", in_pair)
    pair_1 = lax.ppermute(own_1, "row", in_pair)
    ahead_1 = lax.ppermute(own_1, "row", ahead)
    ahead_0 = after(ahead_0, own_1)
    behind_0 = lax.ppermute(after(own_0, ahead_0), "row", behind)
    rest_0 = lax.ppermute(ahead_0, "row", in_pair)
    pair_0 = after(pair_0, ahead_0)
    pair_1 = after(pair_1, pair_0)
    ahead_1 = after(ahead_1, pair_1)
    rest_0 = after(rest_0, ahead_1)
    behind_0 = after(behind_0, rest_0)
    rest_1 = lax.ppermute(after(ahead_1, rest_0), "row", in_pair)
    behind_1 = lax.ppermute(after(own_1, rest_0), "row", behind)
    sources_0 = both(own_0, ahead_0) + both(behind_0, pair_0) + both(rest_0)
    out = make_tiles(0, windows, place_0, present, sources_0, None)
    rest_1, behind_1 = after(rest_1, out), after(behind_1, out)
    sources_1 = both(own_1, ahead_1) + both(pair_1) + both(rest_1) + both(behind_1)
    return make_tiles(1, windows, place_1, present, sources_1, out)


def solution(mesh):
    in_specs = (P("subj", None, "row", "col", None), P(("row", "col")), P(("row", "col"), None))
    out_specs = P(("row", "col"), None, "subj", None, None)
    return jax.shard_map(
        on_device, mesh=mesh, in_specs=in_specs, out_specs=out_specs, check_vma=False
    )
```

```python
import functools
import math

import jax
import jax.numpy as jnp
from jax import lax
from jax.experimental import pallas as pl
from jax.experimental.pallas import tpu as pltpu
from jax.sharding import PartitionSpec as P

BLOCK = 128
SIDE = math.exp(-0.5) / (1.0 + 2.0 * math.exp(-0.5))
CENTRE = 1.0 / (1.0 + 2.0 * math.exp(-0.5))
SMALL = pl.CostEstimate(flops=1, bytes_accessed=1, transcendentals=0)
VMEM_BYTES = 20 * 1024 * 1024


def is_even():
    return lax.axis_index("row") % 2 == 0


def is_first():
    return lax.axis_index("col") == 0


def plane_of(layer, y, frames):
    return layer[y] if len(layer.shape) == 3 else layer[y * frames : (y + 1) * frames]


def faces_kernel(bold_ref, gm_ref, *refs):
    windows, frames, slab_x, slab_y, slab_z = bold_ref.shape
    per_frame = slab_x * slab_y
    wide = refs[-1]
    for window in range(windows):
        near_ref, outer_ref, edge_ref = refs[3 * window : 3 * window + 3]
        wide[...] = bold_ref[window].reshape(frames * per_frame, slab_z).astype(jnp.float32)

        def plane(x, y):
            taken = wide[pl.ds(x * slab_y + y, frames, stride=per_frame), :]
            return taken.astype(jnp.bfloat16)

        def store(layer_ref, y, value):
            if len(layer_ref.shape) == 3:
                layer_ref[y] = value
            else:
                layer_ref[y * frames : (y + 1) * frames] = value

        def layers(first_ref, last_ref):
            for y in range(slab_y):
                store(first_ref, y, plane(0, y))
                store(last_ref, y, plane(1, y))

        pl.when(is_even())(functools.partial(layers, outer_ref, near_ref))
        pl.when(~is_even())(functools.partial(layers, near_ref, outer_ref))

        def edges(y):
            for x in range(slab_x):
                edge_ref[x] = plane(x, y)

        if len(near_ref.shape) == 2:
            number = gm_ref[...] + 1
            parts = jnp.concatenate([lax.shift_right_logical(number, 6), number & 63], axis=0)
            near_ref[slab_y * frames :] = parts.astype(jnp.float32).astype(jnp.bfloat16)

        pl.when(is_first())(functools.partial(edges, slab_y - 1))
        pl.when(~is_first())(functools.partial(edges, 0))


def make_faces(bold, gm):
    windows, frames, slab_x, slab_y, slab_z = bold.shape
    layer = jax.ShapeDtypeStruct((slab_y, frames, slab_z), jnp.bfloat16)
    edge = jax.ShapeDtypeStruct((slab_x, frames, slab_z), jnp.bfloat16)
    with_gm = jax.ShapeDtypeStruct(
        (slab_y * frames + 2 * gm.shape[0], slab_z), jnp.bfloat16
    )
    outs = [with_gm, layer, edge] + [layer, layer, edge] * (windows - 1)
    whole = lambda array: pl.BlockSpec(array.shape, lambda _: (0,) * len(array.shape))
    return pl.pallas_call(
        faces_kernel,
        grid=(1,),
        in_specs=[whole(bold), whole(gm)],
        out_specs=[whole(value) for value in outs],
        out_shape=outs,
        scratch_shapes=[pltpu.VMEM((frames * slab_x * slab_y, slab_z), jnp.float32)],
        compiler_params=pltpu.CompilerParams(vmem_limit_bytes=VMEM_BYTES),
        cost_estimate=SMALL,
        name="faces",
    )(bold, gm)


def three_taps(before, here, after):
    return SIDE * before + CENTRE * here + SIDE * after


def along_z(part):
    lane = lax.broadcasted_iota(jnp.int32, part.shape, 1)
    last = part.shape[1] - 1
    before = jnp.where(lane == 0, 0.0, pltpu.roll(part, 1, 1))
    after = jnp.where(lane == last, 0.0, pltpu.roll(part, last, 1))
    return three_taps(before, part, after)


def place_edge(planes, x, edge):
    planes[x, 0] = jnp.where(is_first(), 0.0, edge)
    planes[x, planes.shape[1] - 1] = jnp.where(is_first(), edge, 0.0)


def standardise(smooth):
    frames = smooth.shape[0]
    centred = smooth - jnp.mean(smooth, axis=0, keepdims=True)
    spread = jnp.mean(centred * centred, axis=0, keepdims=True)
    return (centred * lax.rsqrt((spread + 1e-05) * frames)).astype(jnp.bfloat16)


def pick(parts, gm, out_ref):
    voxels = parts[0].shape[1]
    for line in range(0, gm.shape[0], 2):
        wanted = jnp.concatenate([gm[line : line + 1], gm[line + 1 : line + 2]], axis=1)
        voxel = lax.broadcasted_iota(jnp.int32, (voxels, 2 * BLOCK), 0)
        chosen = jnp.where(voxel == wanted, 1.0, 0.0).astype(jnp.bfloat16)
        total = jnp.dot(parts[0][...], chosen, preferred_element_type=jnp.float32)
        for part in parts[1:]:
            total += jnp.dot(part[...], chosen, preferred_element_type=jnp.float32)
        start = line * BLOCK
        out_ref[:, start : start + 2 * BLOCK] = total.astype(out_ref.dtype)


def panel_kernel(
    near_ref, outer_ref, facing_ref, across_ref, edge_ref, corner_ref, gm_ref, out_ref,
    planes, scored,
):
    slab_y, frames, slab_z = outer_ref.shape
    even = is_even()

    def along_x(across, outer, near, facing):
        layers = [part.astype(jnp.float32) for part in (across, outer, near, facing)]
        outer, near = three_taps(*layers[:3]), three_taps(*layers[1:])
        return jnp.where(even, outer, near), jnp.where(even, near, outer)

    for y in range(slab_y):
        planes[0, y + 1], planes[1, y + 1] = along_x(
            across_ref[y],
            outer_ref[y],
            plane_of(near_ref, y, frames),
            plane_of(facing_ref, y, frames),
        )
    outer = jnp.where(even, edge_ref[0], edge_ref[1])
    near = jnp.where(even, edge_ref[1], edge_ref[0])
    for x, edge in enumerate(along_x(corner_ref[0], outer, near, corner_ref[1])):
        place_edge(planes, x, edge)
    for x in range(2):
        for y in range(slab_y):
            part = three_taps(planes[x, y], planes[x, y + 1], planes[x, y + 2])
            start = (x * slab_y + y) * slab_z
            scored[:, start : start + slab_z] = standardise(along_z(part))
    pick([scored], gm_ref[...], out_ref)


def inner_kernel(
    near_ref, outer_ref, edge_ref, gm_ref, out_ref, planes, high, middle, low
):
    slab_y, frames, slab_z = near_ref.shape
    slab_x = edge_ref.shape[0]
    even = is_even()

    def two_taps(here, other):
        return CENTRE * here + SIDE * other

    for y in range(slab_y):
        near, outer = near_ref[y].astype(jnp.float32), outer_ref[y].astype(jnp.float32)
        first, last = jnp.where(even, outer, near), jnp.where(even, near, outer)
        planes[0, y + 1] = two_taps(first, last)
        planes[1, y + 1] = two_taps(last, first)
    edges = [edge_ref[x].astype(jnp.float32) for x in range(slab_x)]
    for x in range(slab_x):
        place_edge(planes, x, two_taps(edges[x], edges[1 - x]))
    for x in range(slab_x):
        for y in range(slab_y):
            part = along_z(three_taps(planes[x, y], planes[x, y + 1], planes[x, y + 2]))
            start = (x * slab_y + y) * slab_z
            for term in (high, middle, low):
                rounded = part.astype(jnp.bfloat16)
                term[:, start : start + slab_z] = rounded
                part = part - rounded.astype(jnp.float32)
    pick([high, middle, low], gm_ref[...], out_ref)


def halo_kernel(
    near_ref, beyond_ref, edge_ref, corner_ref, gm_ref, out_ref, planes, scored
):
    slab_y, frames, slab_z = near_ref.shape
    even = is_even()

    def sides(own, beyond):
        own, beyond = own.astype(jnp.float32), beyond.astype(jnp.float32)
        return jnp.where(even, own, beyond), jnp.where(even, beyond, own)

    for y in range(slab_y):
        planes[0, y + 1], planes[1, y + 1] = sides(near_ref[y], beyond_ref[y])
    own = jnp.where(even, edge_ref[1], edge_ref[0])
    for x, edge in enumerate(sides(own, corner_ref[2])):
        place_edge(planes, x, edge)
    for x in range(2):
        for y in range(slab_y):
            part = three_taps(planes[x, y], planes[x, y + 1], planes[x, y + 2])
            start = (x * slab_y + y) * slab_z
            scored[:, start : start + slab_z] = along_z(part).astype(jnp.bfloat16)
    lines = gm_ref.shape[0] // 2
    number = gm_ref[...].astype(jnp.float32).astype(jnp.int32)
    pick([scored], number[:lines] * 64 + number[lines:] - 1, out_ref)


def join_kernel(inner_ref, halo_ref, out_ref):
    for start in range(0, out_ref.shape[1], BLOCK):
        span = slice(start, start + BLOCK)
        smooth = inner_ref[:, span] + SIDE * halo_ref[:, span].astype(jnp.float32)
        out_ref[:, span] = standardise(smooth)


def call_on_rows(kernel, dtype, frames, rows, operands, scratch, name):
    whole = lambda array: pl.BlockSpec(array.shape, lambda _: (0,) * array.ndim)
    return pl.pallas_call(
        kernel,
        grid=(1,),
        in_specs=[whole(value) for value in operands],
        out_specs=pl.BlockSpec((frames, rows), lambda _: (0, 0)),
        out_shape=jax.ShapeDtypeStruct((frames, rows), dtype),
        scratch_shapes=scratch,
        compiler_params=pltpu.CompilerParams(vmem_limit_bytes=VMEM_BYTES),
        cost_estimate=SMALL,
        name=name,
    )(*operands)


def blur_scratch(first, terms):
    slab_y, frames, slab_z = first.shape
    planes = pltpu.VMEM((2, slab_y + 2, frames, slab_z), jnp.float32)
    return [planes] + [pltpu.VMEM((frames, 2 * slab_y * slab_z), jnp.bfloat16)] * terms


def make_panel(near, outer, facing, across, edge, corner, gm):
    operands = (near, outer, facing, across, edge, corner, gm)
    scratch = blur_scratch(outer, 1)
    return call_on_rows(
        panel_kernel, jnp.bfloat16, outer.shape[1], gm.size, operands, scratch, "blur_score_pick"
    )


def make_inner(near, outer, edge, gm):
    operands = (near, outer, edge, gm)
    scratch = blur_scratch(near, 3)
    return call_on_rows(
        inner_kernel, jnp.float32, near.shape[1], gm.size, operands, scratch, "inner_blur"
    )


def make_halo(near, beyond, edge, corner, gm):
    operands = (near, beyond, edge, corner, gm)
    scratch = blur_scratch(near, 1)
    return call_on_rows(
        halo_kernel, jnp.bfloat16, near.shape[1], gm.size // 2, operands, scratch, "halo_blur"
    )


def join(inner, halo):
    return call_on_rows(
        join_kernel, jnp.bfloat16, *inner.shape, (inner, halo), [], "join_score"
    )


def tiles_kernel(place_ref, present_ref, *refs, sources, window):
    parts = refs[:sources]
    out_ref, held, tiles, sems, out_sems = refs[-5:]
    blocks, slots = out_ref.shape[:2]

    loads = []
    first = 0
    for n, part in enumerate(parts):
        target = held.at[pl.ds(first, part.shape[0])]
        first += part.shape[0]
        loads.append(pltpu.make_async_copy(part, target, sems.at[n]))
        loads[-1].start()
    for load in loads:
        load.wait()

    def partner(block, slot):
        place = place_ref[block, slot]
        start = pl.multiple_of(lax.rem(place, blocks) * BLOCK, BLOCK)
        return held[lax.div(place, blocks), :, pl.ds(start, BLOCK)]

    stores = []
    for block in range(blocks):
        own = held[0, :, block * BLOCK : (block + 1) * BLOCK].T
        for slot in range(0, slots, 2):
            pair = jnp.concatenate([partner(block, slot), partner(block, slot + 1)], axis=1)
            both = jnp.dot(own, pair, preferred_element_type=jnp.float32)
            for n in range(2):
                tile = both[:, n * BLOCK : (n + 1) * BLOCK]
                tile = jnp.where(present_ref[block, slot + n] != 0, tile, 0.0)
                tiles[block, slot + n] = tile.astype(jnp.bfloat16)
        stores.append(
            pltpu.make_async_copy(tiles.at[block], out_ref.at[block, :, window], out_sems.at[block])
        )
        stores[-1].start()
    for store in stores:
        store.wait()


def make_tiles(window, windows, place, present, sources, earlier):
    frames, rows = sources[0].shape[1:]
    total = sum(source.shape[0] for source in sources)
    blocks = rows // BLOCK
    slots = place.shape[1]
    count = len(sources)
    anywhere = pl.BlockSpec(memory_space=pl.ANY)
    operands = list(sources) + ([] if earlier is None else [earlier])
    return pl.pallas_call(
        functools.partial(tiles_kernel, sources=count, window=window),
        grid_spec=pltpu.PrefetchScalarGridSpec(
            num_scalar_prefetch=2,
            grid=(1,),
            in_specs=[anywhere] * len(operands),
            out_specs=anywhere,
            scratch_shapes=[
                pltpu.VMEM((total, frames, rows), jnp.bfloat16),
                pltpu.VMEM((blocks, slots, BLOCK, BLOCK), jnp.bfloat16),
                pltpu.SemaphoreType.DMA((count,)),
                pltpu.SemaphoreType.DMA((blocks,)),
            ],
        ),
        out_shape=jax.ShapeDtypeStruct((blocks, slots, windows, BLOCK, BLOCK), jnp.bfloat16),
        input_output_aliases={} if earlier is None else {2 + count: 0},
        compiler_params=pltpu.CompilerParams(vmem_limit_bytes=VMEM_BYTES),
        cost_estimate=SMALL,
        name="tiles",
    )(place, present, *operands)


def after(value, *earlier):
    return lax.optimization_barrier((value,) + earlier)[0]


def on_device(bold, gm_index, partners):
    row_total = lax.axis_size("row")
    col_total = lax.axis_size("col")
    row = lax.axis_index("row")
    col = lax.axis_index("col")
    even = row % 2 == 0

    def other_col(value):
        return lax.ppermute(value, "col", [(0, 1), (1, 0)])

    ahead = [((i + 2 * (-1) ** i) % row_total, i) for i in range(row_total)]
    behind = [(i, source) for source, i in ahead]
    two_on = [(i, i + 2 * (-1) ** (i + 1)) for i in range(row_total)]
    two_on = [(i, target) for i, target in two_on if 0 <= target < row_total]
    across_pairs = [(i, i - (-1) ** i) for i in range(row_total)]
    across_pairs = [(i, target) for i, target in across_pairs if 0 <= target < row_total]
    in_pair = [(i, i ^ 1) for i in range(row_total)]

    gm = gm_index.reshape(-1, BLOCK)
    blocks, slots = partners.shape
    ids = jnp.maximum(partners, 0)
    slab = ids // blocks
    hop = (slab // col_total - row + 2 + row_total) % row_total
    kind = jnp.where((hop == 1) == even, 4, 3)
    kind = jnp.where(hop == 2, 0, jnp.where((hop == 0) | (hop >= 4), 2 - (even == (hop >= 4)), kind))
    away = (slab % col_total != col).astype(jnp.int32)
    within = ids % blocks
    present = partners >= 0
    joined = jnp.where(kind == 3, 2, kind) + 3 * away
    alone = jnp.where(kind == 3, 4, jnp.where(kind == 4, 6, 8)) + away
    parts_0 = jnp.where(kind == 2, 6 + away, jnp.where(kind == 4, 8 + away, joined))
    parts_1 = jnp.where(kind < 2, kind + 2 * away, alone)
    place_0, place_1 = (
        jnp.where(present, part * blocks + within, 0).astype(jnp.int32)
        for part in (parts_0, parts_1)
    )
    present = present.astype(jnp.int32)

    def both(*parts):
        near = jnp.stack(parts, 0)
        return [near, other_col(near)]

    windows = bold.shape[0]
    frames, slab_y = bold.shape[1], bold.shape[3]

    def ends(*layers):
        planes = [
            jnp.where(col == 0, plane_of(layer, slab_y - 1, frames), plane_of(layer, 0, frames))
            for layer in layers
        ]
        return other_col(jnp.stack(planes, 0))

    near_0, outer_0, face_0, near_1, outer_1, face_1 = make_faces(bold, gm)
    facing_0 = lax.ppermute(near_0, "row", in_pair)
    across_0 = lax.ppermute(outer_0, "row", across_pairs)
    beyond_1 = lax.ppermute(outer_1, "row", two_on)
    edge_0, edge_1 = other_col(face_0), other_col(face_1)
    inner_1 = make_inner(near_1, outer_1, edge_1, after(gm, edge_0))
    facing_0, across_0 = after(facing_0, inner_1), after(across_0, inner_1)
    beyond_1 = after(beyond_1, facing_0, across_0)
    gm_pair = facing_0[slab_y * frames :]
    corner = ends(across_0, facing_0, beyond_1)
    given_1 = make_halo(near_1, beyond_1, edge_1, corner, gm_pair)
    halo_1 = lax.ppermute(given_1, "row", in_pair)
    corner = after(corner, given_1)
    own_0 = make_panel(near_0, outer_0, facing_0, across_0, edge_0, corner, gm)
    ahead_0 = lax.ppermute(own_0, "row", ahead)
    halo_1 = after(halo_1, own_0)
    own_1 = join(inner_1, halo_1)
    pair_0 = lax.ppermute(after(own_0, halo_1), "row", in_pair)
    pair_1 = lax.ppermute(own_1, "row", in_pair)
    ahead_1 = lax.ppermute(own_1, "row", ahead)
    ahead_0 = after(ahead_0, own_1)
    behind_0 = lax.ppermute(after(own_0, ahead_0), "row", behind)
    rest_0 = lax.ppermute(ahead_0, "row", in_pair)
    pair_0 = after(pair_0, ahead_0)
    pair_1 = after(pair_1, pair_0)
    ahead_1 = after(ahead_1, pair_1)
    rest_0 = after(rest_0, ahead_1)
    behind_0 = after(behind_0, rest_0)
    rest_1 = lax.ppermute(ahead_1, "row", in_pair)
    behind_1 = lax.ppermute(after(own_1, ahead_1), "row", behind)
    sources_0 = both(own_0, ahead_0, pair_0) + both(behind_0) + both(rest_0)
    out = make_tiles(0, windows, place_0, present, sources_0, None)
    sources_1 = both(own_1, ahead_1) + both(pair_1) + both(rest_1) + both(behind_1)
    return make_tiles(1, windows, place_1, present, sources_1, out)


def solution(mesh):
    in_specs = (P("subj", None, "row", "col", None), P(("row", "col")), P(("row", "col"), None))
    out_specs = P(("row", "col"), None, "subj", None, None)
    return jax.shard_map(
        on_device, mesh=mesh, in_specs=in_specs, out_specs=out_specs, check_vma=False
    )
```

```python
import functools
import math

import jax
import jax.numpy as jnp
from jax import lax
from jax.experimental import pallas as pl
from jax.experimental.pallas import tpu as pltpu
from jax.sharding import PartitionSpec as P

BLOCK = 128
SIDE = math.exp(-0.5) / (1.0 + 2.0 * math.exp(-0.5))
CENTRE = 1.0 / (1.0 + 2.0 * math.exp(-0.5))
SMALL = pl.CostEstimate(flops=1, bytes_accessed=1, transcendentals=0)
VMEM_BYTES = 20 * 1024 * 1024
TILES_VMEM_BYTES = 28 * 1024 * 1024


def is_even():
    return lax.axis_index("row") % 2 == 0


def is_first():
    return lax.axis_index("col") == 0


def plane_of(layer, y, frames):
    return layer[y] if len(layer.shape) == 3 else layer[y * frames : (y + 1) * frames]


def faces_kernel(bold_ref, gm_ref, *refs):
    windows, frames, slab_x, slab_y, slab_z = bold_ref.shape
    per_frame = slab_x * slab_y
    wide = refs[-1]
    for window in range(windows):
        near_ref, outer_ref, edge_ref = refs[3 * window : 3 * window + 3]
        wide[...] = bold_ref[window].reshape(frames * per_frame, slab_z).astype(jnp.float32)

        def plane(x, y):
            taken = wide[pl.ds(x * slab_y + y, frames, stride=per_frame), :]
            return taken.astype(jnp.bfloat16)

        def store(layer_ref, y, value):
            if len(layer_ref.shape) == 3:
                layer_ref[y] = value
            else:
                layer_ref[y * frames : (y + 1) * frames] = value

        def layers(first_ref, last_ref):
            for y in range(slab_y):
                store(first_ref, y, plane(0, y))
                store(last_ref, y, plane(1, y))

        pl.when(is_even())(functools.partial(layers, outer_ref, near_ref))
        pl.when(~is_even())(functools.partial(layers, near_ref, outer_ref))

        def edges(y):
            for x in range(slab_x):
                edge_ref[x] = plane(x, y)

        if len(near_ref.shape) == 2:
            number = gm_ref[...] + 1
            parts = jnp.concatenate([lax.shift_right_logical(number, 6), number & 63], axis=0)
            near_ref[slab_y * frames :] = parts.astype(jnp.float32).astype(jnp.bfloat16)

        pl.when(is_first())(functools.partial(edges, slab_y - 1))
        pl.when(~is_first())(functools.partial(edges, 0))


def make_faces(bold, gm):
    windows, frames, slab_x, slab_y, slab_z = bold.shape
    layer = jax.ShapeDtypeStruct((slab_y, frames, slab_z), jnp.bfloat16)
    edge = jax.ShapeDtypeStruct((slab_x, frames, slab_z), jnp.bfloat16)
    with_gm = jax.ShapeDtypeStruct(
        (slab_y * frames + 2 * gm.shape[0], slab_z), jnp.bfloat16
    )
    outs = [with_gm, layer, edge] + [layer, layer, edge] * (windows - 1)
    whole = lambda array: pl.BlockSpec(array.shape, lambda _: (0,) * len(array.shape))
    return pl.pallas_call(
        faces_kernel,
        grid=(1,),
        in_specs=[whole(bold), whole(gm)],
        out_specs=[whole(value) for value in outs],
        out_shape=outs,
        scratch_shapes=[pltpu.VMEM((frames * slab_x * slab_y, slab_z), jnp.float32)],
        compiler_params=pltpu.CompilerParams(vmem_limit_bytes=VMEM_BYTES),
        cost_estimate=SMALL,
        name="faces",
    )(bold, gm)


def three_taps(before, here, after):
    return SIDE * before + CENTRE * here + SIDE * after


def along_z(part):
    lane = lax.broadcasted_iota(jnp.int32, part.shape, 1)
    last = part.shape[1] - 1
    before = jnp.where(lane == 0, 0.0, pltpu.roll(part, 1, 1))
    after = jnp.where(lane == last, 0.0, pltpu.roll(part, last, 1))
    return three_taps(before, part, after)


def place_edge(planes, x, edge):
    planes[x, 0] = jnp.where(is_first(), 0.0, edge)
    planes[x, planes.shape[1] - 1] = jnp.where(is_first(), edge, 0.0)


def standardise(smooth):
    frames = smooth.shape[0]
    centred = smooth - jnp.mean(smooth, axis=0, keepdims=True)
    spread = jnp.mean(centred * centred, axis=0, keepdims=True)
    return (centred * lax.rsqrt((spread + 1e-05) * frames)).astype(jnp.bfloat16)


def pick(parts, gm, out_ref):
    voxels = parts[0].shape[1]
    for line in range(0, gm.shape[0], 2):
        wanted = jnp.concatenate([gm[line : line + 1], gm[line + 1 : line + 2]], axis=1)
        voxel = lax.broadcasted_iota(jnp.int32, (voxels, 2 * BLOCK), 0)
        chosen = jnp.where(voxel == wanted, 1.0, 0.0).astype(jnp.bfloat16)
        total = jnp.dot(parts[0][...], chosen, preferred_element_type=jnp.float32)
        for part in parts[1:]:
            total += jnp.dot(part[...], chosen, preferred_element_type=jnp.float32)
        start = line * BLOCK
        out_ref[:, start : start + 2 * BLOCK] = total.astype(out_ref.dtype)


def panel_kernel(
    near_ref, outer_ref, facing_ref, across_ref, edge_ref, corner_ref, gm_ref, out_ref,
    planes, scored,
):
    slab_y, frames, slab_z = outer_ref.shape
    even = is_even()

    def along_x(across, outer, near, facing):
        layers = [part.astype(jnp.float32) for part in (across, outer, near, facing)]
        outer, near = three_taps(*layers[:3]), three_taps(*layers[1:])
        return jnp.where(even, outer, near), jnp.where(even, near, outer)

    for y in range(slab_y):
        planes[0, y + 1], planes[1, y + 1] = along_x(
            across_ref[y],
            outer_ref[y],
            plane_of(near_ref, y, frames),
            plane_of(facing_ref, y, frames),
        )
    outer = jnp.where(even, edge_ref[0], edge_ref[1])
    near = jnp.where(even, edge_ref[1], edge_ref[0])
    for x, edge in enumerate(along_x(corner_ref[0], outer, near, corner_ref[1])):
        place_edge(planes, x, edge)
    for x in range(2):
        for y in range(slab_y):
            part = three_taps(planes[x, y], planes[x, y + 1], planes[x, y + 2])
            start = (x * slab_y + y) * slab_z
            scored[:, start : start + slab_z] = standardise(along_z(part))
    pick([scored], gm_ref[...], out_ref)


def inner_kernel(
    near_ref, outer_ref, edge_ref, gm_ref, out_ref, planes, high, middle, low
):
    slab_y, frames, slab_z = near_ref.shape
    slab_x = edge_ref.shape[0]
    even = is_even()

    def two_taps(here, other):
        return CENTRE * here + SIDE * other

    for y in range(slab_y):
        near, outer = near_ref[y].astype(jnp.float32), outer_ref[y].astype(jnp.float32)
        first, last = jnp.where(even, outer, near), jnp.where(even, near, outer)
        planes[0, y + 1] = two_taps(first, last)
        planes[1, y + 1] = two_taps(last, first)
    edges = [edge_ref[x].astype(jnp.float32) for x in range(slab_x)]
    for x in range(slab_x):
        place_edge(planes, x, two_taps(edges[x], edges[1 - x]))
    for x in range(slab_x):
        for y in range(slab_y):
            part = along_z(three_taps(planes[x, y], planes[x, y + 1], planes[x, y + 2]))
            start = (x * slab_y + y) * slab_z
            for term in (high, middle, low):
                rounded = part.astype(jnp.bfloat16)
                term[:, start : start + slab_z] = rounded
                part = part - rounded.astype(jnp.float32)
    pick([high, middle, low], gm_ref[...], out_ref)


def halo_kernel(
    near_ref, beyond_ref, edge_ref, corner_ref, gm_ref, out_ref, planes, scored
):
    slab_y, frames, slab_z = near_ref.shape
    even = is_even()

    def sides(own, beyond):
        own, beyond = own.astype(jnp.float32), beyond.astype(jnp.float32)
        return jnp.where(even, own, beyond), jnp.where(even, beyond, own)

    for y in range(slab_y):
        planes[0, y + 1], planes[1, y + 1] = sides(near_ref[y], beyond_ref[y])
    own = jnp.where(even, edge_ref[1], edge_ref[0])
    for x, edge in enumerate(sides(own, corner_ref[2])):
        place_edge(planes, x, edge)
    for x in range(2):
        for y in range(slab_y):
            part = three_taps(planes[x, y], planes[x, y + 1], planes[x, y + 2])
            start = (x * slab_y + y) * slab_z
            scored[:, start : start + slab_z] = along_z(part).astype(jnp.bfloat16)
    lines = gm_ref.shape[0] // 2
    number = gm_ref[...].astype(jnp.float32).astype(jnp.int32)
    pick([scored], number[:lines] * 64 + number[lines:] - 1, out_ref)


def join_kernel(inner_ref, halo_ref, out_ref):
    for start in range(0, out_ref.shape[1], BLOCK):
        span = slice(start, start + BLOCK)
        smooth = inner_ref[:, span] + SIDE * halo_ref[:, span].astype(jnp.float32)
        out_ref[:, span] = standardise(smooth)


def call_on_rows(kernel, dtype, frames, rows, operands, scratch, name):
    whole = lambda array: pl.BlockSpec(array.shape, lambda _: (0,) * array.ndim)
    return pl.pallas_call(
        kernel,
        grid=(1,),
        in_specs=[whole(value) for value in operands],
        out_specs=pl.BlockSpec((frames, rows), lambda _: (0, 0)),
        out_shape=jax.ShapeDtypeStruct((frames, rows), dtype),
        scratch_shapes=scratch,
        compiler_params=pltpu.CompilerParams(vmem_limit_bytes=VMEM_BYTES),
        cost_estimate=SMALL,
        name=name,
    )(*operands)


def blur_scratch(first, terms):
    slab_y, frames, slab_z = first.shape
    planes = pltpu.VMEM((2, slab_y + 2, frames, slab_z), jnp.float32)
    return [planes] + [pltpu.VMEM((frames, 2 * slab_y * slab_z), jnp.bfloat16)] * terms


def make_panel(near, outer, facing, across, edge, corner, gm):
    operands = (near, outer, facing, across, edge, corner, gm)
    scratch = blur_scratch(outer, 1)
    return call_on_rows(
        panel_kernel, jnp.bfloat16, outer.shape[1], gm.size, operands, scratch, "blur_score_pick"
    )


def make_inner(near, outer, edge, gm):
    operands = (near, outer, edge, gm)
    scratch = blur_scratch(near, 3)
    return call_on_rows(
        inner_kernel, jnp.float32, near.shape[1], gm.size, operands, scratch, "inner_blur"
    )


def make_halo(near, beyond, edge, corner, gm):
    operands = (near, beyond, edge, corner, gm)
    scratch = blur_scratch(near, 1)
    return call_on_rows(
        halo_kernel, jnp.bfloat16, near.shape[1], gm.size // 2, operands, scratch, "halo_blur"
    )


def join(inner, halo):
    return call_on_rows(
        join_kernel, jnp.bfloat16, *inner.shape, (inner, halo), [], "join_score"
    )


def tiles_kernel(*refs, counts):
    windows = len(counts)
    places, present_ref = refs[:windows], refs[windows]
    out_ref, held, tiles, sems, out_sems = refs[-5:]
    blocks, slots = out_ref.shape[:2]

    loads, used = [], windows + 1
    for window, count in enumerate(counts):
        first, here = 0, []
        for n, part in enumerate(refs[used : used + count]):
            target = held.at[window, pl.ds(first, part.shape[0])]
            here.append(pltpu.make_async_copy(part, target, sems.at[window, n]))
            here[-1].start()
            first += part.shape[0]
        loads.append(here)
        used += count

    stores = []
    for window in range(windows):
        for load in loads[window]:
            load.wait()

        def partner(block, slot):
            place = places[window][block, slot]
            start = pl.multiple_of(lax.rem(place, blocks) * BLOCK, BLOCK)
            return held[window, lax.div(place, blocks), :, pl.ds(start, BLOCK)]

        for block in range(blocks):
            own = held[window, 0, :, block * BLOCK : (block + 1) * BLOCK].T
            for slot in range(0, slots, 2):
                pair = jnp.concatenate([partner(block, slot), partner(block, slot + 1)], axis=1)
                both = jnp.dot(own, pair, preferred_element_type=jnp.float32)
                for n in range(2):
                    tile = both[:, n * BLOCK : (n + 1) * BLOCK]
                    tile = jnp.where(present_ref[block, slot + n] != 0, tile, 0.0)
                    tiles[window, block, slot + n] = tile.astype(jnp.bfloat16)
            store = pltpu.make_async_copy(
                tiles.at[window, block], out_ref.at[block, :, window], out_sems.at[window, block]
            )
            store.start()
            stores.append(store)
    for store in stores:
        store.wait()


def make_tiles(places, present, sources):
    frames, rows = sources[0][0].shape[1:]
    windows = len(sources)
    total = sum(part.shape[0] for part in sources[0])
    counts = tuple(len(parts) for parts in sources)
    operands = [part for parts in sources for part in parts]
    blocks = rows // BLOCK
    slots = present.shape[1]
    anywhere = pl.BlockSpec(memory_space=pl.ANY)
    return pl.pallas_call(
        functools.partial(tiles_kernel, counts=counts),
        grid_spec=pltpu.PrefetchScalarGridSpec(
            num_scalar_prefetch=windows + 1,
            grid=(1,),
            in_specs=[anywhere] * len(operands),
            out_specs=anywhere,
            scratch_shapes=[
                pltpu.VMEM((windows, total, frames, rows), jnp.bfloat16),
                pltpu.VMEM((windows, blocks, slots, BLOCK, BLOCK), jnp.bfloat16),
                pltpu.SemaphoreType.DMA((windows, max(counts))),
                pltpu.SemaphoreType.DMA((windows, blocks)),
            ],
        ),
        out_shape=jax.ShapeDtypeStruct((blocks, slots, windows, BLOCK, BLOCK), jnp.bfloat16),
        compiler_params=pltpu.CompilerParams(vmem_limit_bytes=TILES_VMEM_BYTES),
        cost_estimate=SMALL,
        name="tiles",
    )(*places, present, *operands)


def after(value, *earlier):
    return lax.optimization_barrier((value,) + earlier)[0]


def on_device(bold, gm_index, partners):
    row_total = lax.axis_size("row")
    col_total = lax.axis_size("col")
    row = lax.axis_index("row")
    col = lax.axis_index("col")
    even = row % 2 == 0

    def other_col(value):
        return lax.ppermute(value, "col", [(0, 1), (1, 0)])

    ahead = [((i + 2 * (-1) ** i) % row_total, i) for i in range(row_total)]
    behind = [(i, source) for source, i in ahead]
    two_on = [(i, i + 2 * (-1) ** (i + 1)) for i in range(row_total)]
    two_on = [(i, target) for i, target in two_on if 0 <= target < row_total]
    across_pairs = [(i, i - (-1) ** i) for i in range(row_total)]
    across_pairs = [(i, target) for i, target in across_pairs if 0 <= target < row_total]
    in_pair = [(i, i ^ 1) for i in range(row_total)]

    gm = gm_index.reshape(-1, BLOCK)
    blocks, slots = partners.shape
    ids = jnp.maximum(partners, 0)
    slab = ids // blocks
    hop = (slab // col_total - row + 2 + row_total) % row_total
    kind = jnp.where((hop == 1) == even, 4, 3)
    kind = jnp.where(hop == 2, 0, jnp.where((hop == 0) | (hop >= 4), 2 - (even == (hop >= 4)), kind))
    away = (slab % col_total != col).astype(jnp.int32)
    within = ids % blocks
    present = partners >= 0
    joined = jnp.where(kind == 3, 2, kind) + 3 * away
    alone = jnp.where(kind == 3, 4, jnp.where(kind == 4, 6, 8)) + away
    parts_0 = jnp.where(kind == 2, 6 + away, jnp.where(kind == 4, 8 + away, joined))
    parts_1 = jnp.where(kind < 2, kind + 2 * away, alone)
    place_0, place_1 = (
        jnp.where(present, part * blocks + within, 0).astype(jnp.int32)
        for part in (parts_0, parts_1)
    )
    present = present.astype(jnp.int32)

    def both(*parts):
        near = jnp.stack(parts, 0)
        return [near, other_col(near)]

    frames, slab_y = bold.shape[1], bold.shape[3]

    def ends(*layers):
        planes = [
            jnp.where(col == 0, plane_of(layer, slab_y - 1, frames), plane_of(layer, 0, frames))
            for layer in layers
        ]
        return other_col(jnp.stack(planes, 0))

    near_0, outer_0, face_0, near_1, outer_1, face_1 = make_faces(bold, gm)
    facing_0 = lax.ppermute(near_0, "row", in_pair)
    across_0 = lax.ppermute(outer_0, "row", across_pairs)
    beyond_1 = lax.ppermute(outer_1, "row", two_on)
    edge_0, edge_1 = other_col(face_0), other_col(face_1)
    inner_1 = make_inner(near_1, outer_1, edge_1, after(gm, edge_0))
    facing_0, across_0 = after(facing_0, inner_1), after(across_0, inner_1)
    beyond_1 = after(beyond_1, facing_0, across_0)
    gm_pair = facing_0[slab_y * frames :]
    corner = ends(across_0, facing_0, beyond_1)
    given_1 = make_halo(near_1, beyond_1, edge_1, corner, gm_pair)
    halo_1 = lax.ppermute(given_1, "row", in_pair)
    corner = after(corner, given_1)
    own_0 = make_panel(near_0, outer_0, facing_0, across_0, edge_0, corner, gm)
    ahead_0 = lax.ppermute(own_0, "row", ahead)
    halo_1 = after(halo_1, own_0)
    own_1 = join(inner_1, halo_1)
    pair_0 = lax.ppermute(after(own_0, halo_1), "row", in_pair)
    pair_1 = lax.ppermute(own_1, "row", in_pair)
    ahead_1 = lax.ppermute(own_1, "row", ahead)
    ahead_0 = after(ahead_0, own_1)
    behind_0 = lax.ppermute(after(own_0, ahead_0), "row", behind)
    rest_0 = lax.ppermute(ahead_0, "row", in_pair)
    pair_0 = after(pair_0, ahead_0)
    pair_1 = after(pair_1, pair_0)
    ahead_1 = after(ahead_1, pair_1)
    rest_0 = after(rest_0, ahead_1)
    behind_0 = after(behind_0, rest_0)
    rest_1 = lax.ppermute(ahead_1, "row", in_pair)
    behind_1 = lax.ppermute(after(own_1, ahead_1), "row", behind)
    sources_0 = both(own_0, ahead_0, pair_0) + both(behind_0) + both(rest_0)
    sources_1 = both(own_1, ahead_1) + both(pair_1) + both(rest_1) + both(behind_1)
    return make_tiles((place_0, place_1), present, (sources_0, sources_1))


def solution(mesh):
    in_specs = (P("subj", None, "row", "col", None), P(("row", "col")), P(("row", "col"), None))
    out_specs = P(("row", "col"), None, "subj", None, None)
    return jax.shard_map(
        on_device, mesh=mesh, in_specs=in_specs, out_specs=out_specs, check_vma=False
    )
```

```python
import functools
import math

import jax
import jax.numpy as jnp
from jax import lax
from jax.experimental import pallas as pl
from jax.experimental.pallas import tpu as pltpu
from jax.sharding import PartitionSpec as P

BLOCK = 128
SIDE = math.exp(-0.5) / (1.0 + 2.0 * math.exp(-0.5))
CENTRE = 1.0 / (1.0 + 2.0 * math.exp(-0.5))
SMALL = pl.CostEstimate(flops=1, bytes_accessed=1, transcendentals=0)
VMEM_BYTES = 12 * 1024 * 1024


def is_even():
    return lax.axis_index("row") % 2 == 0


def is_first():
    return lax.axis_index("col") == 0


def plane_of(layer, y, frames):
    return layer[y] if len(layer.shape) == 3 else layer[y * frames : (y + 1) * frames]


def faces_kernel(bold_ref, gm_ref, *refs):
    windows, frames, slab_x, slab_y, slab_z = bold_ref.shape
    per_frame = slab_x * slab_y
    wide = refs[-1]
    for window in range(windows):
        near_ref, outer_ref, edge_ref = refs[3 * window : 3 * window + 3]
        wide[...] = bold_ref[window].reshape(frames * per_frame, slab_z).astype(jnp.float32)

        def plane(x, y):
            taken = wide[pl.ds(x * slab_y + y, frames, stride=per_frame), :]
            return taken.astype(jnp.bfloat16)

        def store(layer_ref, y, value):
            if len(layer_ref.shape) == 3:
                layer_ref[y] = value
            else:
                layer_ref[y * frames : (y + 1) * frames] = value

        def layers(first_ref, last_ref):
            for y in range(slab_y):
                store(first_ref, y, plane(0, y))
                store(last_ref, y, plane(1, y))

        pl.when(is_even())(functools.partial(layers, outer_ref, near_ref))
        pl.when(~is_even())(functools.partial(layers, near_ref, outer_ref))

        def edges(y):
            for x in range(slab_x):
                edge_ref[x] = plane(x, y)

        if len(near_ref.shape) == 2:
            number = gm_ref[...] + 1
            parts = jnp.concatenate([lax.shift_right_logical(number, 6), number & 63], axis=0)
            near_ref[slab_y * frames :] = parts.astype(jnp.float32).astype(jnp.bfloat16)

        pl.when(is_first())(functools.partial(edges, slab_y - 1))
        pl.when(~is_first())(functools.partial(edges, 0))


def make_faces(bold, gm):
    windows, frames, slab_x, slab_y, slab_z = bold.shape
    layer = jax.ShapeDtypeStruct((slab_y, frames, slab_z), jnp.bfloat16)
    edge = jax.ShapeDtypeStruct((slab_x, frames, slab_z), jnp.bfloat16)
    with_gm = jax.ShapeDtypeStruct(
        (slab_y * frames + 2 * gm.shape[0], slab_z), jnp.bfloat16
    )
    outs = [with_gm, layer, edge] + [layer, layer, edge] * (windows - 1)
    whole = lambda array: pl.BlockSpec(array.shape, lambda _: (0,) * len(array.shape))
    return pl.pallas_call(
        faces_kernel,
        grid=(1,),
        in_specs=[whole(bold), whole(gm)],
        out_specs=[whole(value) for value in outs],
        out_shape=outs,
        scratch_shapes=[pltpu.VMEM((frames * slab_x * slab_y, slab_z), jnp.float32)],
        compiler_params=pltpu.CompilerParams(vmem_limit_bytes=VMEM_BYTES),
        cost_estimate=SMALL,
        name="faces",
    )(bold, gm)


def three_taps(before, here, after):
    return SIDE * before + CENTRE * here + SIDE * after


def along_z(part):
    lane = lax.broadcasted_iota(jnp.int32, part.shape, 1)
    last = part.shape[1] - 1
    before = jnp.where(lane == 0, 0.0, pltpu.roll(part, 1, 1))
    after = jnp.where(lane == last, 0.0, pltpu.roll(part, last, 1))
    return three_taps(before, part, after)


def place_edge(planes, x, edge):
    planes[x, 0] = jnp.where(is_first(), 0.0, edge)
    planes[x, planes.shape[1] - 1] = jnp.where(is_first(), edge, 0.0)


def standardise(smooth):
    frames = smooth.shape[0]
    centred = smooth - jnp.mean(smooth, axis=0, keepdims=True)
    spread = jnp.mean(centred * centred, axis=0, keepdims=True)
    return (centred * lax.rsqrt((spread + 1e-05) * frames)).astype(jnp.bfloat16)


def pick(parts, gm, out_ref):
    voxels = parts[0].shape[1]
    for line in range(0, gm.shape[0], 2):
        wanted = jnp.concatenate([gm[line : line + 1], gm[line + 1 : line + 2]], axis=1)
        voxel = lax.broadcasted_iota(jnp.int32, (voxels, 2 * BLOCK), 0)
        chosen = jnp.where(voxel == wanted, 1.0, 0.0).astype(jnp.bfloat16)
        total = jnp.dot(parts[0][...], chosen, preferred_element_type=jnp.float32)
        for part in parts[1:]:
            total += jnp.dot(part[...], chosen, preferred_element_type=jnp.float32)
        start = line * BLOCK
        out_ref[:, start : start + 2 * BLOCK] = total.astype(out_ref.dtype)


def panel_kernel(
    near_ref, outer_ref, facing_ref, across_ref, edge_ref, corner_ref, gm_ref, out_ref,
    planes, scored,
):
    slab_y, frames, slab_z = outer_ref.shape
    even = is_even()

    def along_x(across, outer, near, facing):
        layers = [part.astype(jnp.float32) for part in (across, outer, near, facing)]
        outer, near = three_taps(*layers[:3]), three_taps(*layers[1:])
        return jnp.where(even, outer, near), jnp.where(even, near, outer)

    for y in range(slab_y):
        planes[0, y + 1], planes[1, y + 1] = along_x(
            across_ref[y],
            outer_ref[y],
            plane_of(near_ref, y, frames),
            plane_of(facing_ref, y, frames),
        )
    outer = jnp.where(even, edge_ref[0], edge_ref[1])
    near = jnp.where(even, edge_ref[1], edge_ref[0])
    for x, edge in enumerate(along_x(corner_ref[0], outer, near, corner_ref[1])):
        place_edge(planes, x, edge)
    for x in range(2):
        for y in range(slab_y):
            part = three_taps(planes[x, y], planes[x, y + 1], planes[x, y + 2])
            start = (x * slab_y + y) * slab_z
            scored[:, start : start + slab_z] = standardise(along_z(part))
    pick([scored], gm_ref[...], out_ref)


def inner_kernel(
    near_ref, outer_ref, edge_ref, gm_ref, out_ref, planes, high, middle, low
):
    slab_y, frames, slab_z = near_ref.shape
    slab_x = edge_ref.shape[0]
    even = is_even()

    def two_taps(here, other):
        return CENTRE * here + SIDE * other

    for y in range(slab_y):
        near, outer = near_ref[y].astype(jnp.float32), outer_ref[y].astype(jnp.float32)
        first, last = jnp.where(even, outer, near), jnp.where(even, near, outer)
        planes[0, y + 1] = two_taps(first, last)
        planes[1, y + 1] = two_taps(last, first)
    edges = [edge_ref[x].astype(jnp.float32) for x in range(slab_x)]
    for x in range(slab_x):
        place_edge(planes, x, two_taps(edges[x], edges[1 - x]))
    for x in range(slab_x):
        for y in range(slab_y):
            part = along_z(three_taps(planes[x, y], planes[x, y + 1], planes[x, y + 2]))
            start = (x * slab_y + y) * slab_z
            for term in (high, middle, low):
                rounded = part.astype(jnp.bfloat16)
                term[:, start : start + slab_z] = rounded
                part = part - rounded.astype(jnp.float32)
    pick([high, middle, low], gm_ref[...], out_ref)


def halo_kernel(
    near_ref, beyond_ref, edge_ref, corner_ref, gm_ref, out_ref, planes, scored
):
    slab_y, frames, slab_z = near_ref.shape
    even = is_even()

    def sides(own, beyond):
        own, beyond = own.astype(jnp.float32), beyond.astype(jnp.float32)
        return jnp.where(even, own, beyond), jnp.where(even, beyond, own)

    for y in range(slab_y):
        planes[0, y + 1], planes[1, y + 1] = sides(near_ref[y], beyond_ref[y])
    own = jnp.where(even, edge_ref[1], edge_ref[0])
    for x, edge in enumerate(sides(own, corner_ref[2])):
        place_edge(planes, x, edge)
    for x in range(2):
        for y in range(slab_y):
            part = three_taps(planes[x, y], planes[x, y + 1], planes[x, y + 2])
            start = (x * slab_y + y) * slab_z
            scored[:, start : start + slab_z] = along_z(part).astype(jnp.bfloat16)
    lines = gm_ref.shape[0] // 2
    number = gm_ref[...].astype(jnp.float32).astype(jnp.int32)
    pick([scored], number[:lines] * 64 + number[lines:] - 1, out_ref)


def join_kernel(inner_ref, halo_ref, out_ref):
    for start in range(0, out_ref.shape[1], BLOCK):
        span = slice(start, start + BLOCK)
        smooth = inner_ref[:, span] + SIDE * halo_ref[:, span].astype(jnp.float32)
        out_ref[:, span] = standardise(smooth)


def call_on_rows(kernel, dtype, frames, rows, operands, scratch, name):
    whole = lambda array: pl.BlockSpec(array.shape, lambda _: (0,) * array.ndim)
    return pl.pallas_call(
        kernel,
        grid=(1,),
        in_specs=[whole(value) for value in operands],
        out_specs=pl.BlockSpec((frames, rows), lambda _: (0, 0)),
        out_shape=jax.ShapeDtypeStruct((frames, rows), dtype),
        scratch_shapes=scratch,
        compiler_params=pltpu.CompilerParams(vmem_limit_bytes=VMEM_BYTES),
        cost_estimate=SMALL,
        name=name,
    )(*operands)


def blur_scratch(first, terms):
    slab_y, frames, slab_z = first.shape
    planes = pltpu.VMEM((2, slab_y + 2, frames, slab_z), jnp.float32)
    return [planes] + [pltpu.VMEM((frames, 2 * slab_y * slab_z), jnp.bfloat16)] * terms


def make_panel(near, outer, facing, across, edge, corner, gm):
    operands = (near, outer, facing, across, edge, corner, gm)
    scratch = blur_scratch(outer, 1)
    return call_on_rows(
        panel_kernel, jnp.bfloat16, outer.shape[1], gm.size, operands, scratch, "blur_score_pick"
    )


def make_inner(near, outer, edge, gm):
    operands = (near, outer, edge, gm)
    scratch = blur_scratch(near, 3)
    return call_on_rows(
        inner_kernel, jnp.float32, near.shape[1], gm.size, operands, scratch, "inner_blur"
    )


def make_halo(near, beyond, edge, corner, gm):
    operands = (near, beyond, edge, corner, gm)
    scratch = blur_scratch(near, 1)
    return call_on_rows(
        halo_kernel, jnp.bfloat16, near.shape[1], gm.size // 2, operands, scratch, "halo_blur"
    )


def join(inner, halo):
    return call_on_rows(
        join_kernel, jnp.bfloat16, *inner.shape, (inner, halo), [], "join_score"
    )


def tiles_kernel(place_ref, present_ref, *refs, sources, window):
    parts = refs[:sources]
    out_ref, held, tiles, sems, out_sems = refs[-5:]
    blocks, slots = out_ref.shape[:2]

    loads = []
    first = 0
    for n, part in enumerate(parts):
        target = held.at[pl.ds(first, part.shape[0])]
        first += part.shape[0]
        loads.append(pltpu.make_async_copy(part, target, sems.at[n]))
        loads[-1].start()
    for load in loads:
        load.wait()

    def partner(block, slot):
        place = place_ref[block, slot]
        start = pl.multiple_of(lax.rem(place, blocks) * BLOCK, BLOCK)
        return held[lax.div(place, blocks), :, pl.ds(start, BLOCK)]

    stores = []
    for block in range(blocks):
        own = held[0, :, block * BLOCK : (block + 1) * BLOCK].T
        for slot in range(0, slots, 2):
            pair = jnp.concatenate([partner(block, slot), partner(block, slot + 1)], axis=1)
            both = jnp.dot(own, pair, preferred_element_type=jnp.float32)
            for n in range(2):
                tile = both[:, n * BLOCK : (n + 1) * BLOCK]
                tile = jnp.where(present_ref[block, slot + n] != 0, tile, 0.0)
                tiles[block, slot + n] = tile.astype(jnp.bfloat16)
        stores.append(
            pltpu.make_async_copy(tiles.at[block], out_ref.at[block, :, window], out_sems.at[block])
        )
        stores[-1].start()
    for store in stores:
        store.wait()


def make_tiles(window, windows, place, present, sources, earlier):
    frames, rows = sources[0].shape[1:]
    total = sum(source.shape[0] for source in sources)
    blocks = rows // BLOCK
    slots = place.shape[1]
    count = len(sources)
    anywhere = pl.BlockSpec(memory_space=pl.ANY)
    operands = list(sources) + ([] if earlier is None else [earlier])
    return pl.pallas_call(
        functools.partial(tiles_kernel, sources=count, window=window),
        grid_spec=pltpu.PrefetchScalarGridSpec(
            num_scalar_prefetch=2,
            grid=(1,),
            in_specs=[anywhere] * len(operands),
            out_specs=anywhere,
            scratch_shapes=[
                pltpu.VMEM((total, frames, rows), jnp.bfloat16),
                pltpu.VMEM((blocks, slots, BLOCK, BLOCK), jnp.bfloat16),
                pltpu.SemaphoreType.DMA((count,)),
                pltpu.SemaphoreType.DMA((blocks,)),
            ],
        ),
        out_shape=jax.ShapeDtypeStruct((blocks, slots, windows, BLOCK, BLOCK), jnp.bfloat16),
        input_output_aliases={} if earlier is None else {2 + count: 0},
        compiler_params=pltpu.CompilerParams(vmem_limit_bytes=VMEM_BYTES),
        cost_estimate=SMALL,
        name="tiles",
    )(place, present, *operands)


def after(value, *earlier):
    return lax.optimization_barrier((value,) + earlier)[0]


def on_device(bold, gm_index, partners):
    row_total = lax.axis_size("row")
    col_total = lax.axis_size("col")
    row = lax.axis_index("row")
    col = lax.axis_index("col")
    even = row % 2 == 0

    def other_col(value):
        return lax.ppermute(value, "col", [(0, 1), (1, 0)])

    ahead = [((i + 2 * (-1) ** i) % row_total, i) for i in range(row_total)]
    behind = [(i, source) for source, i in ahead]
    two_on = [(i, i + 2 * (-1) ** (i + 1)) for i in range(row_total)]
    two_on = [(i, target) for i, target in two_on if 0 <= target < row_total]
    across_pairs = [(i, i - (-1) ** i) for i in range(row_total)]
    across_pairs = [(i, target) for i, target in across_pairs if 0 <= target < row_total]
    in_pair = [(i, i ^ 1) for i in range(row_total)]

    gm = gm_index.reshape(-1, BLOCK)
    blocks, slots = partners.shape
    ids = jnp.maximum(partners, 0)
    slab = ids // blocks
    hop = (slab // col_total - row + 2 + row_total) % row_total
    kind = jnp.where((hop == 1) == even, 4, 3)
    kind = jnp.where(hop == 2, 0, jnp.where((hop == 0) | (hop >= 4), 2 - (even == (hop >= 4)), kind))
    away = (slab % col_total != col).astype(jnp.int32)
    within = ids % blocks
    present = partners >= 0
    joined = jnp.where(kind == 3, 2, kind) + 3 * away
    alone = jnp.where(kind == 3, 4, jnp.where(kind == 4, 6, 8)) + away
    parts_0 = jnp.where(kind == 2, 6 + away, jnp.where(kind == 4, 8 + away, joined))
    parts_1 = jnp.where(kind < 2, kind + 2 * away, alone)
    place_0, place_1 = (
        jnp.where(present, part * blocks + within, 0).astype(jnp.int32)
        for part in (parts_0, parts_1)
    )
    present = present.astype(jnp.int32)

    def both(*parts):
        near = jnp.stack(parts, 0)
        return [near, other_col(near)]

    windows = bold.shape[0]
    frames, slab_y = bold.shape[1], bold.shape[3]

    def ends(*layers):
        planes = [
            jnp.where(col == 0, plane_of(layer, slab_y - 1, frames), plane_of(layer, 0, frames))
            for layer in layers
        ]
        return other_col(jnp.stack(planes, 0))

    near_0, outer_0, face_0, near_1, outer_1, face_1 = make_faces(bold, gm)
    facing_0 = lax.ppermute(near_0, "row", in_pair)
    across_0 = lax.ppermute(outer_0, "row", across_pairs)
    beyond_1 = lax.ppermute(outer_1, "row", two_on)
    edge_0, edge_1 = other_col(face_0), other_col(face_1)
    inner_1 = make_inner(near_1, outer_1, edge_1, after(gm, edge_0))
    facing_0, across_0 = after(facing_0, inner_1), after(across_0, inner_1)
    beyond_1 = after(beyond_1, facing_0, across_0)
    gm_pair = facing_0[slab_y * frames :]
    corner = ends(across_0, facing_0, beyond_1)
    given_1 = make_halo(near_1, beyond_1, edge_1, corner, gm_pair)
    halo_1 = lax.ppermute(given_1, "row", in_pair)
    corner = after(corner, given_1)
    own_0 = make_panel(near_0, outer_0, facing_0, across_0, edge_0, corner, gm)
    ahead_0 = lax.ppermute(own_0, "row", ahead)
    halo_1 = after(halo_1, own_0)
    own_1 = join(inner_1, halo_1)
    pair_0 = lax.ppermute(after(own_0, halo_1), "row", in_pair)
    pair_1 = lax.ppermute(own_1, "row", in_pair)
    ahead_1 = lax.ppermute(own_1, "row", ahead)
    ahead_0 = after(ahead_0, own_1)
    behind_0 = lax.ppermute(after(own_0, ahead_0), "row", behind)
    rest_0 = lax.ppermute(ahead_0, "row", in_pair)
    pair_0 = after(pair_0, ahead_0)
    pair_1 = after(pair_1, pair_0)
    ahead_1 = after(ahead_1, pair_1)
    rest_0 = after(rest_0, ahead_1)
    behind_0 = after(behind_0, rest_0)
    rest_1 = lax.ppermute(ahead_1, "row", in_pair)
    behind_1 = lax.ppermute(after(own_1, ahead_1), "row", behind)
    sources_0 = both(own_0, ahead_0, pair_0) + both(behind_0) + both(rest_0)
    out = make_tiles(0, windows, place_0, present, sources_0, None)
    sources_1 = both(own_1, ahead_1) + both(pair_1) + both(rest_1) + both(behind_1)
    return make_tiles(1, windows, place_1, present, sources_1, out)


def solution(mesh):
    in_specs = (P("subj", None, "row", "col", None), P(("row", "col")), P(("row", "col"), None))
    out_specs = P(("row", "col"), None, "subj", None, None)
    return jax.shard_map(
        on_device, mesh=mesh, in_specs=in_specs, out_specs=out_specs, check_vma=False
    )
```

```python
import functools
import math

import jax
import jax.numpy as jnp
from jax import lax
from jax.experimental import pallas as pl
from jax.experimental.pallas import tpu as pltpu
from jax.sharding import PartitionSpec as P

BLOCK = 128
SIDE = math.exp(-0.5) / (1.0 + 2.0 * math.exp(-0.5))
CENTRE = 1.0 / (1.0 + 2.0 * math.exp(-0.5))
SMALL = pl.CostEstimate(flops=1, bytes_accessed=1, transcendentals=0)
VMEM_BYTES = 12 * 1024 * 1024


def is_even():
    return lax.axis_index("row") % 2 == 0


def is_first():
    return lax.axis_index("col") == 0


def plane_of(layer, y, frames):
    return layer[y] if len(layer.shape) == 3 else layer[y * frames : (y + 1) * frames]


def faces_kernel(bold_ref, gm_ref, *refs):
    windows, frames, slab_x, slab_y, slab_z = bold_ref.shape
    per_frame = slab_x * slab_y
    wide = refs[-1]
    for window in range(windows):
        near_ref, outer_ref, edge_ref = refs[3 * window : 3 * window + 3]
        wide[...] = bold_ref[window].reshape(frames * per_frame, slab_z).astype(jnp.float32)

        def plane(x, y):
            taken = wide[pl.ds(x * slab_y + y, frames, stride=per_frame), :]
            return taken.astype(jnp.bfloat16)

        def store(layer_ref, y, value):
            if len(layer_ref.shape) == 3:
                layer_ref[y] = value
            else:
                layer_ref[y * frames : (y + 1) * frames] = value

        def layers(first_ref, last_ref):
            for y in range(slab_y):
                store(first_ref, y, plane(0, y))
                store(last_ref, y, plane(1, y))

        pl.when(is_even())(functools.partial(layers, outer_ref, near_ref))
        pl.when(~is_even())(functools.partial(layers, near_ref, outer_ref))

        def edges(y):
            for x in range(slab_x):
                edge_ref[x] = plane(x, y)

        if len(near_ref.shape) == 2:
            number = gm_ref[...] + 1
            parts = jnp.concatenate([lax.shift_right_logical(number, 6), number & 63], axis=0)
            near_ref[slab_y * frames :] = parts.astype(jnp.float32).astype(jnp.bfloat16)

        pl.when(is_first())(functools.partial(edges, slab_y - 1))
        pl.when(~is_first())(functools.partial(edges, 0))


def make_faces(bold, gm):
    windows, frames, slab_x, slab_y, slab_z = bold.shape
    layer = jax.ShapeDtypeStruct((slab_y, frames, slab_z), jnp.bfloat16)
    edge = jax.ShapeDtypeStruct((slab_x, frames, slab_z), jnp.bfloat16)
    with_gm = jax.ShapeDtypeStruct(
        (slab_y * frames + 2 * gm.shape[0], slab_z), jnp.bfloat16
    )
    outs = [with_gm, layer, edge] + [layer, layer, edge] * (windows - 1)
    whole = lambda array: pl.BlockSpec(array.shape, lambda _: (0,) * len(array.shape))
    return pl.pallas_call(
        faces_kernel,
        grid=(1,),
        in_specs=[whole(bold), whole(gm)],
        out_specs=[whole(value) for value in outs],
        out_shape=outs,
        scratch_shapes=[pltpu.VMEM((frames * slab_x * slab_y, slab_z), jnp.float32)],
        compiler_params=pltpu.CompilerParams(vmem_limit_bytes=VMEM_BYTES),
        cost_estimate=SMALL,
        name="faces",
    )(bold, gm)


def three_taps(before, here, after):
    return SIDE * before + CENTRE * here + SIDE * after


def along_z(part):
    lane = lax.broadcasted_iota(jnp.int32, part.shape, 1)
    last = part.shape[1] - 1
    before = jnp.where(lane == 0, 0.0, pltpu.roll(part, 1, 1))
    after = jnp.where(lane == last, 0.0, pltpu.roll(part, last, 1))
    return three_taps(before, part, after)


def place_edge(planes, x, edge):
    planes[x, 0] = jnp.where(is_first(), 0.0, edge)
    planes[x, planes.shape[1] - 1] = jnp.where(is_first(), edge, 0.0)


def standardise(smooth):
    frames = smooth.shape[0]
    centred = smooth - jnp.mean(smooth, axis=0, keepdims=True)
    spread = jnp.mean(centred * centred, axis=0, keepdims=True)
    return (centred * lax.rsqrt((spread + 1e-05) * frames)).astype(jnp.bfloat16)


def pick(parts, gm, out_ref):
    voxels = parts[0].shape[1]
    for line in range(0, gm.shape[0], 2):
        wanted = jnp.concatenate([gm[line : line + 1], gm[line + 1 : line + 2]], axis=1)
        voxel = lax.broadcasted_iota(jnp.int32, (voxels, 2 * BLOCK), 0)
        chosen = jnp.where(voxel == wanted, 1.0, 0.0).astype(jnp.bfloat16)
        total = jnp.dot(parts[0][...], chosen, preferred_element_type=jnp.float32)
        for part in parts[1:]:
            total += jnp.dot(part[...], chosen, preferred_element_type=jnp.float32)
        start = line * BLOCK
        out_ref[:, start : start + 2 * BLOCK] = total.astype(out_ref.dtype)


def panel_kernel(
    near_ref, outer_ref, facing_ref, across_ref, edge_ref, corner_ref, gm_ref, out_ref,
    planes, scored,
):
    slab_y, frames, slab_z = outer_ref.shape
    even = is_even()

    def along_x(across, outer, near, facing):
        layers = [part.astype(jnp.float32) for part in (across, outer, near, facing)]
        outer, near = three_taps(*layers[:3]), three_taps(*layers[1:])
        return jnp.where(even, outer, near), jnp.where(even, near, outer)

    for y in range(slab_y):
        planes[0, y + 1], planes[1, y + 1] = along_x(
            across_ref[y],
            outer_ref[y],
            plane_of(near_ref, y, frames),
            plane_of(facing_ref, y, frames),
        )
    outer = jnp.where(even, edge_ref[0], edge_ref[1])
    near = jnp.where(even, edge_ref[1], edge_ref[0])
    for x, edge in enumerate(along_x(corner_ref[0], outer, near, corner_ref[1])):
        place_edge(planes, x, edge)
    for x in range(2):
        for y in range(slab_y):
            part = three_taps(planes[x, y], planes[x, y + 1], planes[x, y + 2])
            start = (x * slab_y + y) * slab_z
            scored[:, start : start + slab_z] = standardise(along_z(part))
    pick([scored], gm_ref[...], out_ref)


def inner_kernel(
    near_ref, outer_ref, edge_ref, gm_ref, out_ref, planes, high, middle, low
):
    slab_y, frames, slab_z = near_ref.shape
    slab_x = edge_ref.shape[0]
    even = is_even()

    def two_taps(here, other):
        return CENTRE * here + SIDE * other

    for y in range(slab_y):
        near, outer = near_ref[y].astype(jnp.float32), outer_ref[y].astype(jnp.float32)
        first, last = jnp.where(even, outer, near), jnp.where(even, near, outer)
        planes[0, y + 1] = two_taps(first, last)
        planes[1, y + 1] = two_taps(last, first)
    edges = [edge_ref[x].astype(jnp.float32) for x in range(slab_x)]
    for x in range(slab_x):
        place_edge(planes, x, two_taps(edges[x], edges[1 - x]))
    for x in range(slab_x):
        for y in range(slab_y):
            part = along_z(three_taps(planes[x, y], planes[x, y + 1], planes[x, y + 2]))
            start = (x * slab_y + y) * slab_z
            for term in (high, middle, low):
                rounded = part.astype(jnp.bfloat16)
                term[:, start : start + slab_z] = rounded
                part = part - rounded.astype(jnp.float32)
    pick([high, middle, low], gm_ref[...], out_ref)


def halo_kernel(
    near_ref, beyond_ref, edge_ref, corner_ref, gm_ref, out_ref, planes, scored
):
    slab_y, frames, slab_z = near_ref.shape
    even = is_even()

    def sides(own, beyond):
        own, beyond = own.astype(jnp.float32), beyond.astype(jnp.float32)
        return jnp.where(even, own, beyond), jnp.where(even, beyond, own)

    for y in range(slab_y):
        planes[0, y + 1], planes[1, y + 1] = sides(near_ref[y], beyond_ref[y])
    own = jnp.where(even, edge_ref[1], edge_ref[0])
    for x, edge in enumerate(sides(own, corner_ref[2])):
        place_edge(planes, x, edge)
    for x in range(2):
        for y in range(slab_y):
            part = three_taps(planes[x, y], planes[x, y + 1], planes[x, y + 2])
            start = (x * slab_y + y) * slab_z
            scored[:, start : start + slab_z] = along_z(part).astype(jnp.bfloat16)
    lines = gm_ref.shape[0] // 2
    number = gm_ref[...].astype(jnp.float32).astype(jnp.int32)
    pick([scored], number[:lines] * 64 + number[lines:] - 1, out_ref)


def join_kernel(inner_ref, halo_ref, out_ref):
    for start in range(0, out_ref.shape[1], BLOCK):
        span = slice(start, start + BLOCK)
        smooth = inner_ref[:, span] + SIDE * halo_ref[:, span].astype(jnp.float32)
        out_ref[:, span] = standardise(smooth)


def call_on_rows(kernel, dtype, frames, rows, operands, scratch, name):
    whole = lambda array: pl.BlockSpec(array.shape, lambda _: (0,) * array.ndim)
    return pl.pallas_call(
        kernel,
        grid=(1,),
        in_specs=[whole(value) for value in operands],
        out_specs=pl.BlockSpec((frames, rows), lambda _: (0, 0)),
        out_shape=jax.ShapeDtypeStruct((frames, rows), dtype),
        scratch_shapes=scratch,
        compiler_params=pltpu.CompilerParams(vmem_limit_bytes=VMEM_BYTES),
        cost_estimate=SMALL,
        name=name,
    )(*operands)


def blur_scratch(first, terms):
    slab_y, frames, slab_z = first.shape
    planes = pltpu.VMEM((2, slab_y + 2, frames, slab_z), jnp.float32)
    return [planes] + [pltpu.VMEM((frames, 2 * slab_y * slab_z), jnp.bfloat16)] * terms


def make_panel(near, outer, facing, across, edge, corner, gm):
    operands = (near, outer, facing, across, edge, corner, gm)
    scratch = blur_scratch(outer, 1)
    return call_on_rows(
        panel_kernel, jnp.bfloat16, outer.shape[1], gm.size, operands, scratch, "blur_score_pick"
    )


def make_inner(near, outer, edge, gm):
    operands = (near, outer, edge, gm)
    scratch = blur_scratch(near, 3)
    return call_on_rows(
        inner_kernel, jnp.float32, near.shape[1], gm.size, operands, scratch, "inner_blur"
    )


def make_halo(near, beyond, edge, corner, gm):
    operands = (near, beyond, edge, corner, gm)
    scratch = blur_scratch(near, 1)
    return call_on_rows(
        halo_kernel, jnp.bfloat16, near.shape[1], gm.size // 2, operands, scratch, "halo_blur"
    )


def join(inner, halo):
    return call_on_rows(
        join_kernel, jnp.bfloat16, *inner.shape, (inner, halo), [], "join_score"
    )


def tiles_kernel(place_ref, present_ref, *refs, sources, window):
    parts = refs[:sources]
    out_ref, held, tiles, sems, out_sems = refs[-5:]
    blocks, slots = out_ref.shape[:2]

    loads = []
    first = 0
    for n, part in enumerate(parts):
        target = held.at[pl.ds(first, part.shape[0])]
        first += part.shape[0]
        loads.append(pltpu.make_async_copy(part, target, sems.at[n]))
        loads[-1].start()
    for load in loads:
        load.wait()

    def partner(block, slot):
        place = place_ref[block, slot]
        start = pl.multiple_of(lax.rem(place, blocks) * BLOCK, BLOCK)
        return held[lax.div(place, blocks), :, pl.ds(start, BLOCK)]

    stores = []
    for block in range(blocks):
        own = held[0, :, block * BLOCK : (block + 1) * BLOCK].T
        for slot in range(0, slots, 2):
            pair = jnp.concatenate([partner(block, slot), partner(block, slot + 1)], axis=1)
            both = jnp.dot(own, pair, preferred_element_type=jnp.float32)
            for n in range(2):
                tile = both[:, n * BLOCK : (n + 1) * BLOCK]
                tile = jnp.where(present_ref[block, slot + n] != 0, tile, 0.0)
                tiles[block, slot + n] = tile.astype(jnp.bfloat16)
        stores.append(
            pltpu.make_async_copy(tiles.at[block], out_ref.at[block, :, window], out_sems.at[block])
        )
        stores[-1].start()
    for store in stores:
        store.wait()


def make_tiles(window, windows, place, present, sources, earlier):
    frames, rows = sources[0].shape[1:]
    total = sum(source.shape[0] for source in sources)
    blocks = rows // BLOCK
    slots = place.shape[1]
    count = len(sources)
    anywhere = pl.BlockSpec(memory_space=pl.ANY)
    in_hbm = pl.BlockSpec(memory_space=pltpu.HBM)
    operands = list(sources) + ([] if earlier is None else [earlier])
    return pl.pallas_call(
        functools.partial(tiles_kernel, sources=count, window=window),
        grid_spec=pltpu.PrefetchScalarGridSpec(
            num_scalar_prefetch=2,
            grid=(1,),
            in_specs=[in_hbm] * len(operands),
            out_specs=anywhere,
            scratch_shapes=[
                pltpu.VMEM((total, frames, rows), jnp.bfloat16),
                pltpu.VMEM((blocks, slots, BLOCK, BLOCK), jnp.bfloat16),
                pltpu.SemaphoreType.DMA((count,)),
                pltpu.SemaphoreType.DMA((blocks,)),
            ],
        ),
        out_shape=jax.ShapeDtypeStruct((blocks, slots, windows, BLOCK, BLOCK), jnp.bfloat16),
        input_output_aliases={} if earlier is None else {2 + count: 0},
        compiler_params=pltpu.CompilerParams(vmem_limit_bytes=VMEM_BYTES),
        cost_estimate=SMALL,
        name="tiles",
    )(place, present, *operands)


def after(value, *earlier):
    return lax.optimization_barrier((value,) + earlier)[0]


def on_device(bold, gm_index, partners):
    row_total = lax.axis_size("row")
    col_total = lax.axis_size("col")
    row = lax.axis_index("row")
    col = lax.axis_index("col")
    even = row % 2 == 0

    def other_col(value):
        return lax.ppermute(value, "col", [(0, 1), (1, 0)])

    ahead = [((i + 2 * (-1) ** i) % row_total, i) for i in range(row_total)]
    behind = [(i, source) for source, i in ahead]
    two_on = [(i, i + 2 * (-1) ** (i + 1)) for i in range(row_total)]
    two_on = [(i, target) for i, target in two_on if 0 <= target < row_total]
    across_pairs = [(i, i - (-1) ** i) for i in range(row_total)]
    across_pairs = [(i, target) for i, target in across_pairs if 0 <= target < row_total]
    in_pair = [(i, i ^ 1) for i in range(row_total)]

    gm = gm_index.reshape(-1, BLOCK)
    blocks, slots = partners.shape
    ids = jnp.maximum(partners, 0)
    slab = ids // blocks
    hop = (slab // col_total - row + 2 + row_total) % row_total
    kind = jnp.where((hop == 1) == even, 4, 3)
    kind = jnp.where(hop == 2, 0, jnp.where((hop == 0) | (hop >= 4), 2 - (even == (hop >= 4)), kind))
    away = (slab % col_total != col).astype(jnp.int32)
    within = ids % blocks
    present = partners >= 0
    joined = jnp.where(kind == 3, 2, kind) + 3 * away
    alone = jnp.where(kind == 3, 4, jnp.where(kind == 4, 6, 8)) + away
    parts_0 = jnp.where(kind == 2, 6 + away, jnp.where(kind == 4, 8 + away, joined))
    parts_1 = jnp.where(kind < 2, kind + 2 * away, alone)
    place_0, place_1 = (
        jnp.where(present, part * blocks + within, 0).astype(jnp.int32)
        for part in (parts_0, parts_1)
    )
    present = present.astype(jnp.int32)

    def both(*parts):
        near = jnp.stack(parts, 0)
        return [near, other_col(near)]

    windows = bold.shape[0]
    frames, slab_y = bold.shape[1], bold.shape[3]

    def ends(*layers):
        planes = [
            jnp.where(col == 0, plane_of(layer, slab_y - 1, frames), plane_of(layer, 0, frames))
            for layer in layers
        ]
        return other_col(jnp.stack(planes, 0))

    near_0, outer_0, face_0, near_1, outer_1, face_1 = make_faces(bold, gm)
    facing_0 = lax.ppermute(near_0, "row", in_pair)
    across_0 = lax.ppermute(outer_0, "row", across_pairs)
    beyond_1 = lax.ppermute(outer_1, "row", two_on)
    edge_0, edge_1 = other_col(face_0), other_col(face_1)
    inner_1 = make_inner(near_1, outer_1, edge_1, after(gm, edge_0))
    facing_0, across_0 = after(facing_0, inner_1), after(across_0, inner_1)
    beyond_1 = after(beyond_1, facing_0, across_0)
    gm_pair = facing_0[slab_y * frames :]
    corner = ends(across_0, facing_0, beyond_1)
    given_1 = make_halo(near_1, beyond_1, edge_1, corner, gm_pair)
    halo_1 = lax.ppermute(given_1, "row", in_pair)
    corner = after(corner, given_1)
    own_0 = make_panel(near_0, outer_0, facing_0, across_0, edge_0, corner, gm)
    ahead_0 = lax.ppermute(own_0, "row", ahead)
    halo_1 = after(halo_1, own_0)
    own_1 = join(inner_1, halo_1)
    pair_0 = lax.ppermute(after(own_0, halo_1), "row", in_pair)
    pair_1 = lax.ppermute(own_1, "row", in_pair)
    ahead_1 = lax.ppermute(own_1, "row", ahead)
    ahead_0 = after(ahead_0, own_1)
    behind_0 = lax.ppermute(after(own_0, ahead_0), "row", behind)
    rest_0 = lax.ppermute(ahead_0, "row", in_pair)
    pair_0 = after(pair_0, ahead_0)
    pair_1 = after(pair_1, pair_0)
    ahead_1 = after(ahead_1, pair_1)
    rest_0 = after(rest_0, ahead_1)
    behind_0 = after(behind_0, rest_0)
    rest_1 = lax.ppermute(ahead_1, "row", in_pair)
    behind_1 = lax.ppermute(after(own_1, ahead_1), "row", behind)
    sources_0 = both(own_0, ahead_0, pair_0) + both(behind_0) + both(rest_0)
    out = make_tiles(0, windows, place_0, present, sources_0, None)
    sources_1 = both(own_1, ahead_1) + both(pair_1) + both(rest_1) + both(behind_1)
    return make_tiles(1, windows, place_1, present, sources_1, out)


def solution(mesh):
    in_specs = (P("subj", None, "row", "col", None), P(("row", "col")), P(("row", "col"), None))
    out_specs = P(("row", "col"), None, "subj", None, None)
    return jax.shard_map(
        on_device, mesh=mesh, in_specs=in_specs, out_specs=out_specs, check_vma=False
    )
```

```python
import functools
import math

import jax
import jax.numpy as jnp
from jax import lax
from jax.experimental import pallas as pl
from jax.experimental.pallas import tpu as pltpu
from jax.sharding import PartitionSpec as P

BLOCK = 128
SIDE = math.exp(-0.5) / (1.0 + 2.0 * math.exp(-0.5))
CENTRE = 1.0 / (1.0 + 2.0 * math.exp(-0.5))
SMALL = pl.CostEstimate(flops=1, bytes_accessed=1, transcendentals=0)
VMEM_BYTES = 20 * 1024 * 1024
TILES_VMEM_BYTES = 60 * 1024 * 1024


def is_even():
    return lax.axis_index("row") % 2 == 0


def is_first():
    return lax.axis_index("col") == 0


def plane_of(layer, y, frames):
    return layer[y] if len(layer.shape) == 3 else layer[y * frames : (y + 1) * frames]


def faces_kernel(bold_ref, gm_ref, *refs):
    windows, frames, slab_x, slab_y, slab_z = bold_ref.shape
    per_frame = slab_x * slab_y
    wide = refs[-1]
    for window in range(windows):
        near_ref, outer_ref, edge_ref = refs[3 * window : 3 * window + 3]
        wide[...] = bold_ref[window].reshape(frames * per_frame, slab_z).astype(jnp.float32)

        def plane(x, y):
            taken = wide[pl.ds(x * slab_y + y, frames, stride=per_frame), :]
            return taken.astype(jnp.bfloat16)

        def store(layer_ref, y, value):
            if len(layer_ref.shape) == 3:
                layer_ref[y] = value
            else:
                layer_ref[y * frames : (y + 1) * frames] = value

        def layers(first_ref, last_ref):
            for y in range(slab_y):
                store(first_ref, y, plane(0, y))
                store(last_ref, y, plane(1, y))

        pl.when(is_even())(functools.partial(layers, outer_ref, near_ref))
        pl.when(~is_even())(functools.partial(layers, near_ref, outer_ref))

        def edges(y):
            for x in range(slab_x):
                edge_ref[x] = plane(x, y)

        if len(near_ref.shape) == 2:
            number = gm_ref[...] + 1
            parts = jnp.concatenate([lax.shift_right_logical(number, 6), number & 63], axis=0)
            near_ref[slab_y * frames :] = parts.astype(jnp.float32).astype(jnp.bfloat16)

        pl.when(is_first())(functools.partial(edges, slab_y - 1))
        pl.when(~is_first())(functools.partial(edges, 0))


def make_faces(bold, gm):
    windows, frames, slab_x, slab_y, slab_z = bold.shape
    layer = jax.ShapeDtypeStruct((slab_y, frames, slab_z), jnp.bfloat16)
    edge = jax.ShapeDtypeStruct((slab_x, frames, slab_z), jnp.bfloat16)
    with_gm = jax.ShapeDtypeStruct(
        (slab_y * frames + 2 * gm.shape[0], slab_z), jnp.bfloat16
    )
    outs = [with_gm, layer, edge] + [layer, layer, edge] * (windows - 1)
    whole = lambda array: pl.BlockSpec(array.shape, lambda _: (0,) * len(array.shape))
    return pl.pallas_call(
        faces_kernel,
        grid=(1,),
        in_specs=[whole(bold), whole(gm)],
        out_specs=[whole(value) for value in outs],
        out_shape=outs,
        scratch_shapes=[pltpu.VMEM((frames * slab_x * slab_y, slab_z), jnp.float32)],
        compiler_params=pltpu.CompilerParams(vmem_limit_bytes=VMEM_BYTES),
        cost_estimate=SMALL,
        name="faces",
    )(bold, gm)


def three_taps(before, here, after):
    return SIDE * before + CENTRE * here + SIDE * after


def along_z(part):
    lane = lax.broadcasted_iota(jnp.int32, part.shape, 1)
    last = part.shape[1] - 1
    before = jnp.where(lane == 0, 0.0, pltpu.roll(part, 1, 1))
    after = jnp.where(lane == last, 0.0, pltpu.roll(part, last, 1))
    return three_taps(before, part, after)


def place_edge(planes, x, edge):
    planes[x, 0] = jnp.where(is_first(), 0.0, edge)
    planes[x, planes.shape[1] - 1] = jnp.where(is_first(), edge, 0.0)


def standardise(smooth):
    frames = smooth.shape[0]
    centred = smooth - jnp.mean(smooth, axis=0, keepdims=True)
    spread = jnp.mean(centred * centred, axis=0, keepdims=True)
    return (centred * lax.rsqrt((spread + 1e-05) * frames)).astype(jnp.bfloat16)


def pick(parts, gm, out_ref):
    voxels = parts[0].shape[1]
    for line in range(0, gm.shape[0], 2):
        wanted = jnp.concatenate([gm[line : line + 1], gm[line + 1 : line + 2]], axis=1)
        voxel = lax.broadcasted_iota(jnp.int32, (voxels, 2 * BLOCK), 0)
        chosen = jnp.where(voxel == wanted, 1.0, 0.0).astype(jnp.bfloat16)
        total = jnp.dot(parts[0][...], chosen, preferred_element_type=jnp.float32)
        for part in parts[1:]:
            total += jnp.dot(part[...], chosen, preferred_element_type=jnp.float32)
        start = line * BLOCK
        out_ref[:, start : start + 2 * BLOCK] = total.astype(out_ref.dtype)


def panel_kernel(
    near_ref, outer_ref, facing_ref, across_ref, edge_ref, corner_ref, gm_ref, out_ref,
    planes, scored,
):
    slab_y, frames, slab_z = outer_ref.shape
    even = is_even()

    def along_x(across, outer, near, facing):
        layers = [part.astype(jnp.float32) for part in (across, outer, near, facing)]
        outer, near = three_taps(*layers[:3]), three_taps(*layers[1:])
        return jnp.where(even, outer, near), jnp.where(even, near, outer)

    for y in range(slab_y):
        planes[0, y + 1], planes[1, y + 1] = along_x(
            across_ref[y],
            outer_ref[y],
            plane_of(near_ref, y, frames),
            plane_of(facing_ref, y, frames),
        )
    outer = jnp.where(even, edge_ref[0], edge_ref[1])
    near = jnp.where(even, edge_ref[1], edge_ref[0])
    for x, edge in enumerate(along_x(corner_ref[0], outer, near, corner_ref[1])):
        place_edge(planes, x, edge)
    for x in range(2):
        for y in range(slab_y):
            part = three_taps(planes[x, y], planes[x, y + 1], planes[x, y + 2])
            start = (x * slab_y + y) * slab_z
            scored[:, start : start + slab_z] = standardise(along_z(part))
    pick([scored], gm_ref[...], out_ref)


def inner_kernel(
    near_ref, outer_ref, edge_ref, gm_ref, out_ref, planes, high, middle, low
):
    slab_y, frames, slab_z = near_ref.shape
    slab_x = edge_ref.shape[0]
    even = is_even()

    def two_taps(here, other):
        return CENTRE * here + SIDE * other

    for y in range(slab_y):
        near, outer = near_ref[y].astype(jnp.float32), outer_ref[y].astype(jnp.float32)
        first, last = jnp.where(even, outer, near), jnp.where(even, near, outer)
        planes[0, y + 1] = two_taps(first, last)
        planes[1, y + 1] = two_taps(last, first)
    edges = [edge_ref[x].astype(jnp.float32) for x in range(slab_x)]
    for x in range(slab_x):
        place_edge(planes, x, two_taps(edges[x], edges[1 - x]))
    for x in range(slab_x):
        for y in range(slab_y):
            part = along_z(three_taps(planes[x, y], planes[x, y + 1], planes[x, y + 2]))
            start = (x * slab_y + y) * slab_z
            for term in (high, middle, low):
                rounded = part.astype(jnp.bfloat16)
                term[:, start : start + slab_z] = rounded
                part = part - rounded.astype(jnp.float32)
    pick([high, middle, low], gm_ref[...], out_ref)


def halo_kernel(
    near_ref, beyond_ref, edge_ref, corner_ref, gm_ref, out_ref, planes, scored
):
    slab_y, frames, slab_z = near_ref.shape
    even = is_even()

    def sides(own, beyond):
        own, beyond = own.astype(jnp.float32), beyond.astype(jnp.float32)
        return jnp.where(even, own, beyond), jnp.where(even, beyond, own)

    for y in range(slab_y):
        planes[0, y + 1], planes[1, y + 1] = sides(near_ref[y], beyond_ref[y])
    own = jnp.where(even, edge_ref[1], edge_ref[0])
    for x, edge in enumerate(sides(own, corner_ref[2])):
        place_edge(planes, x, edge)
    for x in range(2):
        for y in range(slab_y):
            part = three_taps(planes[x, y], planes[x, y + 1], planes[x, y + 2])
            start = (x * slab_y + y) * slab_z
            scored[:, start : start + slab_z] = along_z(part).astype(jnp.bfloat16)
    lines = gm_ref.shape[0] // 2
    number = gm_ref[...].astype(jnp.float32).astype(jnp.int32)
    pick([scored], number[:lines] * 64 + number[lines:] - 1, out_ref)


def join_kernel(inner_ref, halo_ref, out_ref):
    for start in range(0, out_ref.shape[1], BLOCK):
        span = slice(start, start + BLOCK)
        smooth = inner_ref[:, span] + SIDE * halo_ref[:, span].astype(jnp.float32)
        out_ref[:, span] = standardise(smooth)


def call_on_rows(kernel, dtype, frames, rows, operands, scratch, name):
    whole = lambda array: pl.BlockSpec(array.shape, lambda _: (0,) * array.ndim)
    return pl.pallas_call(
        kernel,
        grid=(1,),
        in_specs=[whole(value) for value in operands],
        out_specs=pl.BlockSpec((frames, rows), lambda _: (0, 0)),
        out_shape=jax.ShapeDtypeStruct((frames, rows), dtype),
        scratch_shapes=scratch,
        compiler_params=pltpu.CompilerParams(vmem_limit_bytes=VMEM_BYTES),
        cost_estimate=SMALL,
        name=name,
    )(*operands)


def blur_scratch(first, terms):
    slab_y, frames, slab_z = first.shape
    planes = pltpu.VMEM((2, slab_y + 2, frames, slab_z), jnp.float32)
    return [planes] + [pltpu.VMEM((frames, 2 * slab_y * slab_z), jnp.bfloat16)] * terms


def make_panel(near, outer, facing, across, edge, corner, gm):
    operands = (near, outer, facing, across, edge, corner, gm)
    scratch = blur_scratch(outer, 1)
    return call_on_rows(
        panel_kernel, jnp.bfloat16, outer.shape[1], gm.size, operands, scratch, "blur_score_pick"
    )


def make_inner(near, outer, edge, gm):
    operands = (near, outer, edge, gm)
    scratch = blur_scratch(near, 3)
    return call_on_rows(
        inner_kernel, jnp.float32, near.shape[1], gm.size, operands, scratch, "inner_blur"
    )


def make_halo(near, beyond, edge, corner, gm):
    operands = (near, beyond, edge, corner, gm)
    scratch = blur_scratch(near, 1)
    return call_on_rows(
        halo_kernel, jnp.bfloat16, near.shape[1], gm.size // 2, operands, scratch, "halo_blur"
    )


def join(inner, halo):
    return call_on_rows(
        join_kernel, jnp.bfloat16, *inner.shape, (inner, halo), [], "join_score"
    )


def tiles_kernel(place_ref, present_ref, *refs, sources, window):
    parts = refs[:sources]
    out_ref, held, tiles, sems, out_sems = refs[-5:]
    blocks, slots = out_ref.shape[:2]

    loads = []
    first = 0
    for n, part in enumerate(parts):
        target = held.at[pl.ds(first, part.shape[0])]
        first += part.shape[0]
        loads.append(pltpu.make_async_copy(part, target, sems.at[n]))
        loads[-1].start()
    for load in loads:
        load.wait()

    def partner(block, slot):
        place = place_ref[block, slot]
        start = pl.multiple_of(lax.rem(place, blocks) * BLOCK, BLOCK)
        return held[lax.div(place, blocks), :, pl.ds(start, BLOCK)]

    stores = []
    for block in range(blocks):
        own = held[0, :, block * BLOCK : (block + 1) * BLOCK].T
        for slot in range(0, slots, 2):
            pair = jnp.concatenate([partner(block, slot), partner(block, slot + 1)], axis=1)
            both = jnp.dot(own, pair, preferred_element_type=jnp.float32)
            for n in range(2):
                tile = both[:, n * BLOCK : (n + 1) * BLOCK]
                tile = jnp.where(present_ref[block, slot + n] != 0, tile, 0.0)
                tiles[block, slot + n] = tile.astype(jnp.bfloat16)
        stores.append(
            pltpu.make_async_copy(tiles.at[block], out_ref.at[block, :, window], out_sems.at[block])
        )
        stores[-1].start()
    for store in stores:
        store.wait()


def make_tiles(window, windows, place, present, sources, earlier):
    frames, rows = sources[0].shape[1:]
    total = sum(source.shape[0] for source in sources)
    blocks = rows // BLOCK
    slots = place.shape[1]
    count = len(sources)
    anywhere = pl.BlockSpec(memory_space=pl.ANY)
    operands = list(sources) + ([] if earlier is None else [earlier])
    return pl.pallas_call(
        functools.partial(tiles_kernel, sources=count, window=window),
        grid_spec=pltpu.PrefetchScalarGridSpec(
            num_scalar_prefetch=2,
            grid=(1,),
            in_specs=[anywhere] * len(operands),
            out_specs=anywhere,
            scratch_shapes=[
                pltpu.VMEM((total, frames, rows), jnp.bfloat16),
                pltpu.VMEM((blocks, slots, BLOCK, BLOCK), jnp.bfloat16),
                pltpu.SemaphoreType.DMA((count,)),
                pltpu.SemaphoreType.DMA((blocks,)),
            ],
        ),
        out_shape=jax.ShapeDtypeStruct((blocks, slots, windows, BLOCK, BLOCK), jnp.bfloat16),
        input_output_aliases={} if earlier is None else {2 + count: 0},
        compiler_params=pltpu.CompilerParams(vmem_limit_bytes=TILES_VMEM_BYTES),
        cost_estimate=SMALL,
        name="tiles",
    )(place, present, *operands)


def after(value, *earlier):
    return lax.optimization_barrier((value,) + earlier)[0]


def on_device(bold, gm_index, partners):
    row_total = lax.axis_size("row")
    col_total = lax.axis_size("col")
    row = lax.axis_index("row")
    col = lax.axis_index("col")
    even = row % 2 == 0

    def other_col(value):
        return lax.ppermute(value, "col", [(0, 1), (1, 0)])

    ahead = [((i + 2 * (-1) ** i) % row_total, i) for i in range(row_total)]
    behind = [(i, source) for source, i in ahead]
    two_on = [(i, i + 2 * (-1) ** (i + 1)) for i in range(row_total)]
    two_on = [(i, target) for i, target in two_on if 0 <= target < row_total]
    across_pairs = [(i, i - (-1) ** i) for i in range(row_total)]
    across_pairs = [(i, target) for i, target in across_pairs if 0 <= target < row_total]
    in_pair = [(i, i ^ 1) for i in range(row_total)]

    gm = gm_index.reshape(-1, BLOCK)
    blocks, slots = partners.shape
    ids = jnp.maximum(partners, 0)
    slab = ids // blocks
    hop = (slab // col_total - row + 2 + row_total) % row_total
    kind = jnp.where((hop == 1) == even, 4, 3)
    kind = jnp.where(hop == 2, 0, jnp.where((hop == 0) | (hop >= 4), 2 - (even == (hop >= 4)), kind))
    away = (slab % col_total != col).astype(jnp.int32)
    within = ids % blocks
    present = partners >= 0
    joined = jnp.where(kind == 3, 2, kind) + 3 * away
    alone = jnp.where(kind == 3, 4, jnp.where(kind == 4, 6, 8)) + away
    parts_0 = jnp.where(kind == 2, 6 + away, jnp.where(kind == 4, 8 + away, joined))
    parts_1 = jnp.where(kind < 2, kind + 2 * away, alone)
    place_0, place_1 = (
        jnp.where(present, part * blocks + within, 0).astype(jnp.int32)
        for part in (parts_0, parts_1)
    )
    present = present.astype(jnp.int32)

    def both(*parts):
        near = jnp.stack(parts, 0)
        return [near, other_col(near)]

    windows = bold.shape[0]
    frames, slab_y = bold.shape[1], bold.shape[3]

    def ends(*layers):
        planes = [
            jnp.where(col == 0, plane_of(layer, slab_y - 1, frames), plane_of(layer, 0, frames))
            for layer in layers
        ]
        return other_col(jnp.stack(planes, 0))

    near_0, outer_0, face_0, near_1, outer_1, face_1 = make_faces(bold, gm)
    facing_0 = lax.ppermute(near_0, "row", in_pair)
    across_0 = lax.ppermute(outer_0, "row", across_pairs)
    beyond_1 = lax.ppermute(outer_1, "row", two_on)
    edge_0, edge_1 = other_col(face_0), other_col(face_1)
    inner_1 = make_inner(near_1, outer_1, edge_1, after(gm, edge_0))
    facing_0, across_0 = after(facing_0, inner_1), after(across_0, inner_1)
    beyond_1 = after(beyond_1, facing_0, across_0)
    gm_pair = facing_0[slab_y * frames :]
    corner = ends(across_0, facing_0, beyond_1)
    given_1 = make_halo(near_1, beyond_1, edge_1, corner, gm_pair)
    halo_1 = lax.ppermute(given_1, "row", in_pair)
    corner = after(corner, given_1)
    own_0 = make_panel(near_0, outer_0, facing_0, across_0, edge_0, corner, gm)
    ahead_0 = lax.ppermute(own_0, "row", ahead)
    halo_1 = after(halo_1, own_0)
    own_1 = join(inner_1, halo_1)
    pair_0 = lax.ppermute(after(own_0, halo_1), "row", in_pair)
    pair_1 = lax.ppermute(own_1, "row", in_pair)
    ahead_1 = lax.ppermute(own_1, "row", ahead)
    ahead_0 = after(ahead_0, own_1)
    behind_0 = lax.ppermute(after(own_0, ahead_0), "row", behind)
    rest_0 = lax.ppermute(ahead_0, "row", in_pair)
    pair_0 = after(pair_0, ahead_0)
    pair_1 = after(pair_1, pair_0)
    ahead_1 = after(ahead_1, pair_1)
    rest_0 = after(rest_0, ahead_1)
    behind_0 = after(behind_0, rest_0)
    rest_1 = lax.ppermute(ahead_1, "row", in_pair)
    behind_1 = lax.ppermute(after(own_1, ahead_1), "row", behind)
    sources_0 = both(own_0, ahead_0, pair_0) + both(behind_0) + both(rest_0)
    out = make_tiles(0, windows, place_0, present, sources_0, None)
    sources_1 = both(own_1, ahead_1) + both(pair_1) + both(rest_1) + both(behind_1)
    return make_tiles(1, windows, place_1, present, sources_1, out)


def solution(mesh):
    in_specs = (P("subj", None, "row", "col", None), P(("row", "col")), P(("row", "col"), None))
    out_specs = P(("row", "col"), None, "subj", None, None)
    return jax.shard_map(
        on_device, mesh=mesh, in_specs=in_specs, out_specs=out_specs, check_vma=False
    )
```

```python
import functools
import math

import jax
import jax.numpy as jnp
from jax import lax
from jax.experimental import pallas as pl
from jax.experimental.pallas import tpu as pltpu
from jax.sharding import PartitionSpec as P

BLOCK = 128
SIDE = math.exp(-0.5) / (1.0 + 2.0 * math.exp(-0.5))
CENTRE = 1.0 / (1.0 + 2.0 * math.exp(-0.5))
SMALL = pl.CostEstimate(flops=1, bytes_accessed=1, transcendentals=0)
VMEM_BYTES = 20 * 1024 * 1024


def is_even():
    return lax.axis_index("row") % 2 == 0


def is_first():
    return lax.axis_index("col") == 0


def faces_kernel(bold_ref, *refs):
    windows, frames, slab_x, slab_y, slab_z = bold_ref.shape
    per_frame = slab_x * slab_y
    wide = refs[-1]
    for window in range(windows):
        near_ref, outer_ref, edge_ref = refs[3 * window : 3 * window + 3]
        wide[...] = bold_ref[window].reshape(frames * per_frame, slab_z).astype(jnp.float32)

        def plane(x, y):
            taken = wide[pl.ds(x * slab_y + y, frames, stride=per_frame), :]
            return taken.astype(jnp.bfloat16)

        def layers(first_ref, last_ref):
            for y in range(slab_y):
                first_ref[y] = plane(0, y)
                last_ref[y] = plane(1, y)

        pl.when(is_even())(functools.partial(layers, outer_ref, near_ref))
        pl.when(~is_even())(functools.partial(layers, near_ref, outer_ref))

        def edges(y):
            for x in range(slab_x):
                edge_ref[x] = plane(x, y)

        pl.when(is_first())(functools.partial(edges, slab_y - 1))
        pl.when(~is_first())(functools.partial(edges, 0))


def make_faces(bold):
    windows, frames, slab_x, slab_y, slab_z = bold.shape
    layer = jax.ShapeDtypeStruct((slab_y, frames, slab_z), jnp.bfloat16)
    edge = jax.ShapeDtypeStruct((slab_x, frames, slab_z), jnp.bfloat16)
    whole = lambda array: pl.BlockSpec(array.shape, lambda _: (0,) * len(array.shape))
    return pl.pallas_call(
        faces_kernel,
        grid=(1,),
        in_specs=[whole(bold)],
        out_specs=[whole(layer), whole(layer), whole(edge)] * windows,
        out_shape=[layer, layer, edge] * windows,
        scratch_shapes=[pltpu.VMEM((frames * slab_x * slab_y, slab_z), jnp.float32)],
        compiler_params=pltpu.CompilerParams(vmem_limit_bytes=VMEM_BYTES),
        cost_estimate=SMALL,
        name="faces",
    )(bold)


def three_taps(before, here, after):
    return SIDE * before + CENTRE * here + SIDE * after


def along_z(part):
    lane = lax.broadcasted_iota(jnp.int32, part.shape, 1)
    last = part.shape[1] - 1
    before = jnp.where(lane == 0, 0.0, pltpu.roll(part, 1, 1))
    after = jnp.where(lane == last, 0.0, pltpu.roll(part, last, 1))
    return three_taps(before, part, after)


def place_edge(planes, x, edge):
    planes[x, 0] = jnp.where(is_first(), 0.0, edge)
    planes[x, planes.shape[1] - 1] = jnp.where(is_first(), edge, 0.0)


def standardise(smooth):
    frames = smooth.shape[0]
    centred = smooth - jnp.mean(smooth, axis=0, keepdims=True)
    spread = jnp.mean(centred * centred, axis=0, keepdims=True)
    return (centred * lax.rsqrt((spread + 1e-05) * frames)).astype(jnp.bfloat16)


def pick(parts, gm_ref, out_ref):
    voxels = parts[0].shape[1]
    rows = gm_ref.shape[1]
    step = 2 * BLOCK
    for start in range(0, rows, step):
        wanted = gm_ref[:, start : start + step]
        voxel = lax.broadcasted_iota(jnp.int32, (voxels, step), 0)
        chosen = jnp.where(voxel == wanted, 1.0, 0.0).astype(jnp.bfloat16)
        total = jnp.dot(parts[0][...], chosen, preferred_element_type=jnp.float32)
        for part in parts[1:]:
            total += jnp.dot(part[...], chosen, preferred_element_type=jnp.float32)
        out_ref[:, start : start + step] = total.astype(out_ref.dtype)


def panel_kernel(
    near_ref, outer_ref, facing_ref, across_ref, edge_ref, corner_ref, gm_ref, out_ref,
    planes, scored,
):
    slab_y, frames, slab_z = near_ref.shape
    even = is_even()

    def along_x(across, outer, near, facing):
        layers = [part.astype(jnp.float32) for part in (across, outer, near, facing)]
        outer, near = three_taps(*layers[:3]), three_taps(*layers[1:])
        return jnp.where(even, outer, near), jnp.where(even, near, outer)

    for y in range(slab_y):
        planes[0, y + 1], planes[1, y + 1] = along_x(
            across_ref[y], outer_ref[y], near_ref[y], facing_ref[y]
        )
    outer = jnp.where(even, edge_ref[0], edge_ref[1])
    near = jnp.where(even, edge_ref[1], edge_ref[0])
    for x, edge in enumerate(along_x(corner_ref[0], outer, near, corner_ref[1])):
        place_edge(planes, x, edge)
    for x in range(2):
        for y in range(slab_y):
            part = three_taps(planes[x, y], planes[x, y + 1], planes[x, y + 2])
            start = (x * slab_y + y) * slab_z
            scored[:, start : start + slab_z] = standardise(along_z(part))
    pick([scored], gm_ref, out_ref)


def inner_kernel(
    near_ref, outer_ref, edge_ref, gm_ref, out_ref, planes, high, middle, low
):
    slab_y, frames, slab_z = near_ref.shape
    slab_x = edge_ref.shape[0]
    even = is_even()

    def two_taps(here, other):
        return CENTRE * here + SIDE * other

    for y in range(slab_y):
        near, outer = near_ref[y].astype(jnp.float32), outer_ref[y].astype(jnp.float32)
        first, last = jnp.where(even, outer, near), jnp.where(even, near, outer)
        planes[0, y + 1] = two_taps(first, last)
        planes[1, y + 1] = two_taps(last, first)
    edges = [edge_ref[x].astype(jnp.float32) for x in range(slab_x)]
    for x in range(slab_x):
        place_edge(planes, x, two_taps(edges[x], edges[1 - x]))
    for x in range(slab_x):
        for y in range(slab_y):
            part = along_z(three_taps(planes[x, y], planes[x, y + 1], planes[x, y + 2]))
            start = (x * slab_y + y) * slab_z
            for term in (high, middle, low):
                rounded = part.astype(jnp.bfloat16)
                term[:, start : start + slab_z] = rounded
                part = part - rounded.astype(jnp.float32)
    pick([high, middle, low], gm_ref, out_ref)


def halo_kernel(
    near_ref, beyond_ref, edge_ref, corner_ref, gm_ref, out_ref, planes, scored
):
    slab_y, frames, slab_z = near_ref.shape
    even = is_even()

    def sides(own, beyond):
        own, beyond = own.astype(jnp.float32), beyond.astype(jnp.float32)
        return jnp.where(even, own, beyond), jnp.where(even, beyond, own)

    for y in range(slab_y):
        planes[0, y + 1], planes[1, y + 1] = sides(near_ref[y], beyond_ref[y])
    own = jnp.where(even, edge_ref[1], edge_ref[0])
    for x, edge in enumerate(sides(own, corner_ref[...])):
        place_edge(planes, x, edge)
    for x in range(2):
        for y in range(slab_y):
            part = three_taps(planes[x, y], planes[x, y + 1], planes[x, y + 2])
            start = (x * slab_y + y) * slab_z
            scored[:, start : start + slab_z] = along_z(part).astype(jnp.bfloat16)
    pick([scored], gm_ref, out_ref)


def join_kernel(inner_ref, halo_ref, out_ref):
    for start in range(0, out_ref.shape[1], BLOCK):
        span = slice(start, start + BLOCK)
        smooth = inner_ref[:, span] + SIDE * halo_ref[:, span].astype(jnp.float32)
        out_ref[:, span] = standardise(smooth)


def call_on_rows(kernel, dtype, frames, operands, scratch, name):
    rows = operands[-1].shape[1]
    whole = lambda array: pl.BlockSpec(array.shape, lambda _: (0,) * array.ndim)
    return pl.pallas_call(
        kernel,
        grid=(1,),
        in_specs=[whole(value) for value in operands],
        out_specs=pl.BlockSpec((frames, rows), lambda _: (0, 0)),
        out_shape=jax.ShapeDtypeStruct((frames, rows), dtype),
        scratch_shapes=scratch,
        compiler_params=pltpu.CompilerParams(vmem_limit_bytes=VMEM_BYTES),
        cost_estimate=SMALL,
        name=name,
    )(*operands)


def blur_scratch(first, terms):
    slab_y, frames, slab_z = first.shape
    planes = pltpu.VMEM((2, slab_y + 2, frames, slab_z), jnp.float32)
    return [planes] + [pltpu.VMEM((frames, 2 * slab_y * slab_z), jnp.bfloat16)] * terms


def make_panel(near, outer, facing, across, edge, corner, gm):
    operands = (near, outer, facing, across, edge, corner, gm)
    scratch = blur_scratch(near, 1)
    return call_on_rows(
        panel_kernel, jnp.bfloat16, near.shape[1], operands, scratch, "blur_score_pick"
    )


def make_inner(near, outer, edge, gm):
    operands = (near, outer, edge, gm)
    scratch = blur_scratch(near, 3)
    return call_on_rows(
        inner_kernel, jnp.float32, near.shape[1], operands, scratch, "inner_blur"
    )


def make_halo(near, beyond, edge, corner, gm):
    operands = (near, beyond, edge, corner, gm)
    scratch = blur_scratch(near, 1)
    return call_on_rows(
        halo_kernel, jnp.bfloat16, near.shape[1], operands, scratch, "halo_blur"
    )


def join(inner, halo):
    return call_on_rows(
        join_kernel, jnp.bfloat16, inner.shape[0], (inner, halo), [], "join_score"
    )


def tiles_kernel(place_ref, present_ref, *refs, sources, window):
    parts = refs[:sources]
    out_ref, held, tiles, sems, out_sems = refs[-5:]
    blocks, slots = out_ref.shape[:2]

    loads = []
    first = 0
    for n, part in enumerate(parts):
        target = held.at[pl.ds(first, part.shape[0])]
        first += part.shape[0]
        loads.append(pltpu.make_async_copy(part, target, sems.at[n]))
        loads[-1].start()
    for load in loads:
        load.wait()

    def partner(block, slot):
        place = place_ref[block, slot]
        start = pl.multiple_of(lax.rem(place, blocks) * BLOCK, BLOCK)
        return held[lax.div(place, blocks), :, pl.ds(start, BLOCK)]

    stores = []
    for block in range(blocks):
        own = held[0, :, block * BLOCK : (block + 1) * BLOCK].T
        for slot in range(0, slots, 2):
            pair = jnp.concatenate([partner(block, slot), partner(block, slot + 1)], axis=1)
            both = jnp.dot(own, pair, preferred_element_type=jnp.float32)
            for n in range(2):
                tile = both[:, n * BLOCK : (n + 1) * BLOCK]
                tile = jnp.where(present_ref[block, slot + n] != 0, tile, 0.0)
                tiles[block, slot + n] = tile.astype(jnp.bfloat16)
        stores.append(
            pltpu.make_async_copy(tiles.at[block], out_ref.at[block, :, window], out_sems.at[block])
        )
        stores[-1].start()
    for store in stores:
        store.wait()


def make_tiles(window, windows, place, present, sources, earlier):
    frames, rows = sources[0].shape[1:]
    total = sum(source.shape[0] for source in sources)
    blocks = rows // BLOCK
    slots = place.shape[1]
    count = len(sources)
    anywhere = pl.BlockSpec(memory_space=pl.ANY)
    operands = list(sources) + ([] if earlier is None else [earlier])
    return pl.pallas_call(
        functools.partial(tiles_kernel, sources=count, window=window),
        grid_spec=pltpu.PrefetchScalarGridSpec(
            num_scalar_prefetch=2,
            grid=(1,),
            in_specs=[anywhere] * len(operands),
            out_specs=anywhere,
            scratch_shapes=[
                pltpu.VMEM((total, frames, rows), jnp.bfloat16),
                pltpu.VMEM((blocks, slots, BLOCK, BLOCK), jnp.bfloat16),
                pltpu.SemaphoreType.DMA((count,)),
                pltpu.SemaphoreType.DMA((blocks,)),
            ],
        ),
        out_shape=jax.ShapeDtypeStruct((blocks, slots, windows, BLOCK, BLOCK), jnp.bfloat16),
        input_output_aliases={} if earlier is None else {2 + count: 0},
        compiler_params=pltpu.CompilerParams(vmem_limit_bytes=VMEM_BYTES),
        cost_estimate=SMALL,
        name="tiles",
    )(place, present, *operands)


def after(value, *earlier):
    return lax.optimization_barrier((value,) + earlier)[0]


def on_device(bold, gm_index, partners):
    row_total = lax.axis_size("row")
    col_total = lax.axis_size("col")
    row = lax.axis_index("row")
    col = lax.axis_index("col")
    even = row % 2 == 0

    def other_col(value):
        return lax.ppermute(value, "col", [(0, 1), (1, 0)])

    ahead = [((i + 2 * (-1) ** i) % row_total, i) for i in range(row_total)]
    behind = [(i, source) for source, i in ahead]
    two_on = [(i, i + 2 * (-1) ** (i + 1)) for i in range(row_total)]
    two_on = [(i, target) for i, target in two_on if 0 <= target < row_total]
    across_pairs = [(i, i - (-1) ** i) for i in range(row_total)]
    across_pairs = [(i, target) for i, target in across_pairs if 0 <= target < row_total]
    in_pair = [(i, i ^ 1) for i in range(row_total)]

    gm = gm_index.reshape(1, -1)
    blocks, slots = partners.shape
    ids = jnp.maximum(partners, 0)
    slab = ids // blocks
    hop = (slab // col_total - row + 2 + row_total) % row_total
    kind = jnp.where((hop == 1) == even, 4, 3)
    kind = jnp.where(hop == 2, 0, jnp.where((hop == 0) | (hop >= 4), 2 - (even == (hop >= 4)), kind))
    away = (slab % col_total != col).astype(jnp.int32)
    within = ids % blocks
    present = partners >= 0
    parts_0 = jnp.where(kind == 4, 8 + away, kind // 2 * 4 + kind % 2 + 2 * away)
    alone = jnp.where(kind == 3, 4, jnp.where(kind == 4, 6, 8)) + away
    parts_1 = jnp.where(kind < 2, kind + 2 * away, alone)
    place_0, place_1 = (
        jnp.where(present, part * blocks + within, 0).astype(jnp.int32)
        for part in (parts_0, parts_1)
    )
    present = present.astype(jnp.int32)

    def both(*parts):
        near = jnp.stack(parts, 0)
        return [near, other_col(near)]

    windows = bold.shape[0]
    gm_pair = lax.ppermute(gm, "row", in_pair)

    def ends(*layers):
        return other_col(jnp.stack([jnp.where(col == 0, layer[-1], layer[0]) for layer in layers], 0))

    near_0, outer_0, face_0, near_1, outer_1, face_1 = make_faces(bold)
    beyond_1 = lax.ppermute(outer_1, "row", two_on)
    facing_0 = lax.ppermute(after(near_0, gm_pair), "row", in_pair)
    across_0 = lax.ppermute(after(outer_0, gm_pair), "row", across_pairs)
    edge_0, edge_1 = other_col(face_0), other_col(face_1)
    inner_1 = make_inner(near_1, outer_1, edge_1, after(gm, edge_0))
    beyond_1 = after(beyond_1, inner_1)
    given_1 = make_halo(near_1, beyond_1, edge_1, ends(beyond_1)[0], gm_pair)
    facing_0, across_0 = after(facing_0, given_1), after(across_0, given_1)
    halo_1 = lax.ppermute(after(given_1, facing_0, across_0), "row", in_pair)
    corner_0 = ends(across_0, facing_0)
    own_0 = make_panel(near_0, outer_0, facing_0, across_0, edge_0, corner_0, gm)
    ahead_0 = lax.ppermute(own_0, "row", ahead)
    halo_1 = after(halo_1, own_0)
    own_1 = join(inner_1, halo_1)
    pair_0 = lax.ppermute(after(own_0, halo_1), "row", in_pair)
    pair_1 = lax.ppermute(own_1, "row", in_pair)
    ahead_1 = lax.ppermute(own_1, "row", ahead)
    ahead_0 = after(ahead_0, own_1)
    behind_0 = lax.ppermute(after(own_0, ahead_0), "row", behind)
    rest_0 = lax.ppermute(ahead_0, "row", in_pair)
    pair_0 = after(pair_0, ahead_0)
    pair_1 = after(pair_1, pair_0)
    ahead_1 = after(ahead_1, pair_1)
    rest_0 = after(rest_0, ahead_1)
    behind_0 = after(behind_0, rest_0)
    rest_1 = lax.ppermute(after(ahead_1, rest_0), "row", in_pair)
    behind_1 = lax.ppermute(after(own_1, ahead_1), "row", behind)
    sources_0 = both(own_0, ahead_0) + both(behind_0, pair_0) + both(rest_0)
    out = make_tiles(0, windows, place_0, present, sources_0, None)
    rest_1, behind_1 = after(rest_1, out), after(behind_1, out)
    sources_1 = both(own_1, ahead_1) + both(pair_1) + both(rest_1) + both(behind_1)
    return make_tiles(1, windows, place_1, present, sources_1, out)


def solution(mesh):
    in_specs = (P("subj", None, "row", "col", None), P(("row", "col")), P(("row", "col"), None))
    out_specs = P(("row", "col"), None, "subj", None, None)
    return jax.shard_map(
        on_device, mesh=mesh, in_specs=in_specs, out_specs=out_specs, check_vma=False
    )
```

```python
import functools
import math

import jax
import jax.numpy as jnp
from jax import lax
from jax.experimental import pallas as pl
from jax.experimental.pallas import tpu as pltpu
from jax.sharding import PartitionSpec as P

BLOCK = 128
SIDE = math.exp(-0.5) / (1.0 + 2.0 * math.exp(-0.5))
CENTRE = 1.0 / (1.0 + 2.0 * math.exp(-0.5))
SMALL = pl.CostEstimate(flops=1, bytes_accessed=1, transcendentals=0)
VMEM_BYTES = 20 * 1024 * 1024


def is_even():
    return lax.axis_index("row") % 2 == 0


def is_first():
    return lax.axis_index("col") == 0


def faces_kernel(bold_ref, *refs):
    windows, frames, slab_x, slab_y, slab_z = bold_ref.shape
    per_frame = slab_x * slab_y
    wide = refs[-1]
    for window in range(windows):
        near_ref, outer_ref, edge_ref = refs[3 * window : 3 * window + 3]
        wide[...] = bold_ref[window].reshape(frames * per_frame, slab_z).astype(jnp.float32)

        def plane(x, y):
            taken = wide[pl.ds(x * slab_y + y, frames, stride=per_frame), :]
            return taken.astype(jnp.bfloat16)

        def layers(first_ref, last_ref):
            for y in range(slab_y):
                first_ref[y] = plane(0, y)
                last_ref[y] = plane(1, y)

        pl.when(is_even())(functools.partial(layers, outer_ref, near_ref))
        pl.when(~is_even())(functools.partial(layers, near_ref, outer_ref))

        def edges(y):
            for x in range(slab_x):
                edge_ref[x] = plane(x, y)

        pl.when(is_first())(functools.partial(edges, slab_y - 1))
        pl.when(~is_first())(functools.partial(edges, 0))


def make_faces(bold):
    windows, frames, slab_x, slab_y, slab_z = bold.shape
    layer = jax.ShapeDtypeStruct((slab_y, frames, slab_z), jnp.bfloat16)
    edge = jax.ShapeDtypeStruct((slab_x, frames, slab_z), jnp.bfloat16)
    whole = lambda array: pl.BlockSpec(array.shape, lambda _: (0,) * len(array.shape))
    return pl.pallas_call(
        faces_kernel,
        grid=(1,),
        in_specs=[whole(bold)],
        out_specs=[whole(layer), whole(layer), whole(edge)] * windows,
        out_shape=[layer, layer, edge] * windows,
        scratch_shapes=[pltpu.VMEM((frames * slab_x * slab_y, slab_z), jnp.float32)],
        compiler_params=pltpu.CompilerParams(vmem_limit_bytes=VMEM_BYTES),
        cost_estimate=SMALL,
        name="faces",
    )(bold)


def three_taps(before, here, after):
    return SIDE * before + CENTRE * here + SIDE * after


def along_z(part):
    lane = lax.broadcasted_iota(jnp.int32, part.shape, 1)
    last = part.shape[1] - 1
    before = jnp.where(lane == 0, 0.0, pltpu.roll(part, 1, 1))
    after = jnp.where(lane == last, 0.0, pltpu.roll(part, last, 1))
    return three_taps(before, part, after)


def place_edge(planes, x, edge):
    planes[x, 0] = jnp.where(is_first(), 0.0, edge)
    planes[x, planes.shape[1] - 1] = jnp.where(is_first(), edge, 0.0)


def standardise(smooth):
    frames = smooth.shape[0]
    centred = smooth - jnp.mean(smooth, axis=0, keepdims=True)
    spread = jnp.mean(centred * centred, axis=0, keepdims=True)
    return (centred * lax.rsqrt((spread + 1e-05) * frames)).astype(jnp.bfloat16)


def pick(parts, gm_ref, out_ref):
    voxels = parts[0].shape[1]
    rows = gm_ref.shape[1]
    step = 2 * BLOCK
    for start in range(0, rows, step):
        wanted = gm_ref[:, start : start + step]
        voxel = lax.broadcasted_iota(jnp.int32, (voxels, step), 0)
        chosen = jnp.where(voxel == wanted, 1.0, 0.0).astype(jnp.bfloat16)
        total = jnp.dot(parts[0][...], chosen, preferred_element_type=jnp.float32)
        for part in parts[1:]:
            total += jnp.dot(part[...], chosen, preferred_element_type=jnp.float32)
        out_ref[:, start : start + step] = total.astype(out_ref.dtype)


def panel_kernel(
    near_ref, outer_ref, facing_ref, across_ref, edge_ref, corner_ref, gm_ref, out_ref,
    planes, scored,
):
    slab_y, frames, slab_z = near_ref.shape
    even = is_even()

    def along_x(across, outer, near, facing):
        layers = [part.astype(jnp.float32) for part in (across, outer, near, facing)]
        outer, near = three_taps(*layers[:3]), three_taps(*layers[1:])
        return jnp.where(even, outer, near), jnp.where(even, near, outer)

    for y in range(slab_y):
        planes[0, y + 1], planes[1, y + 1] = along_x(
            across_ref[y], outer_ref[y], near_ref[y], facing_ref[y]
        )
    outer = jnp.where(even, edge_ref[0], edge_ref[1])
    near = jnp.where(even, edge_ref[1], edge_ref[0])
    for x, edge in enumerate(along_x(corner_ref[0], outer, near, corner_ref[1])):
        place_edge(planes, x, edge)
    for x in range(2):
        for y in range(slab_y):
            part = three_taps(planes[x, y], planes[x, y + 1], planes[x, y + 2])
            start = (x * slab_y + y) * slab_z
            scored[:, start : start + slab_z] = standardise(along_z(part))
    pick([scored], gm_ref, out_ref)


def inner_kernel(
    near_ref, outer_ref, edge_ref, gm_ref, out_ref, planes, high, middle, low
):
    slab_y, frames, slab_z = near_ref.shape
    slab_x = edge_ref.shape[0]
    even = is_even()

    def two_taps(here, other):
        return CENTRE * here + SIDE * other

    for y in range(slab_y):
        near, outer = near_ref[y].astype(jnp.float32), outer_ref[y].astype(jnp.float32)
        first, last = jnp.where(even, outer, near), jnp.where(even, near, outer)
        planes[0, y + 1] = two_taps(first, last)
        planes[1, y + 1] = two_taps(last, first)
    edges = [edge_ref[x].astype(jnp.float32) for x in range(slab_x)]
    for x in range(slab_x):
        place_edge(planes, x, two_taps(edges[x], edges[1 - x]))
    for x in range(slab_x):
        for y in range(slab_y):
            part = along_z(three_taps(planes[x, y], planes[x, y + 1], planes[x, y + 2]))
            start = (x * slab_y + y) * slab_z
            for term in (high, middle, low):
                rounded = part.astype(jnp.bfloat16)
                term[:, start : start + slab_z] = rounded
                part = part - rounded.astype(jnp.float32)
    pick([high, middle, low], gm_ref, out_ref)


def halo_kernel(
    near_ref, beyond_ref, edge_ref, corner_ref, gm_ref, out_ref, planes, scored
):
    slab_y, frames, slab_z = near_ref.shape
    even = is_even()

    def sides(own, beyond):
        own, beyond = own.astype(jnp.float32), beyond.astype(jnp.float32)
        return jnp.where(even, own, beyond), jnp.where(even, beyond, own)

    for y in range(slab_y):
        planes[0, y + 1], planes[1, y + 1] = sides(near_ref[y], beyond_ref[y])
    own = jnp.where(even, edge_ref[1], edge_ref[0])
    for x, edge in enumerate(sides(own, corner_ref[...])):
        place_edge(planes, x, edge)
    for x in range(2):
        for y in range(slab_y):
            part = three_taps(planes[x, y], planes[x, y + 1], planes[x, y + 2])
            start = (x * slab_y + y) * slab_z
            scored[:, start : start + slab_z] = along_z(part).astype(jnp.bfloat16)
    pick([scored], gm_ref, out_ref)


def join_kernel(inner_ref, halo_ref, out_ref):
    for start in range(0, out_ref.shape[1], BLOCK):
        span = slice(start, start + BLOCK)
        smooth = inner_ref[:, span] + SIDE * halo_ref[:, span].astype(jnp.float32)
        out_ref[:, span] = standardise(smooth)


def call_on_rows(kernel, dtype, frames, operands, scratch, name):
    rows = operands[-1].shape[1]
    whole = lambda array: pl.BlockSpec(array.shape, lambda _: (0,) * array.ndim)
    return pl.pallas_call(
        kernel,
        grid=(1,),
        in_specs=[whole(value) for value in operands],
        out_specs=pl.BlockSpec((frames, rows), lambda _: (0, 0)),
        out_shape=jax.ShapeDtypeStruct((frames, rows), dtype),
        scratch_shapes=scratch,
        compiler_params=pltpu.CompilerParams(vmem_limit_bytes=VMEM_BYTES),
        cost_estimate=SMALL,
        name=name,
    )(*operands)


def blur_scratch(first, terms):
    slab_y, frames, slab_z = first.shape
    planes = pltpu.VMEM((2, slab_y + 2, frames, slab_z), jnp.float32)
    return [planes] + [pltpu.VMEM((frames, 2 * slab_y * slab_z), jnp.bfloat16)] * terms


def make_panel(near, outer, facing, across, edge, corner, gm):
    operands = (near, outer, facing, across, edge, corner, gm)
    scratch = blur_scratch(near, 1)
    return call_on_rows(
        panel_kernel, jnp.bfloat16, near.shape[1], operands, scratch, "blur_score_pick"
    )


def make_inner(near, outer, edge, gm):
    operands = (near, outer, edge, gm)
    scratch = blur_scratch(near, 3)
    return call_on_rows(
        inner_kernel, jnp.float32, near.shape[1], operands, scratch, "inner_blur"
    )


def make_halo(near, beyond, edge, corner, gm):
    operands = (near, beyond, edge, corner, gm)
    scratch = blur_scratch(near, 1)
    return call_on_rows(
        halo_kernel, jnp.bfloat16, near.shape[1], operands, scratch, "halo_blur"
    )


def join(inner, halo):
    return call_on_rows(
        join_kernel, jnp.bfloat16, inner.shape[0], (inner, halo), [], "join_score"
    )


def tiles_kernel(place_ref, present_ref, *refs, sources, window):
    parts = refs[:sources]
    out_ref, held, tiles, sems, out_sems = refs[-5:]
    blocks, slots = out_ref.shape[:2]

    loads = []
    first = 0
    for n, part in enumerate(parts):
        target = held.at[pl.ds(first, part.shape[0])]
        first += part.shape[0]
        loads.append(pltpu.make_async_copy(part, target, sems.at[n]))
        loads[-1].start()
    for load in loads:
        load.wait()

    def partner(block, slot):
        place = place_ref[block, slot]
        start = pl.multiple_of(lax.rem(place, blocks) * BLOCK, BLOCK)
        return held[lax.div(place, blocks), :, pl.ds(start, BLOCK)]

    stores = []
    for block in range(blocks):
        own = held[0, :, block * BLOCK : (block + 1) * BLOCK].T
        for slot in range(0, slots, 2):
            pair = jnp.concatenate([partner(block, slot), partner(block, slot + 1)], axis=1)
            both = jnp.dot(own, pair, preferred_element_type=jnp.float32)
            for n in range(2):
                tile = both[:, n * BLOCK : (n + 1) * BLOCK]
                tile = jnp.where(present_ref[block, slot + n] != 0, tile, 0.0)
                tiles[block, slot + n] = tile.astype(jnp.bfloat16)
        stores.append(
            pltpu.make_async_copy(tiles.at[block], out_ref.at[block, :, window], out_sems.at[block])
        )
        stores[-1].start()
    for store in stores:
        store.wait()


def make_tiles(window, windows, place, present, sources, earlier):
    frames, rows = sources[0].shape[1:]
    total = sum(source.shape[0] for source in sources)
    blocks = rows // BLOCK
    slots = place.shape[1]
    count = len(sources)
    anywhere = pl.BlockSpec(memory_space=pl.ANY)
    operands = list(sources) + ([] if earlier is None else [earlier])
    return pl.pallas_call(
        functools.partial(tiles_kernel, sources=count, window=window),
        grid_spec=pltpu.PrefetchScalarGridSpec(
            num_scalar_prefetch=2,
            grid=(1,),
            in_specs=[anywhere] * len(operands),
            out_specs=anywhere,
            scratch_shapes=[
                pltpu.VMEM((total, frames, rows), jnp.bfloat16),
                pltpu.VMEM((blocks, slots, BLOCK, BLOCK), jnp.bfloat16),
                pltpu.SemaphoreType.DMA((count,)),
                pltpu.SemaphoreType.DMA((blocks,)),
            ],
        ),
        out_shape=jax.ShapeDtypeStruct((blocks, slots, windows, BLOCK, BLOCK), jnp.bfloat16),
        input_output_aliases={} if earlier is None else {2 + count: 0},
        compiler_params=pltpu.CompilerParams(vmem_limit_bytes=VMEM_BYTES),
        cost_estimate=SMALL,
        name="tiles",
    )(place, present, *operands)


def after(value, *earlier):
    return lax.optimization_barrier((value,) + earlier)[0]


def on_device(bold, gm_index, partners):
    row_total = lax.axis_size("row")
    col_total = lax.axis_size("col")
    row = lax.axis_index("row")
    col = lax.axis_index("col")
    even = row % 2 == 0

    def other_col(value):
        return lax.ppermute(value, "col", [(0, 1), (1, 0)])

    ahead = [((i + 2 * (-1) ** i) % row_total, i) for i in range(row_total)]
    behind = [(i, source) for source, i in ahead]
    two_on = [(i, i + 2 * (-1) ** (i + 1)) for i in range(row_total)]
    two_on = [(i, target) for i, target in two_on if 0 <= target < row_total]
    across_pairs = [(i, i - (-1) ** i) for i in range(row_total)]
    across_pairs = [(i, target) for i, target in across_pairs if 0 <= target < row_total]
    in_pair = [(i, i ^ 1) for i in range(row_total)]

    gm = gm_index.reshape(1, -1)
    blocks, slots = partners.shape
    ids = jnp.maximum(partners, 0)
    slab = ids // blocks
    hop = (slab // col_total - row + 2 + row_total) % row_total
    kind = jnp.where((hop == 1) == even, 4, 3)
    kind = jnp.where(hop == 2, 0, jnp.where((hop == 0) | (hop >= 4), 2 - (even == (hop >= 4)), kind))
    away = (slab % col_total != col).astype(jnp.int32)
    within = ids % blocks
    present = partners >= 0
    parts_0 = jnp.where(kind == 4, 8 + away, kind // 2 * 4 + kind % 2 + 2 * away)
    alone = jnp.where(kind == 3, 4, jnp.where(kind == 4, 6, 8)) + away
    parts_1 = jnp.where(kind < 2, kind + 2 * away, alone)
    place_0, place_1 = (
        jnp.where(present, part * blocks + within, 0).astype(jnp.int32)
        for part in (parts_0, parts_1)
    )
    present = present.astype(jnp.int32)

    def both(*parts):
        near = jnp.stack(parts, 0)
        return [near, other_col(near)]

    windows = bold.shape[0]
    gm_pair = lax.ppermute(gm, "row", in_pair)

    def ends(*layers):
        return other_col(jnp.stack([jnp.where(col == 0, layer[-1], layer[0]) for layer in layers], 0))

    near_0, outer_0, face_0, near_1, outer_1, face_1 = make_faces(bold)
    beyond_1 = lax.ppermute(outer_1, "row", two_on)
    facing_0 = lax.ppermute(after(near_0, gm_pair), "row", in_pair)
    across_0 = lax.ppermute(after(outer_0, gm_pair), "row", across_pairs)
    edge_0, edge_1 = other_col(face_0), other_col(face_1)
    inner_1 = make_inner(near_1, outer_1, edge_1, after(gm, edge_0))
    beyond_1 = after(beyond_1, inner_1)
    given_1 = make_halo(near_1, beyond_1, edge_1, ends(beyond_1)[0], gm_pair)
    facing_0, across_0 = after(facing_0, given_1), after(across_0, given_1)
    halo_1 = lax.ppermute(after(given_1, facing_0, across_0), "row", in_pair)
    corner_0 = ends(across_0, facing_0)
    own_0 = make_panel(near_0, outer_0, facing_0, across_0, edge_0, corner_0, gm)
    ahead_0 = lax.ppermute(own_0, "row", ahead)
    halo_1 = after(halo_1, own_0)
    own_1 = join(inner_1, halo_1)
    pair_0 = lax.ppermute(after(own_0, halo_1), "row", in_pair)
    pair_1 = lax.ppermute(own_1, "row", in_pair)
    ahead_1 = lax.ppermute(own_1, "row", ahead)
    ahead_0 = after(ahead_0, own_1)
    behind_0 = lax.ppermute(after(own_0, ahead_0), "row", behind)
    rest_0 = lax.ppermute(ahead_0, "row", in_pair)
    pair_0 = after(pair_0, ahead_0)
    pair_1 = after(pair_1, pair_0)
    ahead_1 = after(ahead_1, pair_1)
    rest_0 = after(rest_0, ahead_1)
    behind_0 = after(behind_0, rest_0)
    rest_1 = lax.ppermute(after(ahead_1, rest_0), "row", in_pair)
    behind_1 = lax.ppermute(own_1, "row", behind)
    sources_0 = both(own_0, ahead_0) + both(behind_0, pair_0) + both(rest_0)
    out = make_tiles(0, windows, place_0, present, sources_0, None)
    rest_1, behind_1 = after(rest_1, out), after(behind_1, out)
    sources_1 = both(own_1, ahead_1) + both(pair_1) + both(rest_1) + both(behind_1)
    return make_tiles(1, windows, place_1, present, sources_1, out)


def solution(mesh):
    in_specs = (P("subj", None, "row", "col", None), P(("row", "col")), P(("row", "col"), None))
    out_specs = P(("row", "col"), None, "subj", None, None)
    return jax.shard_map(
        on_device, mesh=mesh, in_specs=in_specs, out_specs=out_specs, check_vma=False
    )
```
